32 devices in a mesh: lat: 8 (over z, x), lon: 4 (over y, core).
Axes of the slice: x: 2, y: 2, z: 4, core: 2. Of those that a mesh axis runs over, the one named last changes fastest.
Arguments:
- tracers: float32 [4, 8, 32, 5760], P(None, None, 'lat', 'lon'), may hold values from -6 to 6
- merid_courant: float32 [8, 32, 5760], P(None, 'lat', 'lon'), may hold values from -0.45 to 0.45
- zonal_shift: int32 [8, 32], P(None, 'lat'), may hold values from 0 to 64, as said below
- zonal_fraction: float32 [8, 32], P(None, 'lat'), may hold values from 0 to 1
- cutoff: int32 [32], replicated, may hold values from 1 to 1023
- damping: float32 [32], replicated, may hold values from 0.1 to 0.6
Outputs:
- tracer_out: float32 [4, 8, 32, 5760], P(None, None, 'lat', 'lon')
The draws below stay inside these ranges and needn't reach their ends.
Inputs may be any that keep to these rules, and one draw needn't show every extreme that they name: `zonal_shift`: in row j no displacement exceeds 1 + (64 * |2j - 31|) // 32, a limit that grows toward the poles; below it the values are random.
All inputs are finite; a program needn't handle non-finite values.
Results may differ from the reference program's by a relative error of at most 0.00005.
Values sent between devices are 32-bit elements; how exact they have to be, the bound alone decides.
No kernel may reach another device: no remote copies, remote signals or barrier semaphores. Data moves between devices by JAX's collectives and lax.ppermute only.
A program may use at most 64 MiB of HBM per device.

```python
import jax
import jax.numpy as jnp

NLON = 5760
NTR = 4
MODES = 1024
SMAX = 64
LEV = 8
NLAT = 32


def draw_zonal_shift(key, part):
    row_index = jnp.arange(NLAT, dtype=jnp.int32)
    distance = jnp.abs(2 * row_index + 1 - NLAT)
    row_limit = 1 + SMAX * distance // NLAT
    values = jax.random.randint(key, (LEV, NLAT), 0, SMAX + 1, dtype=jnp.int32)
    values = jnp.minimum(values, row_limit[None, :])
    return values.at[0, 0].set(SMAX).astype(jnp.int32)


def draw_cutoff(key, part):
    values = jax.random.randint(key, (NLAT,), 1, MODES, dtype=jnp.int32)
    return values.at[0].set(MODES - 1).astype(jnp.int32)


def steps_of(rng, dims, pieces, low, high):
    loudness = 1.0
    for position, shards_of in pieces:
        steps = jax.random.uniform(jax.random.fold_in(jax.random.fold_in(rng, 6), position), (shards_of,), jnp.float32, low / len(pieces), high / len(pieces))
        loudness = loudness * jnp.repeat(jnp.exp(steps), dims[position] // shards_of).reshape((-1,) + (1,) * (len(dims) - 1 - position))
    return loudness


def gaussian(stream_key, extent, width, limit, pieces=(), kind=jnp.bfloat16):
    array = width * jax.random.normal(stream_key, extent, jnp.float32)
    if pieces:
        array = array * steps_of(stream_key, extent, pieces, -0.22, 0.18)
    return jnp.clip(array, -limit, limit).astype(kind)


def setup_inputs(seed: int = 0) -> dict:
    keys = jax.random.split(jax.random.key(seed), 7)
    tracers = gaussian(keys[0], (NTR, LEV, NLAT, NLON), 1.0, 6.0, ((2, 8), (3, 4)), jnp.float32)
    merid_courant = jnp.clip(jax.random.uniform(keys[1], (LEV, NLAT, NLON), jnp.float32, -0.45, 0.45) * steps_of(keys[1], (LEV, NLAT, NLON), ((1, 8), (2, 4)), -0.4, 0.0), -0.45, 0.45)
    zonal_shift = draw_zonal_shift(jax.random.fold_in(keys[6], 71), 0)
    zonal_fraction = jnp.clip(1.0 * jax.random.uniform(keys[3], (LEV, NLAT), jnp.float32) ** steps_of(keys[3], (LEV, NLAT), ((1, 8),), -0.2, 0.2), 0.0, 1.0)
    cutoff = draw_cutoff(jax.random.fold_in(keys[6], 71), 0)
    damping = jnp.clip(jax.random.uniform(keys[5], (NLAT,), jnp.float32, 0.1, 0.6), 0.1, 0.6)
    return dict(tracers=tracers, merid_courant=merid_courant, zonal_shift=zonal_shift, zonal_fraction=zonal_fraction, cutoff=cutoff, damping=damping)


def reference(tracers, merid_courant, zonal_shift, zonal_fraction, cutoff, damping):
    zeros_row = jnp.zeros_like(tracers[:, :, :1])
    below_cells = jnp.concatenate([zeros_row, tracers[:, :, :-1]], axis=2)
    face_flux = jnp.maximum(merid_courant, 0.0)[None] * below_cells + jnp.minimum(merid_courant, 0.0)[None] * tracers
    face_flux = face_flux.at[:, :, 0].set(0.0)
    north_flux = jnp.concatenate([face_flux[:, :, 1:], zeros_row], axis=2)
    advected = tracers + face_flux - north_flux
    columns = jnp.arange(NLON, dtype=jnp.int32)
    source = (columns[None, None, :] - zonal_shift[:, :, None]) % NLON
    prior = (source - 1) % NLON

    def pick_cells(index_grid):
        return jnp.take_along_axis(advected, jnp.broadcast_to(index_grid[None], advected.shape), axis=3)

    fraction_here = zonal_fraction[None, :, :, None]
    shifted = (1.0 - fraction_here) * pick_cells(source) + fraction_here * pick_cells(prior)
    spectrum = jnp.fft.rfft(shifted, axis=3)
    wavenumber = jnp.arange(NLON // 2 + 1, dtype=jnp.int32)
    kept_modes = (wavenumber[None, :] <= cutoff[:, None]).astype(shifted.dtype)
    low_part = jnp.fft.irfft(spectrum * kept_modes[None, None], n=NLON, axis=3).astype(shifted.dtype)
    damp_factor = damping[None, None, :, None]
    filtered = damp_factor * shifted + (1.0 - damp_factor) * low_part
    row_index = jnp.arange(NLAT, dtype=jnp.int32)
    in_caps = (row_index < NLAT // 4) | (row_index >= NLAT - NLAT // 4)
    return jnp.where(in_caps[None, None, :, None], filtered, shifted)
```

```python
import functools
import math

import jax
import jax.numpy as jnp
import numpy as np
from jax import lax
from jax.experimental import pallas as pl
from jax.experimental.pallas import tpu as pltpu
from jax.sharding import PartitionSpec as P

MODES = 1024
SMAX = 64
RADIX = 16
HALF = RADIX // 2
LANES = 128


def passed_along(block, axis, distance):
    devices = range(lax.axis_size(axis))
    route = [(i - distance, i) for i in devices if i - distance in devices]
    return lax.ppermute(block, axis, route)


def passed_around(value, axis, steps):
    count = lax.axis_size(axis)
    pairs = [(source, (source + steps) % count) for source in range(count)]
    return lax.ppermute(value, axis, pairs)


def times_phase(value, numerator, denominator):
    re, im = value
    eighth = (8 * numerator % (8 * denominator)) / denominator
    if eighth == 0:
        return re, im
    if eighth == 2:
        return -im, re
    if eighth == 4:
        return -re, -im
    if eighth == 6:
        return im, -re
    c = math.cos(2 * math.pi * numerator / denominator)
    s = math.sin(2 * math.pi * numerator / denominator)
    if eighth == 7:
        return (re + im) * c, (im - re) * c
    if eighth == 1:
        return (re - im) * c, (re + im) * c
    return re * c - im * s, re * s + im * c


def real_dft(values):
    n = len(values)
    if n == 2:
        return [(values[0] + values[1], None), (values[0] - values[1], None)]
    even, odd = real_dft(values[0::2]), real_dft(values[1::2])
    out = [None] * (n // 2 + 1)
    for r in range(n // 4 + 1):
        (er, ei), (tr, ti) = even[r], odd[r]
        if r == 0:
            out[0] = (er + tr, None)
            out[n // 2] = (er - tr, None)
        elif r == n // 4:
            out[r] = (er, -tr)
        else:
            tr, ti = times_phase((tr, ti), -r, n)
            out[r] = (er + tr, ei + ti)
            out[n // 2 - r] = (er - tr, ti - ei)
    return out


def real_inverse(spectrum):
    n = 2 * (len(spectrum) - 1)
    if n == 2:
        a, b = spectrum[0][0], spectrum[1][0]
        return [a + b, a - b]
    even, odd = [None] * (n // 4 + 1), [None] * (n // 4 + 1)
    for r in range(n // 4 + 1):
        (ar, ai), (br, bi) = spectrum[r], spectrum[n // 2 - r]
        if r == 0:
            even[0] = (ar + br, None)
            odd[0] = (ar - br, None)
        elif r == n // 4:
            even[r] = (ar + ar, None)
            odd[r] = (-(ai + ai), None)
        else:
            even[r] = (ar + br, ai - bi)
            odd[r] = times_phase((ar - br, ai + bi), r, n)
    out = [None] * n
    out[0::2] = real_inverse(even)
    out[1::2] = real_inverse(odd)
    return out


def split(value):
    high = value.astype(jnp.bfloat16)
    return high, (value - high.astype(jnp.float32)).astype(jnp.bfloat16)


def product(left, right_high, right_low):
    high, low = split(left)
    dot = functools.partial(jnp.dot, preferred_element_type=jnp.float32)
    return dot(high, right_high) + (dot(high, right_low) + dot(low, right_high))


def filter_kernel(
    cap_ref, cutoff_ref, shift_ref, fraction_ref, damping_ref, phase_ref,
    fwd_high, fwd_low, inv_high, inv_low, *refs
):
    parts = (len(refs) - 3) // 2
    ins, outs = refs[:parts], refs[parts : 2 * parts]
    moved_ref, stack_ref, back_ref = refs[2 * parts :]
    row_count, levels, columns = ins[0].shape
    lon_cells = parts * columns
    piece = lon_cells // RADIX
    padded = stack_ref.shape[1]
    modes = fwd_high.shape[1] // 2
    group = levels * 2 * (HALF + 1)

    for row in range(row_count):
        circle = jnp.concatenate([ref[row] for ref in ins], axis=1)
        distance = shift_ref[row][:, :1]
        for bit in range(SMAX.bit_length()):
            pushed = pltpu.roll(circle, 1 << bit, 1)
            circle = jnp.where((distance >> bit) & 1 == 1, pushed, circle)
        share = fraction_ref[row][:, :1]
        circle = (1.0 - share) * circle + share * pltpu.roll(circle, 1, 1)
        moved_ref[row, :, :lon_cells] = circle
        moved_ref[row, :, lon_cells:] = circle[:, :LANES]

    @pl.when(cap_ref[0] == 0)
    def _():
        for row in range(row_count):
            for part in range(parts):
                start = part * columns
                outs[part][row] = moved_ref[row, :, start : start + columns]

    @pl.when(cap_ref[0] != 0)
    def _():
        for row in range(row_count):
            for tile in range(0, padded, LANES):
                lanes = slice(tile, tile + LANES)
                starts = [piece * u + tile for u in range(RADIX)]
                spectrum = real_dft([moved_ref[row, :, s : s + LANES] for s in starts])
                for r, (re, im) in enumerate(spectrum):
                    base = row * group + 2 * r * levels
                    if r == 0:
                        im = jnp.zeros_like(re)
                    else:
                        c, s = phase_ref[2 * r : 2 * r + 1, lanes], phase_ref[2 * r + 1 : 2 * r + 2, lanes]
                        if im is None:
                            re, im = re * c, -(re * s)
                        else:
                            re, im = re * c + im * s, im * c - re * s
                    stack_ref[base : base + levels, lanes] = re
                    stack_ref[base + levels : base + 2 * levels, lanes] = im
        coeffs = product(stack_ref[...], fwd_high[...], fwd_low[...])
        mode = lax.broadcasted_iota(jnp.int32, (levels, modes), 1) - modes // 2
        for row in range(row_count):
            for r in range(HALF + 1):
                base = row * group + 2 * r * levels
                re, im = coeffs[base : base + levels], coeffs[base + levels : base + 2 * levels]
                wavenumber = jnp.abs(RADIX * mode + r)
                weight = jnp.where(wavenumber <= cutoff_ref[row], 1.0 / lon_cells, 0.0)
                x_re = (re[:, :modes] + im[:, modes:]) * weight
                x_im = (im[:, :modes] - re[:, modes:]) * weight
                back_ref[base : base + levels, :modes] = x_re
                back_ref[base : base + levels, modes:] = -x_im
                back_ref[base + levels : base + 2 * levels, :modes] = x_im
                back_ref[base + levels : base + 2 * levels, modes:] = x_re
        stack_ref[...] = product(back_ref[...], inv_high[...], inv_low[...])
        for row in range(row_count):
            keep = damping_ref[row]
            for tile in range(0, padded, LANES):
                lanes = slice(tile, tile + LANES)
                spectrum = []
                for r in range(HALF + 1):
                    base = row * group + 2 * r * levels
                    re = stack_ref[base : base + levels, lanes]
                    im = stack_ref[base + levels : base + 2 * levels, lanes]
                    if r > 0:
                        c, s = phase_ref[2 * r : 2 * r + 1, lanes], phase_ref[2 * r + 1 : 2 * r + 2, lanes]
                        re, im = re * c - im * s, re * s + im * c
                    spectrum.append((re, im))
                width = min(LANES, piece - tile)
                for u, low in enumerate(real_inverse(spectrum)):
                    start = piece * u + tile
                    shifted = moved_ref[row, :, start : start + LANES]
                    result = keep * shifted + (1.0 - keep) * low
                    part, offset = start // columns, start % columns
                    outs[part][row, :, offset : offset + width] = result[:, :width]


def filter_tables(lon_cells):
    piece = lon_cells // RADIX
    padded = -(-piece // LANES) * LANES
    modes = 2 * MODES // RADIX
    q = np.arange(modes) - modes // 2
    angle = 2 * np.pi * (np.arange(piece)[:, None] * q[None, :] % piece) / piece
    table = np.zeros((padded, 2 * modes))
    table[:piece, :modes] = np.cos(angle)
    table[:piece, modes:] = np.sin(angle)
    high = table.astype(jnp.bfloat16)
    low = (table - high.astype(np.float64)).astype(jnp.bfloat16)
    r = np.arange(HALF + 1)
    turn = 2 * np.pi * r[:, None] * np.arange(padded)[None, :] / lon_cells
    phase = np.stack([np.cos(turn), np.sin(turn)], axis=1).reshape(-1, padded)
    return phase.astype(np.float32), high, low, np.ascontiguousarray(high.T), np.ascontiguousarray(low.T)


def filtered(chunks, is_cap, cut_rows, shift_rows, fraction_rows, damp_rows):
    row_count, levels, columns = chunks[0].shape
    parts = len(chunks)
    lon_cells = parts * columns
    tables = filter_tables(lon_cells)
    padded, double = tables[1].shape
    group = levels * 2 * (HALF + 1)
    spread = lambda v: jnp.broadcast_to(v[:, :, None], v.shape + (LANES,))
    vmem = pl.BlockSpec(memory_space=pltpu.VMEM)
    smem = pl.BlockSpec(memory_space=pltpu.SMEM)
    return pl.pallas_call(
        filter_kernel,
        out_shape=[jax.ShapeDtypeStruct(c.shape, jnp.float32) for c in chunks],
        in_specs=[smem, smem, vmem, vmem, smem] + [vmem] * (5 + parts),
        out_specs=[vmem] * parts,
        scratch_shapes=[
            pltpu.VMEM((row_count, levels, lon_cells + LANES), jnp.float32),
            pltpu.VMEM((row_count * group, padded), jnp.float32),
            pltpu.VMEM((row_count * group, double), jnp.float32),
        ],
        compiler_params=pltpu.CompilerParams(vmem_limit_bytes=24 << 20),
    )(
        is_cap, cut_rows, spread(shift_rows), spread(fraction_rows), damp_rows,
        *[jnp.asarray(t) for t in tables], *chunks,
    )


def body(tracers, merid_courant, zonal_shift, zonal_fraction, cutoff, damping):
    tracer_count, level_count, row_count, column_count = tracers.shape
    lat_count = lax.axis_size("lat")
    lat_index = lax.axis_index("lat")
    lon_count = lax.axis_size("lon")
    lon_index = lax.axis_index("lon")
    share = tracer_count // lon_count

    cells = tracers.transpose(0, 2, 1, 3)
    speed = merid_courant.transpose(1, 0, 2)
    below = passed_along(cells[:, row_count - 1], "lat", 1)
    above = passed_along(jnp.concatenate([cells[:, 0], speed[:1]], axis=0), "lat", -1)

    def flux_of(face_speed, south, north):
        return jnp.maximum(face_speed, 0.0)[None] * south + jnp.minimum(face_speed, 0.0)[None] * north

    first = jnp.where(lat_index > 0, flux_of(speed[0], below, cells[:, 0]), 0.0)
    last = flux_of(above[tracer_count], cells[:, row_count - 1], above[:tracer_count])
    last = jnp.where(lat_index < lat_count - 1, last, 0.0)
    fluxes = [first]
    fluxes += [flux_of(speed[j], cells[:, j - 1], cells[:, j]) for j in range(1, row_count)]
    fluxes.append(last)
    advected = jnp.stack(
        [cells[:, j] + fluxes[j] - fluxes[j + 1] for j in range(row_count)], axis=1
    ).reshape(lon_count, share * row_count, level_count, column_count)

    chunks = [None] * lon_count
    for step in range(lon_count):
        mine = lax.dynamic_index_in_dim(advected, (lon_index + step) % lon_count, 0, False)
        chunks[-step % lon_count] = passed_around(mine, "lon", step) if step else mine

    quarter = lat_count // 4
    is_cap = (lat_index < quarter) | (lat_index >= lat_count - quarter)
    row_base = lat_index * row_count
    cut_rows = jnp.tile(lax.dynamic_slice_in_dim(cutoff, row_base, row_count), share)
    damp_rows = jnp.tile(lax.dynamic_slice_in_dim(damping, row_base, row_count), share)
    shift_rows = jnp.tile(zonal_shift.T, (share, 1))
    fraction_rows = jnp.tile(zonal_fraction.T, (share, 1))
    results = filtered(
        chunks, is_cap.astype(jnp.int32)[None], cut_rows, shift_rows, fraction_rows, damp_rows
    )
    back = [passed_around(r, "lon", step) if step else r for step, r in enumerate(results)]
    stacked = jnp.stack(back, axis=0)
    order = (lon_index - jnp.arange(lon_count)) % lon_count
    stacked = jnp.concatenate(
        [lax.dynamic_slice_in_dim(stacked, order[t], 1, 0) for t in range(lon_count)], axis=0
    )
    stacked = stacked.reshape(tracer_count, row_count, level_count, column_count)
    return stacked.transpose(0, 2, 1, 3)


def solution(mesh):
    placed = (
        P(None, None, "lat", "lon"),
        P(None, "lat", "lon"),
        P(None, "lat"),
        P(None, "lat"),
        P(),
        P(),
    )
    return jax.shard_map(
        body, mesh=mesh, in_specs=placed, out_specs=P(None, None, "lat", "lon"), check_vma=False
    )
```

```python
import functools
import math

import jax
import jax.numpy as jnp
import numpy as np
from jax import lax
from jax.experimental import pallas as pl
from jax.experimental.pallas import tpu as pltpu
from jax.sharding import PartitionSpec as P

MODES = 1024
SMAX = 64
RADIX = 16
HALF = RADIX // 2
LANES = 128
SPAN = 9 * LANES


def times_phase(value, numerator, denominator):
    re, im = value
    eighth = (8 * numerator % (8 * denominator)) / denominator
    if eighth == 0:
        return re, im
    if eighth == 2:
        return -im, re
    if eighth == 4:
        return -re, -im
    if eighth == 6:
        return im, -re
    c = math.cos(2 * math.pi * numerator / denominator)
    s = math.sin(2 * math.pi * numerator / denominator)
    if eighth == 7:
        return (re + im) * c, (im - re) * c
    if eighth == 1:
        return (re - im) * c, (re + im) * c
    return re * c - im * s, re * s + im * c


def real_dft(values):
    n = len(values)
    if n == 2:
        return [(values[0] + values[1], None), (values[0] - values[1], None)]
    even, odd = real_dft(values[0::2]), real_dft(values[1::2])
    out = [None] * (n // 2 + 1)
    for r in range(n // 4 + 1):
        (er, ei), (tr, ti) = even[r], odd[r]
        if r == 0:
            out[0] = (er + tr, None)
            out[n // 2] = (er - tr, None)
        elif r == n // 4:
            out[r] = (er, -tr)
        else:
            tr, ti = times_phase((tr, ti), -r, n)
            out[r] = (er + tr, ei + ti)
            out[n // 2 - r] = (er - tr, ti - ei)
    return out


def real_inverse(spectrum):
    n = 2 * (len(spectrum) - 1)
    if n == 2:
        a, b = spectrum[0][0], spectrum[1][0]
        return [a + b, a - b]
    even, odd = [None] * (n // 4 + 1), [None] * (n // 4 + 1)
    for r in range(n // 4 + 1):
        (ar, ai), (br, bi) = spectrum[r], spectrum[n // 2 - r]
        if r == 0:
            even[0] = (ar + br, None)
            odd[0] = (ar - br, None)
        elif r == n // 4:
            even[r] = (ar + ar, None)
            odd[r] = (-(ai + ai), None)
        else:
            even[r] = (ar + br, ai - bi)
            odd[r] = times_phase((ar - br, ai + bi), r, n)
    out = [None] * n
    out[0::2] = real_inverse(even)
    out[1::2] = real_inverse(odd)
    return out


def split(value):
    high = value.astype(jnp.bfloat16)
    return high, (value - high.astype(jnp.float32)).astype(jnp.bfloat16)


def product(left, right_high, right_low):
    high, low = split(left)
    dot = functools.partial(jnp.dot, preferred_element_type=jnp.float32)
    return dot(high, right_high) + (dot(high, right_low) + dot(low, right_high))


def filter_kernel(
    cap_ref, cutoff_ref, shift_ref, fraction_ref, damping_ref, phase_ref,
    fwd_high, fwd_low, inv_high, inv_low, in_ref, out_ref,
    circle_ref, moved_ref, stack_ref, back_ref,
):
    parts, height, columns = in_ref.shape
    row_count, levels = shift_ref.shape[:2]
    lon_cells = parts * columns
    piece = lon_cells // RADIX
    padded = stack_ref.shape[1]
    modes = fwd_high.shape[1] // 2
    group = levels * 2 * (HALF + 1)

    for row in range(row_count):
        own = slice(row * levels, (row + 1) * levels)
        for part in range(parts):
            start = LANES + part * columns
            circle_ref[row, :, start : start + columns] = in_ref[part, own]
        circle_ref[row, :, :LANES] = in_ref[parts - 1, own, columns - LANES :]
        distance = shift_ref[row]
        share = fraction_ref[row]
        for start in range(0, lon_cells, SPAN):
            width = min(SPAN, lon_cells - start) + LANES
            block = circle_ref[row, :, start : start + width]
            distances = jnp.concatenate([distance] * (width // LANES), axis=1)
            shares = jnp.concatenate([share] * (width // LANES), axis=1)
            for bit in range(SMAX.bit_length()):
                pushed = pltpu.roll(block, 1 << bit, 1)
                block = jnp.where((distances >> bit) & 1 == 1, pushed, block)
            block = (1.0 - shares) * block + shares * pltpu.roll(block, 1, 1)
            moved_ref[row, :, start : start + width - LANES] = block[:, LANES:]
            if start == 0:
                moved_ref[row, :, lon_cells:] = block[:, LANES : 2 * LANES]

    @pl.when(cap_ref[0] == 0)
    def _():
        for row in range(row_count):
            own = slice(row * levels, (row + 1) * levels)
            for part in range(parts):
                start = part * columns
                out_ref[part, own] = moved_ref[row, :, start : start + columns]

    @pl.when(cap_ref[0] != 0)
    def _():
        for row in range(row_count):
            for tile in range(0, padded, LANES):
                lanes = slice(tile, tile + LANES)
                starts = [piece * u + tile for u in range(RADIX)]
                spectrum = real_dft([moved_ref[row, :, s : s + LANES] for s in starts])
                for r, (re, im) in enumerate(spectrum):
                    base = row * group + 2 * r * levels
                    if r == 0:
                        im = jnp.zeros_like(re)
                    else:
                        c, s = phase_ref[2 * r : 2 * r + 1, lanes], phase_ref[2 * r + 1 : 2 * r + 2, lanes]
                        if im is None:
                            re, im = re * c, -(re * s)
                        else:
                            re, im = re * c + im * s, im * c - re * s
                    stack_ref[base : base + levels, lanes] = re
                    stack_ref[base + levels : base + 2 * levels, lanes] = im
        coeffs = product(stack_ref[...], fwd_high[...], fwd_low[...])
        mode = lax.broadcasted_iota(jnp.int32, (levels, modes), 1) - modes // 2
        for row in range(row_count):
            for r in range(HALF + 1):
                base = row * group + 2 * r * levels
                re, im = coeffs[base : base + levels], coeffs[base + levels : base + 2 * levels]
                wavenumber = jnp.abs(RADIX * mode + r)
                weight = jnp.where(wavenumber <= cutoff_ref[row], 1.0 / lon_cells, 0.0)
                x_re = (re[:, :modes] + im[:, modes:]) * weight
                x_im = (im[:, :modes] - re[:, modes:]) * weight
                back_ref[base : base + levels, :modes] = x_re
                back_ref[base : base + levels, modes:] = -x_im
                back_ref[base + levels : base + 2 * levels, :modes] = x_im
                back_ref[base + levels : base + 2 * levels, modes:] = x_re
        stack_ref[...] = product(back_ref[...], inv_high[...], inv_low[...])
        for row in range(row_count):
            own = slice(row * levels, (row + 1) * levels)
            keep = damping_ref[row]
            for tile in range(0, padded, LANES):
                lanes = slice(tile, tile + LANES)
                spectrum = []
                for r in range(HALF + 1):
                    base = row * group + 2 * r * levels
                    re = stack_ref[base : base + levels, lanes]
                    im = stack_ref[base + levels : base + 2 * levels, lanes]
                    if r > 0:
                        c, s = phase_ref[2 * r : 2 * r + 1, lanes], phase_ref[2 * r + 1 : 2 * r + 2, lanes]
                        re, im = re * c - im * s, re * s + im * c
                    spectrum.append((re, im))
                width = min(LANES, piece - tile)
                for u, low in enumerate(real_inverse(spectrum)):
                    start = piece * u + tile
                    shifted = moved_ref[row, :, start : start + LANES]
                    result = keep * shifted + (1.0 - keep) * low
                    part, offset = start // columns, start % columns
                    out_ref[part, own, offset : offset + width] = result[:, :width]


def filter_tables(lon_cells):
    piece = lon_cells // RADIX
    padded = -(-piece // LANES) * LANES
    modes = 2 * MODES // RADIX
    q = np.arange(modes) - modes // 2
    angle = 2 * np.pi * (np.arange(piece)[:, None] * q[None, :] % piece) / piece
    table = np.zeros((padded, 2 * modes))
    table[:piece, :modes] = np.cos(angle)
    table[:piece, modes:] = np.sin(angle)
    high = table.astype(jnp.bfloat16)
    low = (table - high.astype(np.float64)).astype(jnp.bfloat16)
    r = np.arange(HALF + 1)
    turn = 2 * np.pi * r[:, None] * np.arange(padded)[None, :] / lon_cells
    phase = np.stack([np.cos(turn), np.sin(turn)], axis=1).reshape(-1, padded)
    return phase.astype(np.float32), high, low, np.ascontiguousarray(high.T), np.ascontiguousarray(low.T)


def filtered(chunks, is_cap, cut_rows, shift_rows, fraction_rows, damp_rows):
    parts, height, columns = chunks.shape
    row_count, levels = shift_rows.shape
    lon_cells = parts * columns
    tables = filter_tables(lon_cells)
    padded, double = tables[1].shape
    group = levels * 2 * (HALF + 1)
    spread = lambda v: jnp.broadcast_to(v[:, :, None], v.shape + (LANES,))
    vmem = pl.BlockSpec(memory_space=pltpu.VMEM)
    smem = pl.BlockSpec(memory_space=pltpu.SMEM)
    return pl.pallas_call(
        filter_kernel,
        out_shape=jax.ShapeDtypeStruct(chunks.shape, jnp.float32),
        in_specs=[smem, smem, vmem, vmem, smem] + [vmem] * 6,
        out_specs=vmem,
        scratch_shapes=[
            pltpu.VMEM((row_count, levels, lon_cells + LANES), jnp.float32),
            pltpu.VMEM((row_count, levels, lon_cells + LANES), jnp.float32),
            pltpu.VMEM((row_count * group, padded), jnp.float32),
            pltpu.VMEM((row_count * group, double), jnp.float32),
        ],
        compiler_params=pltpu.CompilerParams(vmem_limit_bytes=24 << 20),
        cost_estimate=pl.CostEstimate(flops=int(2e9), bytes_accessed=1 << 20, transcendentals=0),
    )(
        is_cap, cut_rows, spread(shift_rows), spread(fraction_rows), damp_rows,
        *[jnp.asarray(t) for t in tables], chunks,
    )


def swapped(value, axis, first):
    count = lax.axis_size(axis)
    pairs = []
    for low in range(first, count - 1, 2):
        pairs += [(low, low + 1), (low + 1, low)]
    return lax.ppermute(value, axis, pairs)


def exchanged(value, axis):
    return lax.all_to_all(value, axis, 0, 0)


def body(tracers, merid_courant, zonal_shift, zonal_fraction, cutoff, damping):
    tracer_count, level_count, row_count, column_count = tracers.shape
    lat_count = lax.axis_size("lat")
    lat_index = lax.axis_index("lat")
    lon_count = lax.axis_size("lon")
    share = tracer_count // lon_count
    top = row_count - 1

    cells = tracers.transpose(2, 0, 1, 3)
    speed = merid_courant.transpose(1, 0, 2)
    south_edge = jnp.concatenate([cells[0], speed[:1]], axis=0).reshape(-1, column_count)
    north_edge = jnp.concatenate([cells[top], speed[:1]], axis=0).reshape(-1, column_count)
    is_even = lat_index % 2 == 0
    near = swapped(jnp.where(is_even, north_edge, south_edge), "lat", 0)
    far = swapped(jnp.where(is_even, south_edge, north_edge), "lat", 1)

    def flux_of(face_speed, south, north):
        return jnp.maximum(face_speed, 0.0)[None] * south + jnp.minimum(face_speed, 0.0)[None] * north

    def packed(rows):
        block = jnp.stack(rows, axis=1)
        return block.reshape(lon_count, share * len(rows) * level_count, column_count)

    def unpacked(block, count):
        return block.reshape(tracer_count, count, level_count, column_count)

    quarter = lat_count // 4
    is_cap = (lat_index < quarter) | (lat_index >= lat_count - quarter)
    is_cap = is_cap.astype(jnp.int32)[None]
    row_base = lat_index * row_count
    cut_rows = lax.dynamic_slice_in_dim(cutoff, row_base, row_count)
    damp_rows = lax.dynamic_slice_in_dim(damping, row_base, row_count)

    def stepped(rows, numbers):
        pick = lambda v: jnp.concatenate([v[j : j + 1] for j in numbers] * share, axis=0)
        chunks = exchanged(packed(rows), "lon")
        result = filtered(
            chunks, is_cap, pick(cut_rows), pick(zonal_shift.T), pick(zonal_fraction.T), pick(damp_rows)
        )
        return unpacked(exchanged(result, "lon"), len(numbers))

    fluxes = [None] + [flux_of(speed[j], cells[j - 1], cells[j]) for j in range(1, row_count)] + [None]
    inner = stepped(
        [cells[j] + fluxes[j] - fluxes[j + 1] for j in range(1, top)], list(range(1, top))
    )

    near = near.reshape(tracer_count + 1, level_count, column_count)
    far = far.reshape(tracer_count + 1, level_count, column_count)
    below = jnp.where(is_even, far, near)
    above = jnp.where(is_even, near, far)
    first = jnp.where(lat_index > 0, flux_of(speed[0], below[:tracer_count], cells[0]), 0.0)
    last = flux_of(above[tracer_count], cells[top], above[:tracer_count])
    last = jnp.where(lat_index < lat_count - 1, last, 0.0)
    outer = stepped([cells[0] + first - fluxes[1], cells[top] + fluxes[top] - last], [0, top])
    result = jnp.concatenate([outer[:, :1], inner, outer[:, 1:]], axis=1)
    return result.transpose(0, 2, 1, 3)


def solution(mesh):
    placed = (
        P(None, None, "lat", "lon"),
        P(None, "lat", "lon"),
        P(None, "lat"),
        P(None, "lat"),
        P(),
        P(),
    )
    return jax.shard_map(
        body, mesh=mesh, in_specs=placed, out_specs=P(None, None, "lat", "lon"), check_vma=False
    )
```

```python
import functools
import math

import jax
import jax.numpy as jnp
import numpy as np
from jax import lax
from jax.experimental import pallas as pl
from jax.experimental.pallas import tpu as pltpu
from jax.sharding import PartitionSpec as P

MODES = 1024
SMAX = 64
RADIX = 16
HALF = RADIX // 2
LANES = 128
SPAN = 6 * LANES
PAIR = 2


def times_phase(value, numerator, denominator):
    re, im = value
    eighth = (8 * numerator % (8 * denominator)) / denominator
    if eighth == 0:
        return re, im
    if eighth == 2:
        return -im, re
    if eighth == 4:
        return -re, -im
    if eighth == 6:
        return im, -re
    c = math.cos(2 * math.pi * numerator / denominator)
    s = math.sin(2 * math.pi * numerator / denominator)
    if eighth == 7:
        return (re + im) * c, (im - re) * c
    if eighth == 1:
        return (re - im) * c, (re + im) * c
    return re * c - im * s, re * s + im * c


def real_dft(values):
    n = len(values)
    if n == 2:
        return [(values[0] + values[1], None), (values[0] - values[1], None)]
    even, odd = real_dft(values[0::2]), real_dft(values[1::2])
    out = [None] * (n // 2 + 1)
    for r in range(n // 4 + 1):
        (er, ei), (tr, ti) = even[r], odd[r]
        if r == 0:
            out[0] = (er + tr, None)
            out[n // 2] = (er - tr, None)
        elif r == n // 4:
            out[r] = (er, -tr)
        else:
            tr, ti = times_phase((tr, ti), -r, n)
            out[r] = (er + tr, ei + ti)
            out[n // 2 - r] = (er - tr, ti - ei)
    return out


def real_inverse(spectrum):
    n = 2 * (len(spectrum) - 1)
    if n == 2:
        a, b = spectrum[0][0], spectrum[1][0]
        return [a + b, a - b]
    even, odd = [None] * (n // 4 + 1), [None] * (n // 4 + 1)
    for r in range(n // 4 + 1):
        (ar, ai), (br, bi) = spectrum[r], spectrum[n // 2 - r]
        if r == 0:
            even[0] = (ar + br, None)
            odd[0] = (ar - br, None)
        elif r == n // 4:
            even[r] = (ar + ar, None)
            odd[r] = (-(ai + ai), None)
        else:
            even[r] = (ar + br, ai - bi)
            odd[r] = times_phase((ar - br, ai + bi), r, n)
    out = [None] * n
    out[0::2] = real_inverse(even)
    out[1::2] = real_inverse(odd)
    return out


def four(values, sign):
    (ar, ai), (br, bi), (cr, ci), (dr, di) = values
    pr, pi, mr, mi = ar + cr, ai + ci, ar - cr, ai - ci
    qr, qi, nr, ni = br + dr, bi + di, br - dr, bi - di
    if sign > 0:
        nr, ni = -nr, -ni
    return [(pr + qr, pi + qi), (mr + ni, mi - nr), (pr - qr, pi - qi), (mr - ni, mi + nr)]


def half_dft(x):
    out = [None] * 9
    out[0::2] = real_dft(x)
    odd = four([times_phase((x[v], -x[v + 4]), -v, 16) for v in range(4)], -1)
    out[1], out[5] = odd[0], odd[1]
    out[7] = (odd[2][0], -odd[2][1])
    out[3] = (odd[3][0], -odd[3][1])
    return out


def half_inverse(w):
    even = real_inverse(w[0::2])
    odd = four([w[1], w[5], (w[7][0], -w[7][1]), (w[3][0], -w[3][1])], 1)
    odd = [times_phase(value, v, 16) for v, value in enumerate(odd)]
    return [even[v] + odd[v][0] for v in range(4)] + [even[v + 4] - odd[v][1] for v in range(4)]


def split(value):
    high = value.astype(jnp.bfloat16)
    return high, (value - high.astype(jnp.float32)).astype(jnp.bfloat16)


def product(left, right_high, right_low):
    high, low = split(left)
    dot = functools.partial(jnp.dot, preferred_element_type=jnp.float32)
    return dot(high, right_high) + (dot(high, right_low) + dot(low, right_high))


def spans(columns, width):
    return [slice(start, min(start + width, columns)) for start in range(0, columns, width)]


def is_cap(lat):
    count = lax.axis_size("lat")
    return (lat < count // 4) | (lat >= count - count // 4)


def flux_of(face_speed, south, north):
    return jnp.maximum(face_speed, 0.0) * south + jnp.minimum(face_speed, 0.0) * north


def begin_kernel(cells_ref, speed_ref, near_ref, far_ref, mine_ref, send_ref, edge_mine_ref, edge_send_ref):
    tracer_count, levels, row_count, columns = cells_ref.shape
    share = tracer_count // PAIR
    core = lax.rem(lax.axis_index("lon"), PAIR)
    is_even = lax.rem(lax.axis_index("lat"), 2) == 0
    for lanes in spans(columns, 3 * LANES):
        speed = [speed_ref[:, j, lanes] for j in range(row_count)]
        near_ref[tracer_count * levels :, lanes] = speed[0]
        far_ref[tracer_count * levels :, lanes] = speed[0]
        for which, (inner_ref, outer_ref) in enumerate(
            [(mine_ref, edge_mine_ref), (send_ref, edge_send_ref)]
        ):
            for i in range(share):
                t = lax.rem(core + which, PAIR) * share + i
                x = [cells_ref[t, :, j, lanes] for j in range(row_count)]
                place = pl.ds(pl.multiple_of(t * levels, levels), levels)
                near_ref[place, lanes] = jnp.where(is_even, x[-1], x[0])
                far_ref[place, lanes] = jnp.where(is_even, x[0], x[-1])
                flux = [flux_of(speed[j], x[j - 1], x[j]) for j in range(1, row_count)]
                for j in range(1, row_count - 1):
                    inner_ref[i, j - 1, :, lanes] = x[j] + flux[j - 1] - flux[j]
                outer_ref[i, 0, :, lanes] = x[0] - flux[0]
                outer_ref[i, 1, :, lanes] = x[-1] + flux[-1]


def edge_kernel(
    near_out_ref, far_out_ref, near_first_ref, near_later_ref, far_first_ref, far_later_ref,
    edge_mine_ref, edge_send_ref, mine_ref, send_ref,
):
    share, _, levels, columns = edge_mine_ref.shape
    total = share * PAIR * levels
    core = lax.rem(lax.axis_index("lon"), PAIR)
    lat = lax.axis_index("lat")
    is_even = lax.rem(lat, 2) == 0
    cap = is_cap(lat)
    for lanes in spans(columns, 3 * LANES):

        def received(place):
            near = jnp.where(cap, near_first_ref[place, lanes], near_later_ref[place, lanes])
            far = jnp.where(cap, far_first_ref[place, lanes], far_later_ref[place, lanes])
            return jnp.where(is_even, far, near), jnp.where(is_even, near, far)

        speed_below = near_out_ref[total:, lanes]
        speed_above = received(slice(total, total + levels))[1]
        speed_below = jnp.where(lat > 0, speed_below, 0.0)
        speed_above = jnp.where(lat < lax.axis_size("lat") - 1, speed_above, 0.0)
        for which, (partial_ref, out_ref) in enumerate(
            [(edge_mine_ref, mine_ref), (edge_send_ref, send_ref)]
        ):
            for i in range(share):
                t = lax.rem(core + which, PAIR) * share + i
                place = pl.ds(pl.multiple_of(t * levels, levels), levels)
                below, above = received(place)
                near_own, far_own = near_out_ref[place, lanes], far_out_ref[place, lanes]
                south = jnp.where(is_even, far_own, near_own)
                north = jnp.where(is_even, near_own, far_own)
                out_ref[i, 0, :, lanes] = partial_ref[i, 0, :, lanes] + flux_of(speed_below, below, south)
                out_ref[i, 1, :, lanes] = partial_ref[i, 1, :, lanes] - flux_of(speed_above, north, above)


def forward_kernel(mine_ref, theirs_ref, phase_ref, high_ref, low_ref, message_ref, held_ref, stack_ref):
    share, number, levels, columns = mine_ref.shape
    piece = columns * PAIR // HALF
    padded = stack_ref.shape[1]
    modes = high_ref.shape[1] // 2
    group = levels * 2 * (HALF + 1)
    core = lax.rem(lax.axis_index("lon"), PAIR)
    count = share * number
    for n in range(count):
        i, j = divmod(n, number)
        held_ref[core, n, :, :columns] = mine_ref[i, j]
        held_ref[1 - core, n, :, :columns] = theirs_ref[i, j]
        for pos in range(PAIR):
            held_ref[pos, n, :, columns:] = jnp.zeros((levels, held_ref.shape[3] - columns), jnp.float32)
        message_ref[n, :, 2 * MODES :] = held_ref[PAIR - 1, n, :, columns - LANES : columns]

    @pl.when(is_cap(lax.axis_index("lat")))
    def _():
        for n in range(count):
            for tile in range(0, padded, LANES):
                lanes = slice(tile, tile + LANES)
                x = []
                for u in range(HALF):
                    pos, start = divmod(u * piece, columns)
                    x.append(held_ref[pos, n, :, start + tile : start + tile + LANES])
                for r, (re, im) in enumerate(half_dft(x)):
                    base = n * group + 2 * r * levels
                    if r == 0:
                        im = jnp.zeros_like(re)
                    else:
                        c, s = phase_ref[2 * r : 2 * r + 1, lanes], phase_ref[2 * r + 1 : 2 * r + 2, lanes]
                        if im is None:
                            re, im = re * c, -(re * s)
                        else:
                            re, im = re * c + im * s, im * c - re * s
                    stack_ref[base : base + levels, lanes] = re
                    stack_ref[base + levels : base + 2 * levels, lanes] = im
        coeffs = product(stack_ref[...], high_ref[...], low_ref[...])
        upper = lax.broadcasted_iota(jnp.int32, (levels, modes), 1) >= modes // 2
        for n in range(count):
            first = None
            for r in [0, HALF] + list(range(1, HALF)):
                base = n * group + 2 * r * levels
                re, im = coeffs[base : base + levels], coeffs[base + levels : base + 2 * levels]
                x_re = re[:, :modes] + im[:, modes:]
                x_im = im[:, :modes] - re[:, modes:]
                if r == 0:
                    first = x_re, x_im
                    continue
                slot = r
                if r == HALF:
                    x_re = jnp.where(upper, first[0], pltpu.roll(x_re, modes // 2, 1))
                    x_im = jnp.where(upper, first[1], pltpu.roll(x_im, modes // 2, 1))
                    slot = 0
                message_ref[n, :, 2 * slot * modes : (2 * slot + 1) * modes] = x_re
                message_ref[n, :, (2 * slot + 1) * modes : (2 * slot + 2) * modes] = x_im


def row_vector(ref, row, levels):
    level = lax.broadcasted_iota(jnp.int32, (levels, LANES), 0)
    out = jnp.full((levels, LANES), ref[row, 0])
    for i in range(1, levels):
        out = jnp.where(level == i, ref[row, i], out)
    return out


def displaced(block, distance, share):
    repeat = block.shape[1] // LANES
    distances = jnp.concatenate([distance] * repeat, axis=1)
    shares = jnp.concatenate([share] * repeat, axis=1)
    for bit in range(SMAX.bit_length()):
        pushed = pltpu.roll(block, 1 << bit, 1)
        block = jnp.where((distances >> bit) & 1 == 1, pushed, block)
    return (1.0 - shares) * block + shares * pltpu.roll(block, 1, 1)


def wave_angle(steps, lon_cells):
    steps = lax.rem(steps, lon_cells)
    return steps.astype(jnp.float32) * (2.0 * math.pi / lon_cells)


def shift_kernel(
    rows, columns, shift_ref, fraction_ref, cutoff_ref, wave_ref, held_ref, moved_ref, gain_ref
):
    _, count, levels, padded = held_ref.shape
    number = len(rows)
    lon_cells = columns * PAIR * PAIR
    modes = gain_ref.shape[3]
    lat = lax.axis_index("lat")
    for j, row in enumerate(rows):
        distance = row_vector(shift_ref, row, levels)
        share = row_vector(fraction_ref, row, levels)
        for n in range(j, count, number):
            for pos in range(PAIR):
                for lanes in spans(padded, SPAN):
                    if lanes.start:
                        block = held_ref[pos, n, :, lanes.start - LANES : lanes.stop]
                    else:
                        tail = held_ref[PAIR - 1 - pos, n, :, columns - LANES : columns]
                        block = jnp.concatenate([tail, held_ref[pos, n, :, lanes]], axis=1)
                    moved_ref[n, pos, :, lanes] = displaced(block, distance, share)[:, LANES:]

    @pl.when(is_cap(lat))
    def _():
        lane = lax.broadcasted_iota(jnp.int32, (levels, modes), 1)
        mode = lane - modes // 2
        for j, row in enumerate(rows):
            distance = row_vector(shift_ref, row, levels)
            share = row_vector(fraction_ref, row, levels)
            limit = cutoff_ref[lat * shift_ref.shape[0] + row]
            wide = wave_angle(RADIX * mode * distance, lon_cells)
            wide_re, wide_im = jnp.cos(wide), -jnp.sin(wide)
            fine = wave_angle(lane * distance, lon_cells)
            fine_re, fine_im = jnp.cos(fine), -jnp.sin(fine)
            for r in range(HALF + 1):
                wavenumber = RADIX * mode + r
                kept = jnp.abs(wavenumber) <= limit
                if r in (0, HALF):
                    kept = kept & (wavenumber >= 0)
                weight = jnp.full((levels, modes), (1.0 if r % 2 == 0 and r not in (0, HALF) else 2.0) / lon_cells)
                if r == 0:
                    weight = jnp.where(wavenumber == 0, 1.0 / lon_cells, weight)
                weight = jnp.where(kept, weight, 0.0)
                mix_re = (1.0 - share) + share * wave_ref[2 * r : 2 * r + 1]
                mix_im = -share * wave_ref[2 * r + 1 : 2 * r + 2]
                turn_re, turn_im = fine_re[:, r : r + 1], fine_im[:, r : r + 1]
                re, im = wide_re * turn_re - wide_im * turn_im, wide_re * turn_im + wide_im * turn_re
                gain_ref[j, 2 * r] = (re * mix_re - im * mix_im) * weight
                gain_ref[j, 2 * r + 1] = (re * mix_im + im * mix_re) * weight


def inverse_kernel(
    rows, columns, shift_ref, fraction_ref, damping_ref, phase_ref, high_ref, low_ref,
    held_ref, moved_ref, gain_ref, own_ref, other_ref, mine_ref, send_ref,
    stack_ref, back_ref, pair_ref,
):
    _, count, levels, _ = held_ref.shape
    number = len(rows)
    piece = columns * PAIR // HALF
    padded = stack_ref.shape[1]
    modes = gain_ref.shape[3]
    group = levels * 2 * (HALF + 1)
    lat = lax.axis_index("lat")
    core = lax.rem(lax.axis_index("lon"), PAIR)
    cap = is_cap(lat)
    for j, row in enumerate(rows):
        distance = row_vector(shift_ref, row, levels)
        share = row_vector(fraction_ref, row, levels)
        for n in range(j, count, number):
            rim = other_ref[n, :, 2 * MODES :]
            block = jnp.concatenate([rim, held_ref[0, n, :, :LANES]], axis=1)
            moved_ref[n, 0, :, :LANES] = displaced(block, distance, share)[:, LANES:]

    @pl.when(jnp.logical_not(cap))
    def _():
        for n in range(count):
            i, j = divmod(n, number)
            mine_ref[i, j] = moved_ref[n, core, :, :columns]
            send_ref[i, j] = moved_ref[n, 1 - core, :, :columns]

    @pl.when(cap)
    def _():
        for n in range(count):
            j = n % number
            for r in range(HALF + 1):
                slot = r % HALF
                ours, theirs = (
                    [ref[n, :, (2 * slot + part) * modes : (2 * slot + part + 1) * modes] for part in range(2)]
                    for ref in (own_ref, other_ref)
                )
                if r % 2:
                    re, im = ours[0] - theirs[0], ours[1] - theirs[1]
                else:
                    re, im = ours[0] + theirs[0], ours[1] + theirs[1]
                if r == HALF:
                    re, im = pltpu.roll(re, modes // 2, 1), pltpu.roll(im, modes // 2, 1)
                g_re, g_im = gain_ref[j, 2 * r], gain_ref[j, 2 * r + 1]
                re, im = re * g_re - im * g_im, re * g_im + im * g_re
                base = n * group + 2 * r * levels
                back_ref[base : base + levels, :modes] = re
                back_ref[base : base + levels, modes:] = -im
                back_ref[base + levels : base + 2 * levels, :modes] = im
                back_ref[base + levels : base + 2 * levels, modes:] = re
        stack_ref[...] = product(back_ref[...], high_ref[...], low_ref[...])
        for n in range(count):
            i, j = divmod(n, number)
            keep = damping_ref[lat * shift_ref.shape[0] + rows[j]]
            for tile in range(0, padded, LANES):
                lanes = slice(tile, tile + LANES)
                spectrum = []
                for r in range(HALF + 1):
                    base = n * group + 2 * r * levels
                    re = stack_ref[base : base + levels, lanes]
                    im = stack_ref[base + levels : base + 2 * levels, lanes]
                    if r > 0:
                        c, s = phase_ref[2 * r : 2 * r + 1, lanes], phase_ref[2 * r + 1 : 2 * r + 2, lanes]
                        re, im = re * c - im * s, re * s + im * c
                    spectrum.append((re, im))
                width = min(LANES, piece - tile)
                for u, value in enumerate(half_inverse(spectrum)):
                    pos, start = divmod(u * piece, columns)
                    start += tile
                    shifted = moved_ref[n, pos, :, start : start + LANES]
                    result = keep * shifted + (1.0 - keep) * value
                    pair_ref[pos, n, :, start : start + width] = result[:, :width]
        for n in range(count):
            i, j = divmod(n, number)
            mine_ref[i, j] = pair_ref[core, n, :, :columns]
            send_ref[i, j] = pair_ref[1 - core, n, :, :columns]


def end_kernel(inner_ref, inner_back_ref, outer_ref, outer_back_ref, out_ref):
    tracer_count, levels, row_count, columns = out_ref.shape
    share = tracer_count // PAIR
    core = lax.rem(lax.axis_index("lon"), PAIR)
    for which, (inner, outer) in enumerate([(inner_ref, outer_ref), (inner_back_ref, outer_back_ref)]):
        for i in range(share):
            t = lax.rem(core + which, PAIR) * share + i
            for j in range(row_count):
                if j in (0, row_count - 1):
                    out_ref[t, :, j, :] = outer[i, min(j, 1)]
                else:
                    out_ref[t, :, j, :] = inner[i, j - 1]


def filter_tables(lon_cells):
    piece = lon_cells // RADIX
    padded = -(-piece // LANES) * LANES
    modes = 2 * MODES // RADIX
    q = np.arange(modes) - modes // 2
    angle = 2 * np.pi * (np.arange(piece)[:, None] * q[None, :] % piece) / piece
    table = np.zeros((padded, 2 * modes))
    table[:piece, :modes] = np.cos(angle)
    table[:piece, modes:] = np.sin(angle)
    high = table.astype(jnp.bfloat16)
    low = (table - high.astype(np.float64)).astype(jnp.bfloat16)
    r = np.arange(HALF + 1)[:, None]

    def waves(steps):
        angle = 2 * np.pi * steps / lon_cells
        pairs = np.stack([np.cos(angle), np.sin(angle)], axis=1)
        return pairs.reshape(-1, steps.shape[1]).astype(np.float32)

    phase = waves(r * np.arange(padded)[None, :])
    wave = waves(RADIX * q[None, :] + r)
    return phase, wave, high, low, np.ascontiguousarray(high.T), np.ascontiguousarray(low.T)


def call(kernel, outs, operands, scratch=(), flops=0):
    vmem = pl.BlockSpec(memory_space=pltpu.VMEM)
    smem = pl.BlockSpec(memory_space=pltpu.SMEM)
    scalars = [v for v, place in operands if place]
    specs = [smem if place else vmem for v, place in operands]
    shapes = [jax.ShapeDtypeStruct(shape, jnp.float32) for shape in outs]
    size = sum(4 * math.prod(shape) for shape in outs)
    return pl.pallas_call(
        kernel,
        out_shape=shapes,
        in_specs=specs,
        out_specs=[vmem] * len(shapes),
        scratch_shapes=[pltpu.VMEM(shape, jnp.float32) for shape in scratch],
        compiler_params=pltpu.CompilerParams(vmem_limit_bytes=24 << 20),
        cost_estimate=pl.CostEstimate(flops=flops, bytes_accessed=2 * size, transcendentals=0),
    )(*[v for v, place in operands])


def permuted(value, axis, pairs):
    return lax.ppermute(value, axis, pairs)


def body(tracers, merid_courant, zonal_shift, zonal_fraction, cutoff, damping):
    tracer_count, level_count, row_count, column_count = tracers.shape
    lat_count = lax.axis_size("lat")
    lon_count = lax.axis_size("lon")
    assert lon_count == PAIR * PAIR and tracer_count % PAIR == 0 and row_count > 2
    share = tracer_count // PAIR
    top = row_count - 1
    lon_cells = column_count * lon_count
    phase, wave, fwd_high, fwd_low, inv_high, inv_low = [jnp.asarray(t) for t in filter_tables(lon_cells)]
    padded, double = fwd_high.shape
    width = -(-column_count // LANES) * LANES
    assert column_count - lon_cells // RADIX + padded <= width
    group = level_count * 2 * (HALF + 1)
    shift_rows, fraction_rows = zonal_shift.T, zonal_fraction.T

    swap_core = lambda v: permuted(v, "lon", [(p, p ^ 1) for p in range(lon_count)])
    swap_half = lambda v: permuted(v, "lon", [(p, p ^ 2) for p in range(lon_count)])
    caps = [b for b in range(lat_count) if b < lat_count // 4 or b >= lat_count - lat_count // 4]

    edge_shape = ((tracer_count + 1) * level_count, column_count)
    inner_shape = (share, row_count - 2, level_count, column_count)
    outer_shape = (share, 2, level_count, column_count)
    near_out, far_out, inner_mine, inner_send, outer_mine, outer_send = call(
        begin_kernel,
        [edge_shape] * 2 + [inner_shape] * 2 + [outer_shape] * 2,
        [(tracers, 0), (merid_courant, 0)],
    )
    inner_theirs = swap_core(inner_send)

    def halo(value, first, to_caps):
        pairs = []
        for b in range(first, lat_count - 1, 2):
            pairs += [(s, d) for s, d in ((b, b + 1), (b + 1, b)) if (d in caps) == to_caps]
        return permuted(value, "lat", pairs)

    near_first, far_first = halo(near_out, 0, True), halo(far_out, 1, True)

    def forward(mine, theirs):
        count = mine.shape[0] * mine.shape[1]
        message, held = call(
            forward_kernel,
            [(count, level_count, 2 * MODES + LANES), (PAIR, count, level_count, width)],
            [(v, 0) for v in (mine, theirs, phase, fwd_high, fwd_low)],
            [(count * group, padded)],
            2 * 3 * count * group * padded * double,
        )
        return message, held

    def shifted(rows, held):
        count = held.shape[1]
        return call(
            functools.partial(shift_kernel, rows, column_count),
            [(count, PAIR, level_count, width), (len(rows), 2 * (HALF + 1), level_count, double // 2)],
            [(shift_rows, 1), (fraction_rows, 1), (cutoff, 1), (wave, 0), (held, 0)],
        )

    def inverse(rows, held, moved, gain, own, other):
        count = held.shape[1]
        shape = (share, len(rows), level_count, column_count)
        return call(
            functools.partial(inverse_kernel, rows, column_count),
            [shape, shape],
            [(shift_rows, 1), (fraction_rows, 1), (damping, 1)]
            + [(v, 0) for v in (phase, inv_high, inv_low, held, moved, gain, own, other)],
            [(count * group, padded), (count * group, double), (PAIR, count, level_count, width)],
            2 * 3 * count * group * padded * double,
        )

    inner_rows, outer_rows = list(range(1, top)), [0, top]
    inner_own, inner_held = forward(inner_mine, inner_theirs)
    inner_other = swap_half(inner_own)
    near_later, far_later = halo(near_out, 0, False), halo(far_out, 1, False)
    inner_moved, inner_gain = shifted(inner_rows, inner_held)

    outer_mine, outer_send = call(
        edge_kernel,
        [outer_shape] * 2,
        [(v, 0) for v in (near_out, far_out, near_first, near_later, far_first, far_later, outer_mine, outer_send)],
    )
    outer_theirs = swap_core(outer_send)
    outer_own, outer_held = forward(outer_mine, outer_theirs)
    outer_other = swap_half(outer_own)
    outer_moved, outer_gain = shifted(outer_rows, outer_held)

    inner_mine, inner_send = inverse(
        inner_rows, inner_held, inner_moved, inner_gain, inner_own, inner_other
    )
    inner_back = swap_core(inner_send)
    outer_mine, outer_send = inverse(
        outer_rows, outer_held, outer_moved, outer_gain, outer_own, outer_other
    )
    outer_back = swap_core(outer_send)
    (result,) = call(
        end_kernel,
        [tracers.shape],
        [(v, 0) for v in (inner_mine, inner_back, outer_mine, outer_back)],
    )
    return result


def solution(mesh):
    placed = (
        P(None, None, "lat", "lon"),
        P(None, "lat", "lon"),
        P(None, "lat"),
        P(None, "lat"),
        P(),
        P(),
    )
    return jax.shard_map(
        body, mesh=mesh, in_specs=placed, out_specs=P(None, None, "lat", "lon"), check_vma=False
    )
```

```python
import functools
import math

import jax
import jax.numpy as jnp
import numpy as np
from jax import lax
from jax.experimental import pallas as pl
from jax.experimental.pallas import tpu as pltpu
from jax.sharding import PartitionSpec as P

MODES = 1024
SMAX = 64
RADIX = 16
HALF = RADIX // 2
LANES = 128
PAIR = 2


def times_phase(value, numerator, denominator):
    re, im = value
    eighth = (8 * numerator % (8 * denominator)) / denominator
    if eighth == 0:
        return re, im
    if eighth == 2:
        return -im, re
    if eighth == 4:
        return -re, -im
    if eighth == 6:
        return im, -re
    c = math.cos(2 * math.pi * numerator / denominator)
    s = math.sin(2 * math.pi * numerator / denominator)
    if eighth == 7:
        return (re + im) * c, (im - re) * c
    if eighth == 1:
        return (re - im) * c, (re + im) * c
    return re * c - im * s, re * s + im * c


def real_dft(values):
    n = len(values)
    if n == 2:
        return [(values[0] + values[1], None), (values[0] - values[1], None)]
    even, odd = real_dft(values[0::2]), real_dft(values[1::2])
    out = [None] * (n // 2 + 1)
    for r in range(n // 4 + 1):
        (er, ei), (tr, ti) = even[r], odd[r]
        if r == 0:
            out[0] = (er + tr, None)
            out[n // 2] = (er - tr, None)
        elif r == n // 4:
            out[r] = (er, -tr)
        else:
            tr, ti = times_phase((tr, ti), -r, n)
            out[r] = (er + tr, ei + ti)
            out[n // 2 - r] = (er - tr, ti - ei)
    return out


def real_inverse(spectrum):
    n = 2 * (len(spectrum) - 1)
    if n == 2:
        a, b = spectrum[0][0], spectrum[1][0]
        return [a + b, a - b]
    even, odd = [None] * (n // 4 + 1), [None] * (n // 4 + 1)
    for r in range(n // 4 + 1):
        (ar, ai), (br, bi) = spectrum[r], spectrum[n // 2 - r]
        if r == 0:
            even[0] = (ar + br, None)
            odd[0] = (ar - br, None)
        elif r == n // 4:
            even[r] = (ar + ar, None)
            odd[r] = (-(ai + ai), None)
        else:
            even[r] = (ar + br, ai - bi)
            odd[r] = times_phase((ar - br, ai + bi), r, n)
    out = [None] * n
    out[0::2] = real_inverse(even)
    out[1::2] = real_inverse(odd)
    return out


def four(values, sign):
    (ar, ai), (br, bi), (cr, ci), (dr, di) = values
    pr, pi, mr, mi = ar + cr, ai + ci, ar - cr, ai - ci
    qr, qi, nr, ni = br + dr, bi + di, br - dr, bi - di
    if sign > 0:
        nr, ni = -nr, -ni
    return [(pr + qr, pi + qi), (mr + ni, mi - nr), (pr - qr, pi - qi), (mr - ni, mi + nr)]


def half_dft(x):
    out = [None] * 9
    out[0::2] = real_dft(x)
    odd = four([times_phase((x[v], -x[v + 4]), -v, 16) for v in range(4)], -1)
    out[1], out[5] = odd[0], odd[1]
    out[7] = (odd[2][0], -odd[2][1])
    out[3] = (odd[3][0], -odd[3][1])
    return out


def half_inverse(w):
    even = real_inverse(w[0::2])
    odd = four([w[1], w[5], (w[7][0], -w[7][1]), (w[3][0], -w[3][1])], 1)
    odd = [times_phase(value, v, 16) for v, value in enumerate(odd)]
    return [even[v] + odd[v][0] for v in range(4)] + [even[v + 4] - odd[v][1] for v in range(4)]


def split(value):
    high = value.astype(jnp.bfloat16)
    return high, (value - high.astype(jnp.float32)).astype(jnp.bfloat16)


def product(left, table_high, table_low, side):
    high, low = split(left)

    def dot(x, y):
        return lax.dot_general(x, y, (((1,), (side,)), ((), ())), preferred_element_type=jnp.float32)

    return dot(high, table_high) + (dot(high, table_low) + dot(low, table_high))


def spans(columns, width):
    return [slice(start, min(start + width, columns)) for start in range(0, columns, width)]


def is_cap(lat):
    count = lax.axis_size("lat")
    return (lat < count // 4) | (lat >= count - count // 4)


def flux_of(face_speed, south, north):
    return jnp.maximum(face_speed, 0.0) * south + jnp.minimum(face_speed, 0.0) * north


def near_is_north():
    return lax.rem(lax.axis_index("lat"), 2) == 0


def inner_kernel(cells_ref, speed_ref, mine_ref, send_ref):
    tracer_count, levels, row_count, columns = cells_ref.shape
    share = tracer_count // PAIR
    core = lax.rem(lax.axis_index("lon"), PAIR)
    for lanes in spans(columns, 3 * LANES):
        speed = [speed_ref[:, j, lanes] for j in range(row_count)]
        for which, out_ref in enumerate([mine_ref, send_ref]):
            for i in range(share):
                t = lax.rem(core + which, PAIR) * share + i
                x = [cells_ref[t, :, j, lanes] for j in range(row_count)]
                flux = [flux_of(speed[j], x[j - 1], x[j]) for j in range(1, row_count)]
                for j in range(1, row_count - 1):
                    out_ref[i, j - 1, :, lanes] = x[j] + flux[j - 1] - flux[j]


def outer_kernel(cells_ref, speed_ref, after_ref, near_ref, far_ref, near_part_ref, far_part_ref):
    tracer_count, levels, row_count, columns = cells_ref.shape
    north = near_is_north()
    for lanes in spans(columns, 3 * LANES):
        speed = [speed_ref[:, j, lanes] for j in (0, 1, row_count - 1)]
        near_ref[tracer_count * levels :, lanes] = speed[0]
        far_ref[tracer_count * levels :, lanes] = speed[0]
        for t in range(tracer_count):
            first, second = cells_ref[t, :, 0, lanes], cells_ref[t, :, 1, lanes]
            third, last = cells_ref[t, :, row_count - 2, lanes], cells_ref[t, :, row_count - 1, lanes]
            place = slice(t * levels, (t + 1) * levels)
            near_ref[place, lanes] = jnp.where(north, last, first)
            far_ref[place, lanes] = jnp.where(north, first, last)
            south_part = first - flux_of(speed[1], first, second)
            north_part = last + flux_of(speed[2], third, last)
            near_part_ref[t, :, lanes] = jnp.where(north, north_part, south_part)
            far_part_ref[t, :, lanes] = jnp.where(north, south_part, north_part)


def edge_kernel(is_near, own_ref, got_ref, part_ref, after_ref, mine_ref, send_ref):
    tracer_count, levels, columns = part_ref.shape
    share = tracer_count // PAIR
    total = tracer_count * levels
    core = lax.rem(lax.axis_index("lon"), PAIR)
    lat = lax.axis_index("lat")
    north = near_is_north() if is_near else jnp.logical_not(near_is_north())
    wall = jnp.where(north, lat == lax.axis_size("lat") - 1, lat == 0)
    for lanes in spans(columns, 3 * LANES):
        speed = jnp.where(north, got_ref[total:, lanes], own_ref[total:, lanes])
        speed = jnp.where(wall, 0.0, speed)
        for which, out_ref in enumerate([mine_ref, send_ref]):
            for i in range(share):
                t = lax.rem(core + which, PAIR) * share + i
                place = pl.ds(pl.multiple_of(t * levels, levels), levels)
                own, got = own_ref[place, lanes], got_ref[place, lanes]
                flux = flux_of(speed, jnp.where(north, own, got), jnp.where(north, got, own))
                out_ref[i, 0, :, lanes] = part_ref[t, :, lanes] + jnp.where(north, -flux, flux)


def forward_kernel(relay, *refs):
    if relay:
        *refs, relay_ref, stack_ref = refs
        *refs, source_ref, message_ref, held_ref = refs
        relay_ref[...] = source_ref[...]
    else:
        *refs, message_ref, held_ref, stack_ref = refs
    mine_ref, theirs_ref, phase_ref, high_ref, low_ref = refs[:5]
    share, number, levels, columns = mine_ref.shape
    piece = columns * PAIR // HALF
    padded = stack_ref.shape[1]
    modes = high_ref.shape[1] // 2
    group = levels * 2 * (HALF + 1)
    core = lax.rem(lax.axis_index("lon"), PAIR)
    count = share * number
    for n in range(count):
        i, j = divmod(n, number)
        held_ref[core, n, :, :columns] = mine_ref[i, j]
        held_ref[1 - core, n, :, :columns] = theirs_ref[i, j]
        for pos in range(PAIR):
            held_ref[pos, n, :, columns:] = jnp.zeros((levels, held_ref.shape[3] - columns), jnp.float32)
        message_ref[n, :, 2 * MODES :] = held_ref[PAIR - 1, n, :, columns - LANES : columns]

    @pl.when(is_cap(lax.axis_index("lat")))
    def _():
        for n in range(count):
            for tile in range(0, padded, LANES):
                lanes = slice(tile, tile + LANES)
                x = []
                for u in range(HALF):
                    pos, start = divmod(u * piece, columns)
                    x.append(held_ref[pos, n, :, start + tile : start + tile + LANES])
                for r, (re, im) in enumerate(half_dft(x)):
                    base = n * group + 2 * r * levels
                    if r == 0:
                        im = jnp.zeros_like(re)
                    else:
                        c, s = phase_ref[2 * r : 2 * r + 1, lanes], phase_ref[2 * r + 1 : 2 * r + 2, lanes]
                        if im is None:
                            re, im = re * c, -(re * s)
                        else:
                            re, im = re * c + im * s, im * c - re * s
                    stack_ref[base : base + levels, lanes] = re
                    stack_ref[base + levels : base + 2 * levels, lanes] = im
        coeffs = product(stack_ref[...], high_ref[...], low_ref[...], 0)
        upper = lax.broadcasted_iota(jnp.int32, (levels, modes), 1) >= modes // 2
        for n in range(count):
            first = None
            for r in [0, HALF] + list(range(1, HALF)):
                base = n * group + 2 * r * levels
                re, im = coeffs[base : base + levels], coeffs[base + levels : base + 2 * levels]
                x_re = re[:, :modes] + im[:, modes:]
                x_im = im[:, :modes] - re[:, modes:]
                if r == 0:
                    first = x_re, x_im
                    continue
                slot = r
                if r == HALF:
                    x_re = jnp.where(upper, first[0], pltpu.roll(x_re, modes // 2, 1))
                    x_im = jnp.where(upper, first[1], pltpu.roll(x_im, modes // 2, 1))
                    slot = 0
                message_ref[n, :, 2 * slot * modes : (2 * slot + 1) * modes] = x_re
                message_ref[n, :, (2 * slot + 1) * modes : (2 * slot + 2) * modes] = x_im


def row_vector(ref, row, levels):
    level = lax.broadcasted_iota(jnp.int32, (levels, LANES), 0)
    out = jnp.full((levels, LANES), ref[row, 0])
    for i in range(1, levels):
        out = jnp.where(level == i, ref[row, i], out)
    return out


def displaced(tiles, distance, share):
    lane = lax.broadcasted_iota(jnp.int32, distance.shape, 1)

    def moved(steps):
        index = (lane - steps) & (LANES - 1)
        turned = [jnp.take_along_axis(v, index, axis=1, mode="promise_in_bounds") for v in tiles]
        from_left = lane < steps
        return [jnp.where(from_left, a, b) for a, b in zip(turned, turned[1:])]

    pairs = zip(moved(distance), moved(distance + 1))
    return [(1.0 - share) * here + share * earlier for here, earlier in pairs]


def rows_of(which, row_count):
    if which == "inner":
        return list(range(1, row_count - 1))
    north = near_is_north() if which == "near" else jnp.logical_not(near_is_north())
    return [jnp.where(north, row_count - 1, 0)]


def wave_angle(steps, lon_cells):
    steps = lax.rem(steps, lon_cells)
    return steps.astype(jnp.float32) * (2.0 * math.pi / lon_cells)


def shift_kernel(
    which, columns, shift_ref, fraction_ref, cutoff_ref, wave_ref, held_ref, after_ref, moved_ref, gain_ref
):
    _, count, levels, padded = held_ref.shape
    rows = rows_of(which, shift_ref.shape[0])
    number = len(rows)
    lon_cells = columns * PAIR * PAIR
    modes = gain_ref.shape[3]
    lat = lax.axis_index("lat")
    for j, row in enumerate(rows):
        distance = row_vector(shift_ref, row, levels)
        share = row_vector(fraction_ref, row, levels)
        for n in range(j, count, number):
            for pos in range(PAIR):
                tiles = [held_ref[PAIR - 1 - pos, n, :, columns - LANES : columns]]
                tiles += [held_ref[pos, n, :, lanes] for lanes in spans(padded, LANES)]
                for lanes, tile in zip(spans(padded, LANES), displaced(tiles, distance, share)):
                    moved_ref[n, pos, :, lanes] = tile

    @pl.when(is_cap(lat))
    def _():
        lane = lax.broadcasted_iota(jnp.int32, (levels, modes), 1)
        mode = lane - modes // 2
        for j, row in enumerate(rows):
            distance = row_vector(shift_ref, row, levels)
            share = row_vector(fraction_ref, row, levels)
            limit = cutoff_ref[lat * shift_ref.shape[0] + row]
            wide = wave_angle(RADIX * mode * distance, lon_cells)
            wide_re, wide_im = jnp.cos(wide), -jnp.sin(wide)
            fine = wave_angle(lane * distance, lon_cells)
            fine_re, fine_im = jnp.cos(fine), -jnp.sin(fine)
            for r in range(HALF + 1):
                wavenumber = RADIX * mode + r
                kept = jnp.abs(wavenumber) <= limit
                if r in (0, HALF):
                    kept = kept & (wavenumber >= 0)
                weight = jnp.full((levels, modes), (1.0 if r % 2 == 0 and r not in (0, HALF) else 2.0) / lon_cells)
                if r == 0:
                    weight = jnp.where(wavenumber == 0, 1.0 / lon_cells, weight)
                weight = jnp.where(kept, weight, 0.0)
                mix_re = (1.0 - share) + share * wave_ref[2 * r : 2 * r + 1]
                mix_im = -share * wave_ref[2 * r + 1 : 2 * r + 2]
                turn_re, turn_im = fine_re[:, r : r + 1], fine_im[:, r : r + 1]
                re, im = wide_re * turn_re - wide_im * turn_im, wide_re * turn_im + wide_im * turn_re
                gain_ref[j, 2 * r] = (re * mix_re - im * mix_im) * weight
                gain_ref[j, 2 * r + 1] = (re * mix_im + im * mix_re) * weight


def inverse_kernel(
    which, columns, shift_ref, fraction_ref, damping_ref, phase_ref, high_ref, low_ref,
    held_ref, moved_ref, gain_ref, own_ref, other_ref, after_ref, mine_ref, send_ref,
    stack_ref, back_ref, pair_ref,
):
    _, count, levels, _ = held_ref.shape
    rows = rows_of(which, shift_ref.shape[0])
    number = len(rows)
    piece = columns * PAIR // HALF
    padded = stack_ref.shape[1]
    modes = gain_ref.shape[3]
    group = levels * 2 * (HALF + 1)
    lat = lax.axis_index("lat")
    core = lax.rem(lax.axis_index("lon"), PAIR)
    cap = is_cap(lat)
    for j, row in enumerate(rows):
        distance = row_vector(shift_ref, row, levels)
        share = row_vector(fraction_ref, row, levels)
        for n in range(j, count, number):
            tiles = [other_ref[n, :, 2 * MODES :], held_ref[0, n, :, :LANES]]
            (moved_ref[n, 0, :, :LANES],) = displaced(tiles, distance, share)

    @pl.when(jnp.logical_not(cap))
    def _():
        for n in range(count):
            i, j = divmod(n, number)
            mine_ref[i, j] = moved_ref[n, core, :, :columns]
            send_ref[i, j] = moved_ref[n, 1 - core, :, :columns]

    @pl.when(cap)
    def _():
        for n in range(count):
            j = n % number
            for r in range(HALF + 1):
                slot = r % HALF
                ours, theirs = (
                    [ref[n, :, (2 * slot + part) * modes : (2 * slot + part + 1) * modes] for part in range(2)]
                    for ref in (own_ref, other_ref)
                )
                if r % 2:
                    re, im = ours[0] - theirs[0], ours[1] - theirs[1]
                else:
                    re, im = ours[0] + theirs[0], ours[1] + theirs[1]
                if r == HALF:
                    re, im = pltpu.roll(re, modes // 2, 1), pltpu.roll(im, modes // 2, 1)
                g_re, g_im = gain_ref[j, 2 * r], gain_ref[j, 2 * r + 1]
                re, im = re * g_re - im * g_im, re * g_im + im * g_re
                base = n * group + 2 * r * levels
                back_ref[base : base + levels, :modes] = re
                back_ref[base : base + levels, modes:] = -im
                back_ref[base + levels : base + 2 * levels, :modes] = im
                back_ref[base + levels : base + 2 * levels, modes:] = re
        stack_ref[...] = product(back_ref[...], high_ref[...], low_ref[...], 1)
        for n in range(count):
            i, j = divmod(n, number)
            keep = damping_ref[lat * shift_ref.shape[0] + rows[j]]
            for tile in range(0, padded, LANES):
                lanes = slice(tile, tile + LANES)
                spectrum = []
                for r in range(HALF + 1):
                    base = n * group + 2 * r * levels
                    re = stack_ref[base : base + levels, lanes]
                    im = stack_ref[base + levels : base + 2 * levels, lanes]
                    if r > 0:
                        c, s = phase_ref[2 * r : 2 * r + 1, lanes], phase_ref[2 * r + 1 : 2 * r + 2, lanes]
                        re, im = re * c - im * s, re * s + im * c
                    spectrum.append((re, im))
                width = min(LANES, piece - tile)
                for u, value in enumerate(half_inverse(spectrum)):
                    pos, start = divmod(u * piece, columns)
                    start += tile
                    shifted = moved_ref[n, pos, :, start : start + LANES]
                    result = keep * shifted + (1.0 - keep) * value
                    pair_ref[pos, n, :, start : start + width] = result[:, :width]
        for n in range(count):
            i, j = divmod(n, number)
            mine_ref[i, j] = pair_ref[core, n, :, :columns]
            send_ref[i, j] = pair_ref[1 - core, n, :, :columns]


def end_kernel(*refs):
    *refs, out_ref = refs
    tracer_count, levels, row_count, columns = out_ref.shape
    share = tracer_count // PAIR
    core = lax.rem(lax.axis_index("lon"), PAIR)
    north = near_is_north()
    for place, (inner, near, far) in enumerate([refs[:3], refs[3:]]):
        for i in range(share):
            t = lax.rem(core + place, PAIR) * share + i
            for lanes in spans(columns, 4 * LANES):
                a, b = near[i, 0, :, lanes], far[i, 0, :, lanes]
                out_ref[t, :, 0, lanes] = jnp.where(north, b, a)
                out_ref[t, :, row_count - 1, lanes] = jnp.where(north, a, b)
                for j in range(1, row_count - 1):
                    out_ref[t, :, j, lanes] = inner[i, j - 1, :, lanes]


def filter_tables(lon_cells):
    piece = lon_cells // RADIX
    padded = -(-piece // LANES) * LANES
    modes = 2 * MODES // RADIX
    q = np.arange(modes) - modes // 2
    angle = 2 * np.pi * (np.arange(piece)[:, None] * q[None, :] % piece) / piece
    table = np.zeros((padded, 2 * modes))
    table[:piece, :modes] = np.cos(angle)
    table[:piece, modes:] = np.sin(angle)
    high = table.astype(jnp.bfloat16)
    low = (table - high.astype(np.float64)).astype(jnp.bfloat16)
    r = np.arange(HALF + 1)[:, None]

    def waves(steps):
        angle = 2 * np.pi * steps / lon_cells
        pairs = np.stack([np.cos(angle), np.sin(angle)], axis=1)
        return pairs.reshape(-1, steps.shape[1]).astype(np.float32)

    phase = waves(r * np.arange(padded)[None, :])
    wave = waves(RADIX * q[None, :] + r)
    return phase, wave, high, low


SMALL, WHOLE, UNREAD = pltpu.SMEM, pltpu.VMEM, pl.ANY


def call(kernel, outs, operands, scratch=(), flops=0):
    size = sum(4 * math.prod(shape) for shape in outs)
    return pl.pallas_call(
        kernel,
        out_shape=[jax.ShapeDtypeStruct(shape, jnp.float32) for shape in outs],
        in_specs=[pl.BlockSpec(memory_space=place) for _, place in operands],
        out_specs=[pl.BlockSpec(memory_space=WHOLE)] * len(outs),
        scratch_shapes=[pltpu.VMEM(shape, jnp.float32) for shape in scratch],
        compiler_params=pltpu.CompilerParams(vmem_limit_bytes=24 << 20),
        cost_estimate=pl.CostEstimate(flops=flops, bytes_accessed=2 * size, transcendentals=0),
    )(*[v for v, _ in operands])


def whole(*values):
    return [(v, WHOLE) for v in values]


def body(tracers, merid_courant, zonal_shift, zonal_fraction, cutoff, damping):
    tracer_count, level_count, row_count, column_count = tracers.shape
    lat_count = lax.axis_size("lat")
    lon_count = lax.axis_size("lon")
    assert lon_count == PAIR * PAIR and tracer_count % PAIR == 0 and row_count > 2
    share = tracer_count // PAIR
    lon_cells = column_count * lon_count
    phase, wave, high, low = [jnp.asarray(t) for t in filter_tables(lon_cells)]
    padded, double = high.shape
    width = -(-column_count // LANES) * LANES
    assert column_count - lon_cells // RADIX + padded <= width
    group = level_count * 2 * (HALF + 1)
    shift_rows, fraction_rows = zonal_shift.T, zonal_fraction.T

    def swap_core(value):
        return lax.ppermute(value, "lon", [(p, p ^ 1) for p in range(lon_count)])

    def swap_half(value):
        return lax.ppermute(value, "lon", [(p, p ^ 2) for p in range(lon_count)])

    def swap_band(value, first):
        pairs = []
        for b in range(first, lat_count - 1, 2):
            pairs += [(b, b + 1), (b + 1, b)]
        return lax.ppermute(value, "lat", pairs)

    def set_shape(number):
        return (share, number, level_count, column_count)

    def forward(mine, theirs, after, relay=None):
        count = mine.shape[0] * mine.shape[1]
        outs = [(count, level_count, 2 * MODES + LANES), (PAIR, count, level_count, width)]
        operands = whole(mine, theirs, phase, high, low) + [(after, UNREAD)]
        if relay is not None:
            outs.append(relay.shape)
            operands += whole(relay)
        return call(
            functools.partial(forward_kernel, relay is not None),
            outs,
            operands,
            [(count * group, padded)],
            2 * 3 * count * group * padded * double,
        )

    def shifted(which, held, after):
        count = held.shape[1]
        number = count // share
        return call(
            functools.partial(shift_kernel, which, column_count),
            [(count, PAIR, level_count, width), (number, 2 * (HALF + 1), level_count, double // 2)],
            [(shift_rows, SMALL), (fraction_rows, SMALL), (cutoff, SMALL)]
            + whole(wave, held)
            + [(after, UNREAD)],
        )

    def inverse(which, held, moved, gain, own, other, after):
        count = held.shape[1]
        return call(
            functools.partial(inverse_kernel, which, column_count),
            [set_shape(count // share)] * 2,
            [(shift_rows, SMALL), (fraction_rows, SMALL), (damping, SMALL)]
            + whole(phase, high, low, held, moved, gain, own, other)
            + [(after, UNREAD)],
            [(count * group, padded), (count * group, double), (PAIR, count, level_count, width)],
            2 * 3 * count * group * padded * double,
        )

    inner_mine, inner_send = call(
        inner_kernel, [set_shape(row_count - 2)] * 2, whole(tracers, merid_courant)
    )
    inner_theirs = swap_core(inner_send)
    edge_shape = ((tracer_count + 1) * level_count, column_count)
    part_shape = (tracer_count, level_count, column_count)
    near_own, far_own, near_part, far_part = call(
        outer_kernel,
        [edge_shape] * 2 + [part_shape] * 2,
        whole(tracers, merid_courant) + [(inner_mine, UNREAD)],
    )
    near_got = swap_band(near_own, 0)
    inner_own, inner_held, far_relay = forward(inner_mine, inner_theirs, near_part, far_own)
    inner_other = swap_half(inner_own)
    far_got = swap_band(far_relay, 1)
    inner_moved, inner_gain = shifted("inner", inner_held, inner_own)

    near_mine, near_send = call(
        functools.partial(edge_kernel, True),
        [set_shape(1)] * 2,
        whole(near_own, near_got, near_part) + [(inner_moved, UNREAD)],
    )
    near_theirs = swap_core(near_send)
    near_own, near_held, = forward(near_mine, near_theirs, inner_moved)
    near_other = swap_half(near_own)
    near_moved, near_gain = shifted("near", near_held, near_own)

    far_mine, far_send = call(
        functools.partial(edge_kernel, False),
        [set_shape(1)] * 2,
        whole(far_own, far_got, far_part) + [(near_moved, UNREAD)],
    )
    far_theirs = swap_core(far_send)
    far_own, far_held = forward(far_mine, far_theirs, near_moved)
    far_other = swap_half(far_own)
    far_moved, far_gain = shifted("far", far_held, far_own)

    inner = inverse("inner", inner_held, inner_moved, inner_gain, inner_own, inner_other, far_moved)
    inner_back = swap_core(inner[1])
    near = inverse("near", near_held, near_moved, near_gain, near_own, near_other, inner[0])
    near_back = swap_core(near[1])
    far = inverse("far", far_held, far_moved, far_gain, far_own, far_other, near[0])
    far_back = swap_core(far[1])
    (result,) = call(
        end_kernel,
        [tracers.shape],
        whole(inner[0], near[0], far[0], inner_back, near_back, far_back),
    )
    return result


def solution(mesh):
    placed = (
        P(None, None, "lat", "lon"),
        P(None, "lat", "lon"),
        P(None, "lat"),
        P(None, "lat"),
        P(),
        P(),
    )
    return jax.shard_map(
        body, mesh=mesh, in_specs=placed, out_specs=P(None, None, "lat", "lon"), check_vma=False
    )
```

```python
import functools
import math

import jax
import jax.numpy as jnp
import numpy as np
from jax import lax
from jax.experimental import pallas as pl
from jax.experimental.pallas import tpu as pltpu
from jax.sharding import PartitionSpec as P

MODES = 1024
SMAX = 64
RADIX = 16
HALF = RADIX // 2
LANES = 128
PAIR = 2


def times_phase(value, numerator, denominator):
    re, im = value
    eighth = (8 * numerator % (8 * denominator)) / denominator
    if eighth == 0:
        return re, im
    if eighth == 2:
        return -im, re
    if eighth == 4:
        return -re, -im
    if eighth == 6:
        return im, -re
    c = math.cos(2 * math.pi * numerator / denominator)
    s = math.sin(2 * math.pi * numerator / denominator)
    if eighth == 7:
        return (re + im) * c, (im - re) * c
    if eighth == 1:
        return (re - im) * c, (re + im) * c
    return re * c - im * s, re * s + im * c


def real_dft(values):
    n = len(values)
    if n == 2:
        return [(values[0] + values[1], None), (values[0] - values[1], None)]
    even, odd = real_dft(values[0::2]), real_dft(values[1::2])
    out = [None] * (n // 2 + 1)
    for r in range(n // 4 + 1):
        (er, ei), (tr, ti) = even[r], odd[r]
        if r == 0:
            out[0] = (er + tr, None)
            out[n // 2] = (er - tr, None)
        elif r == n // 4:
            out[r] = (er, -tr)
        else:
            tr, ti = times_phase((tr, ti), -r, n)
            out[r] = (er + tr, ei + ti)
            out[n // 2 - r] = (er - tr, ti - ei)
    return out


def real_inverse(spectrum):
    n = 2 * (len(spectrum) - 1)
    if n == 2:
        a, b = spectrum[0][0], spectrum[1][0]
        return [a + b, a - b]
    even, odd = [None] * (n // 4 + 1), [None] * (n // 4 + 1)
    for r in range(n // 4 + 1):
        (ar, ai), (br, bi) = spectrum[r], spectrum[n // 2 - r]
        if r == 0:
            even[0] = (ar + br, None)
            odd[0] = (ar - br, None)
        elif r == n // 4:
            even[r] = (ar + ar, None)
            odd[r] = (-(ai + ai), None)
        else:
            even[r] = (ar + br, ai - bi)
            odd[r] = times_phase((ar - br, ai + bi), r, n)
    out = [None] * n
    out[0::2] = real_inverse(even)
    out[1::2] = real_inverse(odd)
    return out


def four(values, sign):
    (ar, ai), (br, bi), (cr, ci), (dr, di) = values
    pr, pi, mr, mi = ar + cr, ai + ci, ar - cr, ai - ci
    qr, qi, nr, ni = br + dr, bi + di, br - dr, bi - di
    if sign > 0:
        nr, ni = -nr, -ni
    return [(pr + qr, pi + qi), (mr + ni, mi - nr), (pr - qr, pi - qi), (mr - ni, mi + nr)]


def half_dft(x):
    out = [None] * 9
    out[0::2] = real_dft(x)
    odd = four([times_phase((x[v], -x[v + 4]), -v, 16) for v in range(4)], -1)
    out[1], out[5] = odd[0], odd[1]
    out[7] = (odd[2][0], -odd[2][1])
    out[3] = (odd[3][0], -odd[3][1])
    return out


def half_inverse(w):
    even = real_inverse(w[0::2])
    odd = four([w[1], w[5], (w[7][0], -w[7][1]), (w[3][0], -w[3][1])], 1)
    odd = [times_phase(value, v, 16) for v, value in enumerate(odd)]
    return [even[v] + odd[v][0] for v in range(4)] + [even[v + 4] - odd[v][1] for v in range(4)]


def split(value):
    high = value.astype(jnp.bfloat16)
    return high, (value - high.astype(jnp.float32)).astype(jnp.bfloat16)


def product(left, table_high, table_low, side):
    high, low = split(left)

    def dot(x, y):
        return lax.dot_general(x, y, (((1,), (side,)), ((), ())), preferred_element_type=jnp.float32)

    return dot(high, table_high) + (dot(high, table_low) + dot(low, table_high))


def spans(columns, width):
    return [slice(start, min(start + width, columns)) for start in range(0, columns, width)]


def is_cap(lat):
    count = lax.axis_size("lat")
    return (lat < count // 4) | (lat >= count - count // 4)


def flux_of(face_speed, south, north):
    return jnp.maximum(face_speed, 0.0) * south + jnp.minimum(face_speed, 0.0) * north


def near_is_north():
    return lax.rem(lax.axis_index("lat"), 2) == 0


def begin_kernel(
    cells_hbm, speed_hbm, mine_ref, send_ref, near_ref, far_ref, near_part_ref, far_part_ref,
    cells_ref, speed_ref, sems,
):
    tracer_count, levels, row_count, columns = cells_ref.shape
    share = tracer_count // PAIR
    core = lax.rem(lax.axis_index("lon"), PAIR)
    north = near_is_north()
    copies = [pltpu.make_async_copy(speed_hbm, speed_ref, sems.at[tracer_count])]
    copies += [
        pltpu.make_async_copy(cells_hbm.at[t], cells_ref.at[t], sems.at[t]) for t in range(tracer_count)
    ]
    for copy in copies:
        copy.start()
    for copy in copies:
        copy.wait()
    for lanes in spans(columns, 2 * LANES):
        speed = [speed_ref[:, j, lanes] for j in range(row_count)]
        near_ref[tracer_count * levels :, lanes] = speed[0]
        far_ref[tracer_count * levels :, lanes] = speed[0]
        for which, out_ref in enumerate([mine_ref, send_ref]):
            for i in range(share):
                t = lax.rem(core + which, PAIR) * share + i
                place = pl.ds(pl.multiple_of(t * levels, levels), levels)
                x = [cells_ref[t, :, j, lanes] for j in range(row_count)]
                flux = [flux_of(speed[j], x[j - 1], x[j]) for j in range(1, row_count)]
                for j in range(1, row_count - 1):
                    out_ref[i, j - 1, :, lanes] = x[j] + flux[j - 1] - flux[j]
                near_ref[place, lanes] = jnp.where(north, x[-1], x[0])
                far_ref[place, lanes] = jnp.where(north, x[0], x[-1])
                south_part, north_part = x[0] - flux[0], x[-1] + flux[-1]
                near_part_ref[t, :, lanes] = jnp.where(north, north_part, south_part)
                far_part_ref[t, :, lanes] = jnp.where(north, south_part, north_part)


def edge_kernel(is_near, own_ref, got_ref, part_ref, after_ref, *refs):
    if is_near:
        source_ref, mine_ref, send_ref, relay_ref = refs
        relay_ref[...] = source_ref[...]
    else:
        mine_ref, send_ref = refs
    tracer_count, levels, columns = part_ref.shape
    share = tracer_count // PAIR
    total = tracer_count * levels
    core = lax.rem(lax.axis_index("lon"), PAIR)
    lat = lax.axis_index("lat")
    north = near_is_north() if is_near else jnp.logical_not(near_is_north())
    wall = jnp.where(north, lat == lax.axis_size("lat") - 1, lat == 0)
    for lanes in spans(columns, 3 * LANES):
        speed = jnp.where(north, got_ref[total:, lanes], own_ref[total:, lanes])
        speed = jnp.where(wall, 0.0, speed)
        for which, out_ref in enumerate([mine_ref, send_ref]):
            for i in range(share):
                t = lax.rem(core + which, PAIR) * share + i
                place = pl.ds(pl.multiple_of(t * levels, levels), levels)
                own, got = own_ref[place, lanes], got_ref[place, lanes]
                flux = flux_of(speed, jnp.where(north, own, got), jnp.where(north, got, own))
                out_ref[i, 0, :, lanes] = part_ref[t, :, lanes] + jnp.where(north, -flux, flux)


def forward_kernel(
    mine_ref, theirs_ref, phase_ref, high_ref, low_ref, after_ref, message_ref, held_ref, stack_ref
):
    share, number, levels, columns = mine_ref.shape
    piece = columns * PAIR // HALF
    padded = stack_ref.shape[1]
    modes = high_ref.shape[1] // 2
    group = levels * 2 * (HALF + 1)
    core = lax.rem(lax.axis_index("lon"), PAIR)
    count = share * number
    for n in range(count):
        i, j = divmod(n, number)
        held_ref[core, n, :, :columns] = mine_ref[i, j]
        held_ref[1 - core, n, :, :columns] = theirs_ref[i, j]
        for pos in range(PAIR):
            held_ref[pos, n, :, columns:] = jnp.zeros((levels, held_ref.shape[3] - columns), jnp.float32)
        message_ref[n, :, 2 * MODES :] = held_ref[PAIR - 1, n, :, columns - LANES : columns]

    @pl.when(is_cap(lax.axis_index("lat")))
    def _():
        for n in range(count):
            for tile in range(0, padded, LANES):
                lanes = slice(tile, tile + LANES)
                x = []
                for u in range(HALF):
                    pos, start = divmod(u * piece, columns)
                    x.append(held_ref[pos, n, :, start + tile : start + tile + LANES])
                for r, (re, im) in enumerate(half_dft(x)):
                    base = n * group + 2 * r * levels
                    if r == 0:
                        im = jnp.zeros_like(re)
                    else:
                        c, s = phase_ref[2 * r : 2 * r + 1, lanes], phase_ref[2 * r + 1 : 2 * r + 2, lanes]
                        if im is None:
                            re, im = re * c, -(re * s)
                        else:
                            re, im = re * c + im * s, im * c - re * s
                    stack_ref[base : base + levels, lanes] = re
                    stack_ref[base + levels : base + 2 * levels, lanes] = im
        coeffs = product(stack_ref[...], high_ref[...], low_ref[...], 0)
        upper = lax.broadcasted_iota(jnp.int32, (levels, modes), 1) >= modes // 2
        for n in range(count):
            first = None
            for r in [0, HALF] + list(range(1, HALF)):
                base = n * group + 2 * r * levels
                re, im = coeffs[base : base + levels], coeffs[base + levels : base + 2 * levels]
                x_re = re[:, :modes] + im[:, modes:]
                x_im = im[:, :modes] - re[:, modes:]
                if r == 0:
                    first = x_re, x_im
                    continue
                slot = r
                if r == HALF:
                    x_re = jnp.where(upper, first[0], pltpu.roll(x_re, modes // 2, 1))
                    x_im = jnp.where(upper, first[1], pltpu.roll(x_im, modes // 2, 1))
                    slot = 0
                message_ref[n, :, 2 * slot * modes : (2 * slot + 1) * modes] = x_re
                message_ref[n, :, (2 * slot + 1) * modes : (2 * slot + 2) * modes] = x_im


def row_vector(ref, row, levels):
    level = lax.broadcasted_iota(jnp.int32, (levels, LANES), 0)
    out = jnp.full((levels, LANES), ref[row, 0])
    for i in range(1, levels):
        out = jnp.where(level == i, ref[row, i], out)
    return out


def displaced(tiles, distance, share):
    lane = lax.broadcasted_iota(jnp.int32, distance.shape, 1)

    def moved(steps):
        index = (lane - steps) & (LANES - 1)
        turned = [jnp.take_along_axis(v, index, axis=1, mode="promise_in_bounds") for v in tiles]
        from_left = lane < steps
        return [jnp.where(from_left, a, b) for a, b in zip(turned, turned[1:])]

    pairs = zip(moved(distance), moved(distance + 1))
    return [(1.0 - share) * here + share * earlier for here, earlier in pairs]


def rows_of(which, row_count):
    if which == "inner":
        return list(range(1, row_count - 1))
    north = near_is_north() if which == "near" else jnp.logical_not(near_is_north())
    return [jnp.where(north, row_count - 1, 0)]


def wave_angle(steps, lon_cells):
    steps = lax.rem(steps, lon_cells)
    return steps.astype(jnp.float32) * (2.0 * math.pi / lon_cells)


def row_kernel(
    columns, shift_ref, fraction_ref, cutoff_ref, damping_ref, wave_ref, after_ref,
    distance_ref, share_ref, keep_ref, gain_ref,
):
    row_count, levels = shift_ref.shape
    lon_cells = columns * PAIR * PAIR
    modes = gain_ref.shape[3]
    lat = lax.axis_index("lat")
    for row in range(row_count):
        distance_ref[row] = row_vector(shift_ref, row, levels).astype(jnp.float32)
        share_ref[row] = row_vector(fraction_ref, row, levels)
        keep_ref[row] = jnp.full((levels, LANES), damping_ref[lat * row_count + row])

    @pl.when(is_cap(lat))
    def _():
        lane = lax.broadcasted_iota(jnp.int32, (levels, modes), 1)
        mode = lane - modes // 2
        for row in range(row_count):
            distance = distance_ref[row].astype(jnp.int32)
            share = share_ref[row]
            limit = cutoff_ref[lat * row_count + row]
            wide = wave_angle(RADIX * mode * distance, lon_cells)
            wide_re, wide_im = jnp.cos(wide), -jnp.sin(wide)
            fine = wave_angle(lane * distance, lon_cells)
            fine_re, fine_im = jnp.cos(fine), -jnp.sin(fine)
            for r in range(HALF + 1):
                wavenumber = RADIX * mode + r
                kept = jnp.abs(wavenumber) <= limit
                if r in (0, HALF):
                    kept = kept & (wavenumber >= 0)
                once = r % 2 == 0 and r not in (0, HALF)
                weight = jnp.full((levels, modes), (1.0 if once else 2.0) / lon_cells)
                if r == 0:
                    weight = jnp.where(wavenumber == 0, 1.0 / lon_cells, weight)
                weight = jnp.where(kept, weight, 0.0)
                mix_re = (1.0 - share) + share * wave_ref[2 * r : 2 * r + 1]
                mix_im = -share * wave_ref[2 * r + 1 : 2 * r + 2]
                turn_re, turn_im = fine_re[:, r : r + 1], fine_im[:, r : r + 1]
                re, im = wide_re * turn_re - wide_im * turn_im, wide_re * turn_im + wide_im * turn_re
                gain_ref[row, 2 * r] = (re * mix_re - im * mix_im) * weight
                gain_ref[row, 2 * r + 1] = (re * mix_im + im * mix_re) * weight


def shift_kernel(which, columns, distance_ref, share_ref, held_ref, after_ref, moved_ref):
    _, count, levels, padded = held_ref.shape
    rows = rows_of(which, share_ref.shape[0])
    number = len(rows)
    for j, row in enumerate(rows):
        distance, share = distance_ref[row].astype(jnp.int32), share_ref[row]
        for n in range(j, count, number):
            for pos in range(PAIR):
                tiles = [held_ref[PAIR - 1 - pos, n, :, columns - LANES : columns]]
                tiles += [held_ref[pos, n, :, lanes] for lanes in spans(padded, LANES)]
                for lanes, tile in zip(spans(padded, LANES), displaced(tiles, distance, share)):
                    moved_ref[n, pos, :, lanes] = tile


def inverse_kernel(
    which, columns, distance_ref, share_ref, keep_ref, gain_ref, phase_ref, high_ref, low_ref,
    held_ref, moved_ref, own_ref, other_ref, after_ref, mine_ref, send_ref,
    stack_ref, back_ref, pair_ref,
):
    _, count, levels, _ = held_ref.shape
    rows = rows_of(which, share_ref.shape[0])
    number = len(rows)
    piece = columns * PAIR // HALF
    padded = stack_ref.shape[1]
    modes = gain_ref.shape[3]
    group = levels * 2 * (HALF + 1)
    core = lax.rem(lax.axis_index("lon"), PAIR)
    cap = is_cap(lax.axis_index("lat"))
    for j, row in enumerate(rows):
        distance, share = distance_ref[row].astype(jnp.int32), share_ref[row]
        for n in range(j, count, number):
            tiles = [other_ref[n, :, 2 * MODES :], held_ref[0, n, :, :LANES]]
            (moved_ref[n, 0, :, :LANES],) = displaced(tiles, distance, share)

    @pl.when(jnp.logical_not(cap))
    def _():
        for n in range(count):
            i, j = divmod(n, number)
            mine_ref[i, j] = moved_ref[n, core, :, :columns]
            send_ref[i, j] = moved_ref[n, 1 - core, :, :columns]

    @pl.when(cap)
    def _():
        for n in range(count):
            row = rows[n % number]
            for r in range(HALF + 1):
                slot = r % HALF
                ours, theirs = (
                    [ref[n, :, (2 * slot + part) * modes : (2 * slot + part + 1) * modes] for part in range(2)]
                    for ref in (own_ref, other_ref)
                )
                if r % 2:
                    re, im = ours[0] - theirs[0], ours[1] - theirs[1]
                else:
                    re, im = ours[0] + theirs[0], ours[1] + theirs[1]
                if r == HALF:
                    re, im = pltpu.roll(re, modes // 2, 1), pltpu.roll(im, modes // 2, 1)
                g_re, g_im = gain_ref[row, 2 * r], gain_ref[row, 2 * r + 1]
                re, im = re * g_re - im * g_im, re * g_im + im * g_re
                base = n * group + 2 * r * levels
                back_ref[base : base + levels, :modes] = re
                back_ref[base : base + levels, modes:] = -im
                back_ref[base + levels : base + 2 * levels, :modes] = im
                back_ref[base + levels : base + 2 * levels, modes:] = re
        stack_ref[...] = product(back_ref[...], high_ref[...], low_ref[...], 1)
        for n in range(count):
            i, j = divmod(n, number)
            keep = keep_ref[rows[j]]
            for tile in range(0, padded, LANES):
                lanes = slice(tile, tile + LANES)
                spectrum = []
                for r in range(HALF + 1):
                    base = n * group + 2 * r * levels
                    re = stack_ref[base : base + levels, lanes]
                    im = stack_ref[base + levels : base + 2 * levels, lanes]
                    if r > 0:
                        c, s = phase_ref[2 * r : 2 * r + 1, lanes], phase_ref[2 * r + 1 : 2 * r + 2, lanes]
                        re, im = re * c - im * s, re * s + im * c
                    spectrum.append((re, im))
                width = min(LANES, piece - tile)
                for u, value in enumerate(half_inverse(spectrum)):
                    pos, start = divmod(u * piece, columns)
                    start += tile
                    shifted = moved_ref[n, pos, :, start : start + LANES]
                    result = keep * shifted + (1.0 - keep) * value
                    pair_ref[pos, n, :, start : start + width] = result[:, :width]
        for n in range(count):
            i, j = divmod(n, number)
            mine_ref[i, j] = pair_ref[core, n, :, :columns]
            send_ref[i, j] = pair_ref[1 - core, n, :, :columns]


def end_kernel(*refs):
    *refs, out_hbm, out_ref, sems = refs
    tracer_count, levels, row_count, columns = out_ref.shape
    share = tracer_count // PAIR
    core = lax.rem(lax.axis_index("lon"), PAIR)
    north = near_is_north()
    copies = []
    for place, (inner, near, far) in enumerate([refs[:3], refs[3:]]):
        for i in range(share):
            slot = place * share + i
            for lanes in spans(columns, 4 * LANES):
                a, b = near[i, 0, :, lanes], far[i, 0, :, lanes]
                out_ref[slot, :, 0, lanes] = jnp.where(north, b, a)
                out_ref[slot, :, row_count - 1, lanes] = jnp.where(north, a, b)
                for j in range(1, row_count - 1):
                    out_ref[slot, :, j, lanes] = inner[i, j - 1, :, lanes]
            t = lax.rem(core + place, PAIR) * share + i
            copies.append(pltpu.make_async_copy(out_ref.at[slot], out_hbm.at[t], sems.at[slot]))
            copies[-1].start()
    for copy in copies:
        copy.wait()


def filter_tables(lon_cells):
    piece = lon_cells // RADIX
    padded = -(-piece // LANES) * LANES
    modes = 2 * MODES // RADIX
    q = np.arange(modes) - modes // 2
    angle = 2 * np.pi * (np.arange(piece)[:, None] * q[None, :] % piece) / piece
    table = np.zeros((padded, 2 * modes))
    table[:piece, :modes] = np.cos(angle)
    table[:piece, modes:] = np.sin(angle)
    high = table.astype(jnp.bfloat16)
    low = (table - high.astype(np.float64)).astype(jnp.bfloat16)
    r = np.arange(HALF + 1)[:, None]

    def waves(steps):
        angle = 2 * np.pi * steps / lon_cells
        pairs = np.stack([np.cos(angle), np.sin(angle)], axis=1)
        return pairs.reshape(-1, steps.shape[1]).astype(np.float32)

    phase = waves(r * np.arange(padded)[None, :])
    wave = waves(RADIX * q[None, :] + r)
    return phase, wave, high, low


SMALL, WHOLE, UNREAD = pltpu.SMEM, pltpu.VMEM, pl.ANY


def call(kernel, outs, operands, scratch=(), sems=0, place=None):
    return pl.pallas_call(
        kernel,
        out_shape=[jax.ShapeDtypeStruct(shape, jnp.float32) for shape in outs],
        in_specs=[pl.BlockSpec(memory_space=place) for _, place in operands],
        out_specs=[pl.BlockSpec(memory_space=place or WHOLE)] * len(outs),
        scratch_shapes=[pltpu.VMEM(shape, jnp.float32) for shape in scratch]
        + ([pltpu.SemaphoreType.DMA((sems,))] if sems else []),
        compiler_params=pltpu.CompilerParams(vmem_limit_bytes=24 << 20),
        cost_estimate=pl.CostEstimate(flops=1, bytes_accessed=1, transcendentals=0),
    )(*[v for v, _ in operands])


def whole(*values):
    return [(v, WHOLE) for v in values]


def body(tracers, merid_courant, zonal_shift, zonal_fraction, cutoff, damping):
    tracer_count, level_count, row_count, column_count = tracers.shape
    lat_count = lax.axis_size("lat")
    lon_count = lax.axis_size("lon")
    assert lon_count == PAIR * PAIR and tracer_count % PAIR == 0 and row_count > 2
    share = tracer_count // PAIR
    lon_cells = column_count * lon_count
    phase, wave, high, low = [jnp.asarray(t) for t in filter_tables(lon_cells)]
    padded, double = high.shape
    width = -(-column_count // LANES) * LANES
    assert column_count - lon_cells // RADIX + padded <= width
    group = level_count * 2 * (HALF + 1)
    shift_rows, fraction_rows = zonal_shift.T, zonal_fraction.T

    def swap_core(value):
        return lax.ppermute(value, "lon", [(p, p ^ 1) for p in range(lon_count)])

    def swap_half(value):
        return lax.ppermute(value, "lon", [(p, p ^ 2) for p in range(lon_count)])

    def swap_band(value, first):
        pairs = []
        for b in range(first, lat_count - 1, 2):
            pairs += [(b, b + 1), (b + 1, b)]
        return lax.ppermute(value, "lat", pairs)

    def set_shape(number):
        return (share, number, level_count, column_count)

    def forward(mine, theirs, after):
        count = mine.shape[0] * mine.shape[1]
        return call(
            forward_kernel,
            [(count, level_count, 2 * MODES + LANES), (PAIR, count, level_count, width)],
            whole(mine, theirs, phase, high, low) + [(after, UNREAD)],
            [(count * group, padded)],
        )

    def shifted(which, held, after):
        count = held.shape[1]
        (moved,) = call(
            functools.partial(shift_kernel, which, column_count),
            [(count, PAIR, level_count, width)],
            whole(distance, fraction, held) + [(after, UNREAD)],
        )
        return moved

    def inverse(which, held, moved, own, other, after):
        count = held.shape[1]
        return call(
            functools.partial(inverse_kernel, which, column_count),
            [set_shape(count // share)] * 2,
            whole(distance, fraction, keep, gain, phase, high, low, held, moved, own, other)
            + [(after, UNREAD)],
            [(count * group, padded), (count * group, double), (PAIR, count, level_count, width)],
        )

    edge_shape = ((tracer_count + 1) * level_count, column_count)
    part_shape = (tracer_count, level_count, column_count)
    inner_mine, inner_send, near_edge, far_edge, near_part, far_part = call(
        begin_kernel,
        [set_shape(row_count - 2)] * 2 + [edge_shape] * 2 + [part_shape] * 2,
        [(tracers, pltpu.HBM), (merid_courant, pltpu.HBM)],
        [tracers.shape, merid_courant.shape],
        tracer_count + 1,
    )
    inner_theirs = swap_core(inner_send)
    near_got = swap_band(near_edge, 0)
    inner_own, inner_held = forward(inner_mine, inner_theirs, near_part)
    inner_other = swap_half(inner_own)
    row_shape = (row_count, level_count, LANES)
    distance, fraction, keep, gain = call(
        functools.partial(row_kernel, column_count),
        [row_shape] * 3 + [(row_count, 2 * (HALF + 1), level_count, double // 2)],
        [(v, SMALL) for v in (shift_rows, fraction_rows, cutoff, damping)]
        + whole(wave)
        + [(inner_own, UNREAD)],
    )
    inner_moved = shifted("inner", inner_held, inner_own)

    near_mine, near_send, far_relay = call(
        functools.partial(edge_kernel, True),
        [set_shape(1)] * 2 + [edge_shape],
        whole(near_edge, near_got, near_part) + [(inner_moved, UNREAD)] + whole(far_edge),
    )
    near_theirs = swap_core(near_send)
    far_got = swap_band(far_relay, 1)
    near_own, near_held = forward(near_mine, near_theirs, inner_moved)
    near_other = swap_half(near_own)
    near_moved = shifted("near", near_held, near_own)
    inner = inverse("inner", inner_held, inner_moved, inner_own, inner_other, near_moved)
    inner_back = swap_core(inner[1])

    far_mine, far_send = call(
        functools.partial(edge_kernel, False),
        [set_shape(1)] * 2,
        whole(far_edge, far_got, far_part) + [(inner[0], UNREAD)],
    )
    far_theirs = swap_core(far_send)
    near = inverse("near", near_held, near_moved, near_own, near_other, far_mine)
    near_back = swap_core(near[1])
    far_own, far_held = forward(far_mine, far_theirs, near[0])
    far_other = swap_half(far_own)
    far_moved = shifted("far", far_held, far_own)
    far = inverse("far", far_held, far_moved, far_own, far_other, far_moved)
    far_back = swap_core(far[1])
    (result,) = call(
        end_kernel,
        [tracers.shape],
        whole(inner[0], near[0], far[0], inner_back, near_back, far_back),
        [tracers.shape],
        tracer_count,
        pltpu.HBM,
    )
    return result


def solution(mesh):
    placed = (
        P(None, None, "lat", "lon"),
        P(None, "lat", "lon"),
        P(None, "lat"),
        P(None, "lat"),
        P(),
        P(),
    )
    return jax.shard_map(
        body, mesh=mesh, in_specs=placed, out_specs=P(None, None, "lat", "lon"), check_vma=False
    )
```

```python
import functools
import math

import jax
import jax.numpy as jnp
import numpy as np
from jax import lax
from jax.experimental import pallas as pl
from jax.experimental.pallas import tpu as pltpu
from jax.sharding import PartitionSpec as P

MODES = 1024
SMAX = 64
RADIX = 16
HALF = RADIX // 2
LANES = 128
PAIR = 2


def times_phase(value, numerator, denominator):
    re, im = value
    eighth = (8 * numerator % (8 * denominator)) / denominator
    if eighth == 0:
        return re, im
    if eighth == 2:
        return -im, re
    if eighth == 4:
        return -re, -im
    if eighth == 6:
        return im, -re
    c = math.cos(2 * math.pi * numerator / denominator)
    s = math.sin(2 * math.pi * numerator / denominator)
    if eighth == 7:
        return (re + im) * c, (im - re) * c
    if eighth == 1:
        return (re - im) * c, (re + im) * c
    return re * c - im * s, re * s + im * c


def real_dft(values):
    n = len(values)
    if n == 2:
        return [(values[0] + values[1], None), (values[0] - values[1], None)]
    even, odd = real_dft(values[0::2]), real_dft(values[1::2])
    out = [None] * (n // 2 + 1)
    for r in range(n // 4 + 1):
        (er, ei), (tr, ti) = even[r], odd[r]
        if r == 0:
            out[0] = (er + tr, None)
            out[n // 2] = (er - tr, None)
        elif r == n // 4:
            out[r] = (er, -tr)
        else:
            tr, ti = times_phase((tr, ti), -r, n)
            out[r] = (er + tr, ei + ti)
            out[n // 2 - r] = (er - tr, ti - ei)
    return out


def real_inverse(spectrum):
    n = 2 * (len(spectrum) - 1)
    if n == 2:
        a, b = spectrum[0][0], spectrum[1][0]
        return [a + b, a - b]
    even, odd = [None] * (n // 4 + 1), [None] * (n // 4 + 1)
    for r in range(n // 4 + 1):
        (ar, ai), (br, bi) = spectrum[r], spectrum[n // 2 - r]
        if r == 0:
            even[0] = (ar + br, None)
            odd[0] = (ar - br, None)
        elif r == n // 4:
            even[r] = (ar + ar, None)
            odd[r] = (-(ai + ai), None)
        else:
            even[r] = (ar + br, ai - bi)
            odd[r] = times_phase((ar - br, ai + bi), r, n)
    out = [None] * n
    out[0::2] = real_inverse(even)
    out[1::2] = real_inverse(odd)
    return out


def four(values, sign):
    (ar, ai), (br, bi), (cr, ci), (dr, di) = values
    pr, pi, mr, mi = ar + cr, ai + ci, ar - cr, ai - ci
    qr, qi, nr, ni = br + dr, bi + di, br - dr, bi - di
    if sign > 0:
        nr, ni = -nr, -ni
    return [(pr + qr, pi + qi), (mr + ni, mi - nr), (pr - qr, pi - qi), (mr - ni, mi + nr)]


def half_dft(x):
    out = [None] * 9
    out[0::2] = real_dft(x)
    odd = four([times_phase((x[v], -x[v + 4]), -v, 16) for v in range(4)], -1)
    out[1], out[5] = odd[0], odd[1]
    out[7] = (odd[2][0], -odd[2][1])
    out[3] = (odd[3][0], -odd[3][1])
    return out


def half_inverse(w):
    even = real_inverse(w[0::2])
    odd = four([w[1], w[5], (w[7][0], -w[7][1]), (w[3][0], -w[3][1])], 1)
    odd = [times_phase(value, v, 16) for v, value in enumerate(odd)]
    return [even[v] + odd[v][0] for v in range(4)] + [even[v + 4] - odd[v][1] for v in range(4)]


def split(value):
    high = value.astype(jnp.bfloat16)
    return high, (value - high.astype(jnp.float32)).astype(jnp.bfloat16)


def product(left, table_high, table_low, side):
    high, low = split(left)

    def dot(x, y):
        return lax.dot_general(x, y, (((1,), (side,)), ((), ())), preferred_element_type=jnp.float32)

    return dot(high, table_high) + (dot(high, table_low) + dot(low, table_high))


def spans(columns, width):
    return [slice(start, min(start + width, columns)) for start in range(0, columns, width)]


def is_cap(lat):
    count = lax.axis_size("lat")
    return (lat < count // 4) | (lat >= count - count // 4)


def flux_of(face_speed, south, north):
    return jnp.maximum(face_speed, 0.0) * south + jnp.minimum(face_speed, 0.0) * north


def near_is_north():
    return lax.rem(lax.axis_index("lat"), 2) == 0


def begin_kernel(
    cells_ref, speed_ref, mine_ref, send_ref, near_ref, far_ref, near_part_ref, far_part_ref
):
    tracer_count, levels, row_count, columns = cells_ref.shape
    share = tracer_count // PAIR
    core = lax.rem(lax.axis_index("lon"), PAIR)
    north = near_is_north()
    for lanes in spans(columns, 2 * LANES):
        speed = [speed_ref[:, j, lanes] for j in range(row_count)]
        near_ref[tracer_count * levels :, lanes] = speed[0]
        far_ref[tracer_count * levels :, lanes] = speed[0]
        for which, out_ref in enumerate([mine_ref, send_ref]):
            for i in range(share):
                t = lax.rem(core + which, PAIR) * share + i
                place = pl.ds(pl.multiple_of(t * levels, levels), levels)
                x = [cells_ref[t, :, j, lanes] for j in range(row_count)]
                flux = [flux_of(speed[j], x[j - 1], x[j]) for j in range(1, row_count)]
                for j in range(1, row_count - 1):
                    out_ref[i, j - 1, :, lanes] = x[j] + flux[j - 1] - flux[j]
                near_ref[place, lanes] = jnp.where(north, x[-1], x[0])
                far_ref[place, lanes] = jnp.where(north, x[0], x[-1])
                south_part, north_part = x[0] - flux[0], x[-1] + flux[-1]
                near_part_ref[t, :, lanes] = jnp.where(north, north_part, south_part)
                far_part_ref[t, :, lanes] = jnp.where(north, south_part, north_part)


def edge_kernel(is_near, own_ref, got_ref, part_ref, after_ref, mine_ref, send_ref):
    tracer_count, levels, columns = part_ref.shape
    share = tracer_count // PAIR
    total = tracer_count * levels
    core = lax.rem(lax.axis_index("lon"), PAIR)
    lat = lax.axis_index("lat")
    north = near_is_north() if is_near else jnp.logical_not(near_is_north())
    wall = jnp.where(north, lat == lax.axis_size("lat") - 1, lat == 0)
    for lanes in spans(columns, 3 * LANES):
        speed = jnp.where(north, got_ref[total:, lanes], own_ref[total:, lanes])
        speed = jnp.where(wall, 0.0, speed)
        for which, out_ref in enumerate([mine_ref, send_ref]):
            for i in range(share):
                t = lax.rem(core + which, PAIR) * share + i
                place = pl.ds(pl.multiple_of(t * levels, levels), levels)
                own, got = own_ref[place, lanes], got_ref[place, lanes]
                flux = flux_of(speed, jnp.where(north, own, got), jnp.where(north, got, own))
                out_ref[i, 0, :, lanes] = part_ref[t, :, lanes] + jnp.where(north, -flux, flux)


def forward_kernel(
    mine_ref, theirs_ref, phase_ref, high_ref, low_ref, after_ref, message_ref, held_ref, stack_ref
):
    share, number, levels, columns = mine_ref.shape
    piece = columns * PAIR // HALF
    padded = stack_ref.shape[1]
    modes = high_ref.shape[1] // 2
    group = levels * 2 * (HALF + 1)
    core = lax.rem(lax.axis_index("lon"), PAIR)
    count = share * number
    for n in range(count):
        i, j = divmod(n, number)
        held_ref[core, n, :, :columns] = mine_ref[i, j]
        held_ref[1 - core, n, :, :columns] = theirs_ref[i, j]
        for pos in range(PAIR):
            held_ref[pos, n, :, columns:] = jnp.zeros((levels, held_ref.shape[3] - columns), jnp.float32)
        message_ref[n, :, 2 * MODES :] = held_ref[PAIR - 1, n, :, columns - LANES : columns]

    @pl.when(is_cap(lax.axis_index("lat")))
    def _():
        for n in range(count):
            for tile in range(0, padded, LANES):
                lanes = slice(tile, tile + LANES)
                x = []
                for u in range(HALF):
                    pos, start = divmod(u * piece, columns)
                    x.append(held_ref[pos, n, :, start + tile : start + tile + LANES])
                for r, (re, im) in enumerate(half_dft(x)):
                    base = n * group + 2 * r * levels
                    if r == 0:
                        im = jnp.zeros_like(re)
                    else:
                        c, s = phase_ref[2 * r : 2 * r + 1, lanes], phase_ref[2 * r + 1 : 2 * r + 2, lanes]
                        if im is None:
                            re, im = re * c, -(re * s)
                        else:
                            re, im = re * c + im * s, im * c - re * s
                    stack_ref[base : base + levels, lanes] = re
                    stack_ref[base + levels : base + 2 * levels, lanes] = im
        coeffs = product(stack_ref[...], high_ref[...], low_ref[...], 0)
        upper = lax.broadcasted_iota(jnp.int32, (levels, modes), 1) >= modes // 2
        for n in range(count):
            first = None
            for r in [0, HALF] + list(range(1, HALF)):
                base = n * group + 2 * r * levels
                re, im = coeffs[base : base + levels], coeffs[base + levels : base + 2 * levels]
                x_re = re[:, :modes] + im[:, modes:]
                x_im = im[:, :modes] - re[:, modes:]
                if r == 0:
                    first = x_re, x_im
                    continue
                slot = r
                if r == HALF:
                    x_re = jnp.where(upper, first[0], pltpu.roll(x_re, modes // 2, 1))
                    x_im = jnp.where(upper, first[1], pltpu.roll(x_im, modes // 2, 1))
                    slot = 0
                message_ref[n, :, 2 * slot * modes : (2 * slot + 1) * modes] = x_re
                message_ref[n, :, (2 * slot + 1) * modes : (2 * slot + 2) * modes] = x_im


def row_vector(ref, row, levels):
    level = lax.broadcasted_iota(jnp.int32, (levels, LANES), 0)
    out = jnp.full((levels, LANES), ref[row, 0])
    for i in range(1, levels):
        out = jnp.where(level == i, ref[row, i], out)
    return out


def displaced(tiles, distance, share):
    lane = lax.broadcasted_iota(jnp.int32, distance.shape, 1)

    def moved(steps):
        index = (lane - steps) & (LANES - 1)
        turned = [jnp.take_along_axis(v, index, axis=1, mode="promise_in_bounds") for v in tiles]
        from_left = lane < steps
        return [jnp.where(from_left, a, b) for a, b in zip(turned, turned[1:])]

    pairs = zip(moved(distance), moved(distance + 1))
    return [(1.0 - share) * here + share * earlier for here, earlier in pairs]


def rows_of(which, row_count):
    if which == "inner":
        return list(range(1, row_count - 1))
    north = near_is_north() if which == "near" else jnp.logical_not(near_is_north())
    return [jnp.where(north, row_count - 1, 0)]


def wave_angle(steps, lon_cells):
    steps = lax.rem(steps, lon_cells)
    return steps.astype(jnp.float32) * (2.0 * math.pi / lon_cells)


def row_kernel(
    columns, shift_ref, fraction_ref, cutoff_ref, damping_ref, wave_ref, after_ref,
    distance_ref, share_ref, keep_ref, gain_ref,
):
    row_count, levels = shift_ref.shape
    lon_cells = columns * PAIR * PAIR
    modes = gain_ref.shape[3]
    lat = lax.axis_index("lat")
    for row in range(row_count):
        distance_ref[row] = row_vector(shift_ref, row, levels).astype(jnp.float32)
        share_ref[row] = row_vector(fraction_ref, row, levels)
        keep_ref[row] = jnp.full((levels, LANES), damping_ref[lat * row_count + row])

    @pl.when(is_cap(lat))
    def _():
        lane = lax.broadcasted_iota(jnp.int32, (levels, modes), 1)
        mode = lane - modes // 2
        for row in range(row_count):
            distance = distance_ref[row].astype(jnp.int32)
            share = share_ref[row]
            limit = cutoff_ref[lat * row_count + row]
            wide = wave_angle(RADIX * mode * distance, lon_cells)
            wide_re, wide_im = jnp.cos(wide), -jnp.sin(wide)
            fine = wave_angle(lane * distance, lon_cells)
            fine_re, fine_im = jnp.cos(fine), -jnp.sin(fine)
            for r in range(HALF + 1):
                wavenumber = RADIX * mode + r
                kept = jnp.abs(wavenumber) <= limit
                if r in (0, HALF):
                    kept = kept & (wavenumber >= 0)
                once = r % 2 == 0 and r not in (0, HALF)
                weight = jnp.full((levels, modes), (1.0 if once else 2.0) / lon_cells)
                if r == 0:
                    weight = jnp.where(wavenumber == 0, 1.0 / lon_cells, weight)
                weight = jnp.where(kept, weight, 0.0)
                mix_re = (1.0 - share) + share * wave_ref[2 * r : 2 * r + 1]
                mix_im = -share * wave_ref[2 * r + 1 : 2 * r + 2]
                turn_re, turn_im = fine_re[:, r : r + 1], fine_im[:, r : r + 1]
                re, im = wide_re * turn_re - wide_im * turn_im, wide_re * turn_im + wide_im * turn_re
                gain_ref[row, 2 * r] = (re * mix_re - im * mix_im) * weight
                gain_ref[row, 2 * r + 1] = (re * mix_im + im * mix_re) * weight


def shift_kernel(which, columns, distance_ref, share_ref, held_ref, after_ref, *refs):
    if which == "inner":
        source_ref, moved_ref, relay_ref = refs
        relay_ref[...] = source_ref[...]
    else:
        (moved_ref,) = refs
    _, count, levels, padded = held_ref.shape
    rows = rows_of(which, share_ref.shape[0])
    number = len(rows)
    for j, row in enumerate(rows):
        distance, share = distance_ref[row].astype(jnp.int32), share_ref[row]
        for n in range(j, count, number):
            for pos in range(PAIR):
                tiles = [held_ref[PAIR - 1 - pos, n, :, columns - LANES : columns]]
                tiles += [held_ref[pos, n, :, lanes] for lanes in spans(padded, LANES)]
                for lanes, tile in zip(spans(padded, LANES), displaced(tiles, distance, share)):
                    moved_ref[n, pos, :, lanes] = tile


def inverse_kernel(
    which, columns, distance_ref, share_ref, keep_ref, gain_ref, phase_ref, high_ref, low_ref,
    held_ref, moved_ref, own_ref, other_ref, after_ref, mine_ref, send_ref,
    stack_ref, back_ref, pair_ref,
):
    _, count, levels, _ = held_ref.shape
    rows = rows_of(which, share_ref.shape[0])
    number = len(rows)
    piece = columns * PAIR // HALF
    padded = stack_ref.shape[1]
    modes = gain_ref.shape[3]
    group = levels * 2 * (HALF + 1)
    core = lax.rem(lax.axis_index("lon"), PAIR)
    cap = is_cap(lax.axis_index("lat"))
    for j, row in enumerate(rows):
        distance, share = distance_ref[row].astype(jnp.int32), share_ref[row]
        for n in range(j, count, number):
            tiles = [other_ref[n, :, 2 * MODES :], held_ref[0, n, :, :LANES]]
            (moved_ref[n, 0, :, :LANES],) = displaced(tiles, distance, share)

    @pl.when(jnp.logical_not(cap))
    def _():
        for n in range(count):
            i, j = divmod(n, number)
            mine_ref[i, j] = moved_ref[n, core, :, :columns]
            send_ref[i, j] = moved_ref[n, 1 - core, :, :columns]

    @pl.when(cap)
    def _():
        for n in range(count):
            row = rows[n % number]
            for r in range(HALF + 1):
                slot = r % HALF
                ours, theirs = (
                    [ref[n, :, (2 * slot + part) * modes : (2 * slot + part + 1) * modes] for part in range(2)]
                    for ref in (own_ref, other_ref)
                )
                if r % 2:
                    re, im = ours[0] - theirs[0], ours[1] - theirs[1]
                else:
                    re, im = ours[0] + theirs[0], ours[1] + theirs[1]
                if r == HALF:
                    re, im = pltpu.roll(re, modes // 2, 1), pltpu.roll(im, modes // 2, 1)
                g_re, g_im = gain_ref[row, 2 * r], gain_ref[row, 2 * r + 1]
                re, im = re * g_re - im * g_im, re * g_im + im * g_re
                base = n * group + 2 * r * levels
                back_ref[base : base + levels, :modes] = re
                back_ref[base : base + levels, modes:] = -im
                back_ref[base + levels : base + 2 * levels, :modes] = im
                back_ref[base + levels : base + 2 * levels, modes:] = re
        stack_ref[...] = product(back_ref[...], high_ref[...], low_ref[...], 1)
        for n in range(count):
            i, j = divmod(n, number)
            keep = keep_ref[rows[j]]
            for tile in range(0, padded, LANES):
                lanes = slice(tile, tile + LANES)
                spectrum = []
                for r in range(HALF + 1):
                    base = n * group + 2 * r * levels
                    re = stack_ref[base : base + levels, lanes]
                    im = stack_ref[base + levels : base + 2 * levels, lanes]
                    if r > 0:
                        c, s = phase_ref[2 * r : 2 * r + 1, lanes], phase_ref[2 * r + 1 : 2 * r + 2, lanes]
                        re, im = re * c - im * s, re * s + im * c
                    spectrum.append((re, im))
                width = min(LANES, piece - tile)
                for u, value in enumerate(half_inverse(spectrum)):
                    pos, start = divmod(u * piece, columns)
                    start += tile
                    shifted = moved_ref[n, pos, :, start : start + LANES]
                    result = keep * shifted + (1.0 - keep) * value
                    pair_ref[pos, n, :, start : start + width] = result[:, :width]
        for n in range(count):
            i, j = divmod(n, number)
            mine_ref[i, j] = pair_ref[core, n, :, :columns]
            send_ref[i, j] = pair_ref[1 - core, n, :, :columns]


def end_kernel(*refs):
    *refs, out_hbm, out_ref, sems = refs
    tracer_count, levels, row_count, columns = out_ref.shape
    share = tracer_count // PAIR
    core = lax.rem(lax.axis_index("lon"), PAIR)
    north = near_is_north()
    copies = []
    for place, (inner, near, far) in enumerate([refs[:3], refs[3:]]):
        for i in range(share):
            slot = place * share + i
            for lanes in spans(columns, 4 * LANES):
                a, b = near[i, 0, :, lanes], far[i, 0, :, lanes]
                out_ref[slot, :, 0, lanes] = jnp.where(north, b, a)
                out_ref[slot, :, row_count - 1, lanes] = jnp.where(north, a, b)
                for j in range(1, row_count - 1):
                    out_ref[slot, :, j, lanes] = inner[i, j - 1, :, lanes]
            t = lax.rem(core + place, PAIR) * share + i
            copies.append(pltpu.make_async_copy(out_ref.at[slot], out_hbm.at[t], sems.at[slot]))
            copies[-1].start()
    for copy in copies:
        copy.wait()


def filter_tables(lon_cells):
    piece = lon_cells // RADIX
    padded = -(-piece // LANES) * LANES
    modes = 2 * MODES // RADIX
    q = np.arange(modes) - modes // 2
    angle = 2 * np.pi * (np.arange(piece)[:, None] * q[None, :] % piece) / piece
    table = np.zeros((padded, 2 * modes))
    table[:piece, :modes] = np.cos(angle)
    table[:piece, modes:] = np.sin(angle)
    high = table.astype(jnp.bfloat16)
    low = (table - high.astype(np.float64)).astype(jnp.bfloat16)
    r = np.arange(HALF + 1)[:, None]

    def waves(steps):
        angle = 2 * np.pi * steps / lon_cells
        pairs = np.stack([np.cos(angle), np.sin(angle)], axis=1)
        return pairs.reshape(-1, steps.shape[1]).astype(np.float32)

    phase = waves(r * np.arange(padded)[None, :])
    wave = waves(RADIX * q[None, :] + r)
    return phase, wave, high, low


SMALL, WHOLE, UNREAD = pltpu.SMEM, pltpu.VMEM, pl.ANY


def call(kernel, outs, operands, scratch=(), sems=0, place=None):
    return pl.pallas_call(
        kernel,
        out_shape=[jax.ShapeDtypeStruct(shape, jnp.float32) for shape in outs],
        in_specs=[pl.BlockSpec(memory_space=place) for _, place in operands],
        out_specs=[pl.BlockSpec(memory_space=place or WHOLE)] * len(outs),
        scratch_shapes=[pltpu.VMEM(shape, jnp.float32) for shape in scratch]
        + ([pltpu.SemaphoreType.DMA((sems,))] if sems else []),
        compiler_params=pltpu.CompilerParams(vmem_limit_bytes=24 << 20),
        cost_estimate=pl.CostEstimate(flops=1, bytes_accessed=1, transcendentals=0),
    )(*[v for v, _ in operands])


def whole(*values):
    return [(v, WHOLE) for v in values]


def body(tracers, merid_courant, zonal_shift, zonal_fraction, cutoff, damping):
    tracer_count, level_count, row_count, column_count = tracers.shape
    lat_count = lax.axis_size("lat")
    lon_count = lax.axis_size("lon")
    assert lon_count == PAIR * PAIR and tracer_count % PAIR == 0 and row_count > 2
    share = tracer_count // PAIR
    lon_cells = column_count * lon_count
    phase, wave, high, low = [jnp.asarray(t) for t in filter_tables(lon_cells)]
    padded, double = high.shape
    width = -(-column_count // LANES) * LANES
    assert column_count - lon_cells // RADIX + padded <= width
    group = level_count * 2 * (HALF + 1)
    shift_rows, fraction_rows = zonal_shift.T, zonal_fraction.T

    def swap_core(value):
        return lax.ppermute(value, "lon", [(p, p ^ 1) for p in range(lon_count)])

    def swap_half(value):
        return lax.ppermute(value, "lon", [(p, p ^ 2) for p in range(lon_count)])

    def swap_band(value, first):
        pairs = []
        for b in range(first, lat_count - 1, 2):
            pairs += [(b, b + 1), (b + 1, b)]
        return lax.ppermute(value, "lat", pairs)

    def set_shape(number):
        return (share, number, level_count, column_count)

    def forward(mine, theirs, after):
        count = mine.shape[0] * mine.shape[1]
        return call(
            forward_kernel,
            [(count, level_count, 2 * MODES + LANES), (PAIR, count, level_count, width)],
            whole(mine, theirs, phase, high, low) + [(after, UNREAD)],
            [(count * group, padded)],
        )

    def shifted(which, held, after, *relay):
        count = held.shape[1]
        return call(
            functools.partial(shift_kernel, which, column_count),
            [(count, PAIR, level_count, width)] + [v.shape for v in relay],
            whole(distance, fraction, held) + [(after, UNREAD)] + whole(*relay),
        )

    def inverse(which, held, moved, own, other, after):
        count = held.shape[1]
        return call(
            functools.partial(inverse_kernel, which, column_count),
            [set_shape(count // share)] * 2,
            whole(distance, fraction, keep, gain, phase, high, low, held, moved, own, other)
            + [(after, UNREAD)],
            [(count * group, padded), (count * group, double), (PAIR, count, level_count, width)],
        )

    edge_shape = ((tracer_count + 1) * level_count, column_count)
    part_shape = (tracer_count, level_count, column_count)
    inner_mine, inner_send, near_edge, far_edge, near_part, far_part = call(
        begin_kernel,
        [set_shape(row_count - 2)] * 2 + [edge_shape] * 2 + [part_shape] * 2,
        whole(tracers, merid_courant),
    )
    inner_theirs = swap_core(inner_send)
    near_got = swap_band(near_edge, 0)
    inner_own, inner_held = forward(inner_mine, inner_theirs, near_part)
    inner_other = swap_half(inner_own)
    row_shape = (row_count, level_count, LANES)
    distance, fraction, keep, gain = call(
        functools.partial(row_kernel, column_count),
        [row_shape] * 3 + [(row_count, 2 * (HALF + 1), level_count, double // 2)],
        [(v, SMALL) for v in (shift_rows, fraction_rows, cutoff, damping)]
        + whole(wave)
        + [(inner_own, UNREAD)],
    )
    inner_moved, far_relay = shifted("inner", inner_held, inner_own, far_edge)
    far_got = swap_band(far_relay, 1)

    near_mine, near_send = call(
        functools.partial(edge_kernel, True),
        [set_shape(1)] * 2,
        whole(near_edge, near_got, near_part) + [(inner_moved, UNREAD)],
    )
    near_theirs = swap_core(near_send)
    near_own, near_held = forward(near_mine, near_theirs, inner_moved)
    near_other = swap_half(near_own)
    (near_moved,) = shifted("near", near_held, near_own)
    inner = inverse("inner", inner_held, inner_moved, inner_own, inner_other, near_moved)
    inner_back = swap_core(inner[1])

    far_mine, far_send = call(
        functools.partial(edge_kernel, False),
        [set_shape(1)] * 2,
        whole(far_edge, far_got, far_part) + [(inner[0], UNREAD)],
    )
    far_theirs = swap_core(far_send)
    far_own, far_held = forward(far_mine, far_theirs, inner[0])
    far_other = swap_half(far_own)
    (far_moved,) = shifted("far", far_held, far_own)
    near = inverse("near", near_held, near_moved, near_own, near_other, far_moved)
    near_back = swap_core(near[1])
    far = inverse("far", far_held, far_moved, far_own, far_other, near[0])
    far_back = swap_core(far[1])
    (result,) = call(
        end_kernel,
        [tracers.shape],
        whole(inner[0], near[0], far[0], inner_back, near_back, far_back),
        [tracers.shape],
        tracer_count,
        pltpu.HBM,
    )
    return result


def solution(mesh):
    placed = (
        P(None, None, "lat", "lon"),
        P(None, "lat", "lon"),
        P(None, "lat"),
        P(None, "lat"),
        P(),
        P(),
    )
    return jax.shard_map(
        body, mesh=mesh, in_specs=placed, out_specs=P(None, None, "lat", "lon"), check_vma=False
    )
```

```python
import functools
import math

import jax
import jax.numpy as jnp
import numpy as np
from jax import lax
from jax.experimental import pallas as pl
from jax.experimental.pallas import tpu as pltpu
from jax.sharding import PartitionSpec as P

MODES = 1024
SMAX = 64
RADIX = 16
HALF = RADIX // 2
LANES = 128
PAIR = 2


def times_phase(value, numerator, denominator):
    re, im = value
    eighth = (8 * numerator % (8 * denominator)) / denominator
    if eighth == 0:
        return re, im
    if eighth == 2:
        return -im, re
    if eighth == 4:
        return -re, -im
    if eighth == 6:
        return im, -re
    c = math.cos(2 * math.pi * numerator / denominator)
    s = math.sin(2 * math.pi * numerator / denominator)
    if eighth == 7:
        return (re + im) * c, (im - re) * c
    if eighth == 1:
        return (re - im) * c, (re + im) * c
    return re * c - im * s, re * s + im * c


def real_dft(values):
    n = len(values)
    if n == 2:
        return [(values[0] + values[1], None), (values[0] - values[1], None)]
    even, odd = real_dft(values[0::2]), real_dft(values[1::2])
    out = [None] * (n // 2 + 1)
    for r in range(n // 4 + 1):
        (er, ei), (tr, ti) = even[r], odd[r]
        if r == 0:
            out[0] = (er + tr, None)
            out[n // 2] = (er - tr, None)
        elif r == n // 4:
            out[r] = (er, -tr)
        else:
            tr, ti = times_phase((tr, ti), -r, n)
            out[r] = (er + tr, ei + ti)
            out[n // 2 - r] = (er - tr, ti - ei)
    return out


def real_inverse(spectrum):
    n = 2 * (len(spectrum) - 1)
    if n == 2:
        a, b = spectrum[0][0], spectrum[1][0]
        return [a + b, a - b]
    even, odd = [None] * (n // 4 + 1), [None] * (n // 4 + 1)
    for r in range(n // 4 + 1):
        (ar, ai), (br, bi) = spectrum[r], spectrum[n // 2 - r]
        if r == 0:
            even[0] = (ar + br, None)
            odd[0] = (ar - br, None)
        elif r == n // 4:
            even[r] = (ar + ar, None)
            odd[r] = (-(ai + ai), None)
        else:
            even[r] = (ar + br, ai - bi)
            odd[r] = times_phase((ar - br, ai + bi), r, n)
    out = [None] * n
    out[0::2] = real_inverse(even)
    out[1::2] = real_inverse(odd)
    return out


def four(values, sign):
    (ar, ai), (br, bi), (cr, ci), (dr, di) = values
    pr, pi, mr, mi = ar + cr, ai + ci, ar - cr, ai - ci
    qr, qi, nr, ni = br + dr, bi + di, br - dr, bi - di
    if sign > 0:
        nr, ni = -nr, -ni
    return [(pr + qr, pi + qi), (mr + ni, mi - nr), (pr - qr, pi - qi), (mr - ni, mi + nr)]


def half_dft(x):
    out = [None] * 9
    out[0::2] = real_dft(x)
    odd = four([times_phase((x[v], -x[v + 4]), -v, 16) for v in range(4)], -1)
    out[1], out[5] = odd[0], odd[1]
    out[7] = (odd[2][0], -odd[2][1])
    out[3] = (odd[3][0], -odd[3][1])
    return out


def half_inverse(w):
    even = real_inverse(w[0::2])
    odd = four([w[1], w[5], (w[7][0], -w[7][1]), (w[3][0], -w[3][1])], 1)
    odd = [times_phase(value, v, 16) for v, value in enumerate(odd)]
    return [even[v] + odd[v][0] for v in range(4)] + [even[v + 4] - odd[v][1] for v in range(4)]


def split(value):
    high = value.astype(jnp.bfloat16)
    return high, (value - high.astype(jnp.float32)).astype(jnp.bfloat16)


def product(left, table_high, table_low, side):
    high, low = split(left)

    def dot(x, y):
        return lax.dot_general(x, y, (((1,), (side,)), ((), ())), preferred_element_type=jnp.float32)

    return dot(high, table_high) + (dot(high, table_low) + dot(low, table_high))


def spans(columns, width):
    return [slice(start, min(start + width, columns)) for start in range(0, columns, width)]


def is_cap(lat):
    count = lax.axis_size("lat")
    return (lat < count // 4) | (lat >= count - count // 4)


def flux_of(face_speed, south, north):
    return jnp.maximum(face_speed, 0.0) * south + jnp.minimum(face_speed, 0.0) * north


def near_is_north():
    return lax.rem(lax.axis_index("lat"), 2) == 0


def begin_kernel(
    cells_ref, speed_ref, mine_ref, send_ref, near_ref, far_ref, near_part_ref, far_part_ref
):
    tracer_count, levels, row_count, columns = cells_ref.shape
    share = tracer_count // PAIR
    core = lax.rem(lax.axis_index("lon"), PAIR)
    north = near_is_north()
    for lanes in spans(columns, 2 * LANES):
        speed = [speed_ref[:, j, lanes] for j in range(row_count)]
        near_ref[tracer_count * levels :, lanes] = speed[0]
        far_ref[tracer_count * levels :, lanes] = speed[0]
        for which, out_ref in enumerate([mine_ref, send_ref]):
            for i in range(share):
                t = lax.rem(core + which, PAIR) * share + i
                place = pl.ds(pl.multiple_of(t * levels, levels), levels)
                x = [cells_ref[t, :, j, lanes] for j in range(row_count)]
                flux = [flux_of(speed[j], x[j - 1], x[j]) for j in range(1, row_count)]
                for j in range(1, row_count - 1):
                    out_ref[i, j - 1, :, lanes] = x[j] + flux[j - 1] - flux[j]
                near_ref[place, lanes] = jnp.where(north, x[-1], x[0])
                far_ref[place, lanes] = jnp.where(north, x[0], x[-1])
                south_part, north_part = x[0] - flux[0], x[-1] + flux[-1]
                near_part_ref[t, :, lanes] = jnp.where(north, north_part, south_part)
                far_part_ref[t, :, lanes] = jnp.where(north, south_part, north_part)


def edge_kernel(is_near, own_ref, got_ref, part_ref, after_ref, mine_ref, send_ref):
    tracer_count, levels, columns = part_ref.shape
    share = tracer_count // PAIR
    total = tracer_count * levels
    core = lax.rem(lax.axis_index("lon"), PAIR)
    lat = lax.axis_index("lat")
    north = near_is_north() if is_near else jnp.logical_not(near_is_north())
    wall = jnp.where(north, lat == lax.axis_size("lat") - 1, lat == 0)
    for lanes in spans(columns, 3 * LANES):
        speed = jnp.where(north, got_ref[total:, lanes], own_ref[total:, lanes])
        speed = jnp.where(wall, 0.0, speed)
        for which, out_ref in enumerate([mine_ref, send_ref]):
            for i in range(share):
                t = lax.rem(core + which, PAIR) * share + i
                place = pl.ds(pl.multiple_of(t * levels, levels), levels)
                own, got = own_ref[place, lanes], got_ref[place, lanes]
                flux = flux_of(speed, jnp.where(north, own, got), jnp.where(north, got, own))
                out_ref[i, 0, :, lanes] = part_ref[t, :, lanes] + jnp.where(north, -flux, flux)


def forward_kernel(
    mine_ref, theirs_ref, phase_ref, high_ref, low_ref, after_ref, message_ref, held_ref, stack_ref
):
    share, number, levels, columns = mine_ref.shape
    piece = columns * PAIR // HALF
    padded = stack_ref.shape[1]
    modes = high_ref.shape[1] // 2
    group = levels * 2 * (HALF + 1)
    core = lax.rem(lax.axis_index("lon"), PAIR)
    count = share * number
    for n in range(count):
        i, j = divmod(n, number)
        held_ref[core, n, :, :columns] = mine_ref[i, j]
        held_ref[1 - core, n, :, :columns] = theirs_ref[i, j]
        for pos in range(PAIR):
            held_ref[pos, n, :, columns:] = jnp.zeros((levels, held_ref.shape[3] - columns), jnp.float32)
        message_ref[n, :, 2 * MODES :] = held_ref[PAIR - 1, n, :, columns - LANES : columns]

    @pl.when(is_cap(lax.axis_index("lat")))
    def _():
        for n in range(count):
            for tile in range(0, padded, LANES):
                lanes = slice(tile, tile + LANES)
                x = []
                for u in range(HALF):
                    pos, start = divmod(u * piece, columns)
                    x.append(held_ref[pos, n, :, start + tile : start + tile + LANES])
                for r, (re, im) in enumerate(half_dft(x)):
                    base = n * group + 2 * r * levels
                    if r == 0:
                        im = jnp.zeros_like(re)
                    else:
                        c, s = phase_ref[2 * r : 2 * r + 1, lanes], phase_ref[2 * r + 1 : 2 * r + 2, lanes]
                        if im is None:
                            re, im = re * c, -(re * s)
                        else:
                            re, im = re * c + im * s, im * c - re * s
                    stack_ref[base : base + levels, lanes] = re
                    stack_ref[base + levels : base + 2 * levels, lanes] = im
        coeffs = product(stack_ref[...], high_ref[...], low_ref[...], 0)
        upper = lax.broadcasted_iota(jnp.int32, (levels, modes), 1) >= modes // 2
        for n in range(count):
            first = None
            for r in [0, HALF] + list(range(1, HALF)):
                base = n * group + 2 * r * levels
                re, im = coeffs[base : base + levels], coeffs[base + levels : base + 2 * levels]
                x_re = re[:, :modes] + im[:, modes:]
                x_im = im[:, :modes] - re[:, modes:]
                if r == 0:
                    first = x_re, x_im
                    continue
                slot = r
                if r == HALF:
                    x_re = jnp.where(upper, first[0], pltpu.roll(x_re, modes // 2, 1))
                    x_im = jnp.where(upper, first[1], pltpu.roll(x_im, modes // 2, 1))
                    slot = 0
                message_ref[n, :, 2 * slot * modes : (2 * slot + 1) * modes] = x_re
                message_ref[n, :, (2 * slot + 1) * modes : (2 * slot + 2) * modes] = x_im


def row_vector(ref, row, levels):
    level = lax.broadcasted_iota(jnp.int32, (levels, LANES), 0)
    out = jnp.full((levels, LANES), ref[row, 0])
    for i in range(1, levels):
        out = jnp.where(level == i, ref[row, i], out)
    return out


def displaced(tiles, distance, share):
    lane = lax.broadcasted_iota(jnp.int32, distance.shape, 1)

    def moved(steps):
        index = (lane - steps) & (LANES - 1)
        turned = [jnp.take_along_axis(v, index, axis=1, mode="promise_in_bounds") for v in tiles]
        from_left = lane < steps
        return [jnp.where(from_left, a, b) for a, b in zip(turned, turned[1:])]

    pairs = zip(moved(distance), moved(distance + 1))
    return [(1.0 - share) * here + share * earlier for here, earlier in pairs]


def rows_of(which, row_count):
    if which == "inner":
        return list(range(1, row_count - 1))
    north = near_is_north() if which == "near" else jnp.logical_not(near_is_north())
    return [jnp.where(north, row_count - 1, 0)]


def wave_angle(steps, lon_cells):
    steps = lax.rem(steps, lon_cells)
    return steps.astype(jnp.float32) * (2.0 * math.pi / lon_cells)


def row_kernel(
    columns, shift_ref, fraction_ref, cutoff_ref, damping_ref, wave_ref, after_ref,
    distance_ref, share_ref, keep_ref, gain_ref,
):
    row_count, levels = shift_ref.shape
    lon_cells = columns * PAIR * PAIR
    modes = gain_ref.shape[3]
    lat = lax.axis_index("lat")
    for row in range(row_count):
        distance_ref[row] = row_vector(shift_ref, row, levels).astype(jnp.float32)
        share_ref[row] = row_vector(fraction_ref, row, levels)
        keep_ref[row] = jnp.full((levels, LANES), damping_ref[lat * row_count + row])

    @pl.when(is_cap(lat))
    def _():
        lane = lax.broadcasted_iota(jnp.int32, (levels, modes), 1)
        mode = lane - modes // 2
        for row in range(row_count):
            distance = distance_ref[row].astype(jnp.int32)
            share = share_ref[row]
            limit = cutoff_ref[lat * row_count + row]
            wide = wave_angle(RADIX * mode * distance, lon_cells)
            wide_re, wide_im = jnp.cos(wide), -jnp.sin(wide)
            fine = wave_angle(lane * distance, lon_cells)
            fine_re, fine_im = jnp.cos(fine), -jnp.sin(fine)
            for r in range(HALF + 1):
                wavenumber = RADIX * mode + r
                kept = jnp.abs(wavenumber) <= limit
                if r in (0, HALF):
                    kept = kept & (wavenumber >= 0)
                once = r % 2 == 0 and r not in (0, HALF)
                weight = jnp.full((levels, modes), (1.0 if once else 2.0) / lon_cells)
                if r == 0:
                    weight = jnp.where(wavenumber == 0, 1.0 / lon_cells, weight)
                weight = jnp.where(kept, weight, 0.0)
                mix_re = (1.0 - share) + share * wave_ref[2 * r : 2 * r + 1]
                mix_im = -share * wave_ref[2 * r + 1 : 2 * r + 2]
                turn_re, turn_im = fine_re[:, r : r + 1], fine_im[:, r : r + 1]
                re, im = wide_re * turn_re - wide_im * turn_im, wide_re * turn_im + wide_im * turn_re
                gain_ref[row, 2 * r] = (re * mix_re - im * mix_im) * weight
                gain_ref[row, 2 * r + 1] = (re * mix_im + im * mix_re) * weight


def shift_kernel(which, columns, distance_ref, share_ref, held_ref, after_ref, *refs):
    if which == "inner":
        source_ref, moved_ref, relay_ref = refs
        relay_ref[...] = source_ref[...]
    else:
        (moved_ref,) = refs
    _, count, levels, padded = held_ref.shape
    rows = rows_of(which, share_ref.shape[0])
    number = len(rows)
    for j, row in enumerate(rows):
        distance, share = distance_ref[row].astype(jnp.int32), share_ref[row]
        for n in range(j, count, number):
            for pos in range(PAIR):
                tiles = [held_ref[PAIR - 1 - pos, n, :, columns - LANES : columns]]
                tiles += [held_ref[pos, n, :, lanes] for lanes in spans(padded, LANES)]
                for lanes, tile in zip(spans(padded, LANES), displaced(tiles, distance, share)):
                    moved_ref[n, pos, :, lanes] = tile


def inverse_kernel(
    which, columns, distance_ref, share_ref, keep_ref, gain_ref, phase_ref, high_ref, low_ref,
    held_ref, moved_ref, own_ref, other_ref, after_ref, mine_ref, send_ref,
    stack_ref, back_ref, pair_ref,
):
    _, count, levels, _ = held_ref.shape
    rows = rows_of(which, share_ref.shape[0])
    number = len(rows)
    piece = columns * PAIR // HALF
    padded = stack_ref.shape[1]
    modes = gain_ref.shape[3]
    group = levels * 2 * (HALF + 1)
    core = lax.rem(lax.axis_index("lon"), PAIR)
    cap = is_cap(lax.axis_index("lat"))
    for j, row in enumerate(rows):
        distance, share = distance_ref[row].astype(jnp.int32), share_ref[row]
        for n in range(j, count, number):
            tiles = [other_ref[n, :, 2 * MODES :], held_ref[0, n, :, :LANES]]
            (moved_ref[n, 0, :, :LANES],) = displaced(tiles, distance, share)

    @pl.when(jnp.logical_not(cap))
    def _():
        for n in range(count):
            i, j = divmod(n, number)
            mine_ref[i, j] = moved_ref[n, core, :, :columns]
            send_ref[i, j] = moved_ref[n, 1 - core, :, :columns]

    @pl.when(cap)
    def _():
        for n in range(count):
            row = rows[n % number]
            for r in range(HALF + 1):
                slot = r % HALF
                ours, theirs = (
                    [ref[n, :, (2 * slot + part) * modes : (2 * slot + part + 1) * modes] for part in range(2)]
                    for ref in (own_ref, other_ref)
                )
                if r % 2:
                    re, im = ours[0] - theirs[0], ours[1] - theirs[1]
                else:
                    re, im = ours[0] + theirs[0], ours[1] + theirs[1]
                if r == HALF:
                    re, im = pltpu.roll(re, modes // 2, 1), pltpu.roll(im, modes // 2, 1)
                g_re, g_im = gain_ref[row, 2 * r], gain_ref[row, 2 * r + 1]
                re, im = re * g_re - im * g_im, re * g_im + im * g_re
                base = n * group + 2 * r * levels
                back_ref[base : base + levels, :modes] = re
                back_ref[base : base + levels, modes:] = -im
                back_ref[base + levels : base + 2 * levels, :modes] = im
                back_ref[base + levels : base + 2 * levels, modes:] = re
        stack_ref[...] = product(back_ref[...], high_ref[...], low_ref[...], 1)
        for n in range(count):
            i, j = divmod(n, number)
            keep = keep_ref[rows[j]]
            for tile in range(0, padded, LANES):
                lanes = slice(tile, tile + LANES)
                spectrum = []
                for r in range(HALF + 1):
                    base = n * group + 2 * r * levels
                    re = stack_ref[base : base + levels, lanes]
                    im = stack_ref[base + levels : base + 2 * levels, lanes]
                    if r > 0:
                        c, s = phase_ref[2 * r : 2 * r + 1, lanes], phase_ref[2 * r + 1 : 2 * r + 2, lanes]
                        re, im = re * c - im * s, re * s + im * c
                    spectrum.append((re, im))
                width = min(LANES, piece - tile)
                for u, value in enumerate(half_inverse(spectrum)):
                    pos, start = divmod(u * piece, columns)
                    start += tile
                    shifted = moved_ref[n, pos, :, start : start + LANES]
                    result = keep * shifted + (1.0 - keep) * value
                    pair_ref[pos, n, :, start : start + width] = result[:, :width]
        for n in range(count):
            i, j = divmod(n, number)
            mine_ref[i, j] = pair_ref[core, n, :, :columns]
            send_ref[i, j] = pair_ref[1 - core, n, :, :columns]


def end_kernel(*refs):
    *refs, out_hbm, out_ref, sems = refs
    tracer_count, levels, row_count, columns = out_ref.shape
    share = tracer_count // PAIR
    core = lax.rem(lax.axis_index("lon"), PAIR)
    north = near_is_north()
    copies = []
    for place, (inner, near, far) in enumerate([refs[:3], refs[3:]]):
        for i in range(share):
            slot = place * share + i
            for lanes in spans(columns, 4 * LANES):
                a, b = near[i, 0, :, lanes], far[i, 0, :, lanes]
                out_ref[slot, :, 0, lanes] = jnp.where(north, b, a)
                out_ref[slot, :, row_count - 1, lanes] = jnp.where(north, a, b)
                for j in range(1, row_count - 1):
                    out_ref[slot, :, j, lanes] = inner[i, j - 1, :, lanes]
            t = lax.rem(core + place, PAIR) * share + i
            copies.append(pltpu.make_async_copy(out_ref.at[slot], out_hbm.at[t], sems.at[slot]))
            copies[-1].start()
    for copy in copies:
        copy.wait()


def filter_tables(lon_cells):
    piece = lon_cells // RADIX
    padded = -(-piece // LANES) * LANES
    modes = 2 * MODES // RADIX
    q = np.arange(modes) - modes // 2
    angle = 2 * np.pi * (np.arange(piece)[:, None] * q[None, :] % piece) / piece
    table = np.zeros((padded, 2 * modes))
    table[:piece, :modes] = np.cos(angle)
    table[:piece, modes:] = np.sin(angle)
    high = table.astype(jnp.bfloat16)
    low = (table - high.astype(np.float64)).astype(jnp.bfloat16)
    r = np.arange(HALF + 1)[:, None]

    def waves(steps):
        angle = 2 * np.pi * steps / lon_cells
        pairs = np.stack([np.cos(angle), np.sin(angle)], axis=1)
        return pairs.reshape(-1, steps.shape[1]).astype(np.float32)

    phase = waves(r * np.arange(padded)[None, :])
    wave = waves(RADIX * q[None, :] + r)
    return phase, wave, high, low


SMALL, WHOLE, UNREAD = pltpu.SMEM, pltpu.VMEM, pl.ANY


def call(kernel, outs, operands, scratch=(), sems=0, place=None):
    return pl.pallas_call(
        kernel,
        out_shape=[jax.ShapeDtypeStruct(shape, jnp.float32) for shape in outs],
        in_specs=[pl.BlockSpec(memory_space=place) for _, place in operands],
        out_specs=[pl.BlockSpec(memory_space=place or WHOLE)] * len(outs),
        scratch_shapes=[pltpu.VMEM(shape, jnp.float32) for shape in scratch]
        + ([pltpu.SemaphoreType.DMA((sems,))] if sems else []),
        compiler_params=pltpu.CompilerParams(vmem_limit_bytes=24 << 20),
        cost_estimate=pl.CostEstimate(flops=1, bytes_accessed=1, transcendentals=0),
    )(*[v for v, _ in operands])


def whole(*values):
    return [(v, WHOLE) for v in values]


def body(tracers, merid_courant, zonal_shift, zonal_fraction, cutoff, damping):
    tracer_count, level_count, row_count, column_count = tracers.shape
    lat_count = lax.axis_size("lat")
    lon_count = lax.axis_size("lon")
    assert lon_count == PAIR * PAIR and tracer_count % PAIR == 0 and row_count > 2
    share = tracer_count // PAIR
    lon_cells = column_count * lon_count
    phase, wave, high, low = [jnp.asarray(t) for t in filter_tables(lon_cells)]
    padded, double = high.shape
    width = -(-column_count // LANES) * LANES
    assert column_count - lon_cells // RADIX + padded <= width
    group = level_count * 2 * (HALF + 1)
    shift_rows, fraction_rows = zonal_shift.T, zonal_fraction.T

    def swap_core(value):
        return lax.ppermute(value, "lon", [(p, p ^ 1) for p in range(lon_count)])

    def swap_half(value):
        return lax.ppermute(value, "lon", [(p, p ^ 2) for p in range(lon_count)])

    def swap_band(value, first):
        pairs = []
        for b in range(first, lat_count - 1, 2):
            pairs += [(b, b + 1), (b + 1, b)]
        return lax.ppermute(value, "lat", pairs)

    def set_shape(number):
        return (share, number, level_count, column_count)

    def forward(mine, theirs, after):
        count = mine.shape[0] * mine.shape[1]
        return call(
            forward_kernel,
            [(count, level_count, 2 * MODES + LANES), (PAIR, count, level_count, width)],
            whole(mine, theirs, phase, high, low) + [(after, UNREAD)],
            [(count * group, padded)],
        )

    def shifted(which, held, after, *relay):
        count = held.shape[1]
        return call(
            functools.partial(shift_kernel, which, column_count),
            [(count, PAIR, level_count, width)] + [v.shape for v in relay],
            whole(distance, fraction, held) + [(after, UNREAD)] + whole(*relay),
        )

    def inverse(which, held, moved, own, other, after):
        count = held.shape[1]
        return call(
            functools.partial(inverse_kernel, which, column_count),
            [set_shape(count // share)] * 2,
            whole(distance, fraction, keep, gain, phase, high, low, held, moved, own, other)
            + [(after, UNREAD)],
            [(count * group, padded), (count * group, double), (PAIR, count, level_count, width)],
        )

    edge_shape = ((tracer_count + 1) * level_count, column_count)
    part_shape = (tracer_count, level_count, column_count)
    inner_mine, inner_send, near_edge, far_edge, near_part, far_part = call(
        begin_kernel,
        [set_shape(row_count - 2)] * 2 + [edge_shape] * 2 + [part_shape] * 2,
        whole(tracers, merid_courant),
    )
    inner_theirs = swap_core(inner_send)
    near_got = swap_band(near_edge, 0)
    inner_own, inner_held = forward(inner_mine, inner_theirs, near_part)
    inner_other = swap_half(inner_own)
    row_shape = (row_count, level_count, LANES)
    distance, fraction, keep, gain = call(
        functools.partial(row_kernel, column_count),
        [row_shape] * 3 + [(row_count, 2 * (HALF + 1), level_count, double // 2)],
        [(v, SMALL) for v in (shift_rows, fraction_rows, cutoff, damping)]
        + whole(wave)
        + [(inner_own, UNREAD)],
    )
    inner_moved, far_relay = shifted("inner", inner_held, inner_own, far_edge)
    far_got = swap_band(far_relay, 1)

    near_mine, near_send = call(
        functools.partial(edge_kernel, True),
        [set_shape(1)] * 2,
        whole(near_edge, near_got, near_part) + [(inner_moved, UNREAD)],
    )
    near_theirs = swap_core(near_send)
    near_own, near_held = forward(near_mine, near_theirs, inner_moved)
    near_other = swap_half(near_own)
    (near_moved,) = shifted("near", near_held, near_own)
    inner = inverse("inner", inner_held, inner_moved, inner_own, inner_other, near_moved)
    inner_back = swap_core(inner[1])

    near = inverse("near", near_held, near_moved, near_own, near_other, inner[0])
    near_back = swap_core(near[1])

    far_mine, far_send = call(
        functools.partial(edge_kernel, False),
        [set_shape(1)] * 2,
        whole(far_edge, far_got, far_part) + [(near[0], UNREAD)],
    )
    far_theirs = swap_core(far_send)
    far_own, far_held = forward(far_mine, far_theirs, near[0])
    far_other = swap_half(far_own)
    (far_moved,) = shifted("far", far_held, far_own)
    far = inverse("far", far_held, far_moved, far_own, far_other, far_moved)
    far_back = swap_core(far[1])
    (result,) = call(
        end_kernel,
        [tracers.shape],
        whole(inner[0], near[0], far[0], inner_back, near_back, far_back),
        [tracers.shape],
        tracer_count,
        pltpu.HBM,
    )
    return result


def solution(mesh):
    placed = (
        P(None, None, "lat", "lon"),
        P(None, "lat", "lon"),
        P(None, "lat"),
        P(None, "lat"),
        P(),
        P(),
    )
    return jax.shard_map(
        body, mesh=mesh, in_specs=placed, out_specs=P(None, None, "lat", "lon"), check_vma=False
    )
```

```python
import functools
import math

import jax
import jax.numpy as jnp
import numpy as np
from jax import lax
from jax.experimental import pallas as pl
from jax.experimental.pallas import tpu as pltpu
from jax.sharding import PartitionSpec as P

MODES = 1024
SMAX = 64
RADIX = 16
HALF = RADIX // 2
LANES = 128
PAIR = 2


def times_phase(value, numerator, denominator):
    re, im = value
    eighth = (8 * numerator % (8 * denominator)) / denominator
    if eighth == 0:
        return re, im
    if eighth == 2:
        return -im, re
    if eighth == 4:
        return -re, -im
    if eighth == 6:
        return im, -re
    c = math.cos(2 * math.pi * numerator / denominator)
    s = math.sin(2 * math.pi * numerator / denominator)
    if eighth == 7:
        return (re + im) * c, (im - re) * c
    if eighth == 1:
        return (re - im) * c, (re + im) * c
    return re * c - im * s, re * s + im * c


def real_dft(values):
    n = len(values)
    if n == 2:
        return [(values[0] + values[1], None), (values[0] - values[1], None)]
    even, odd = real_dft(values[0::2]), real_dft(values[1::2])
    out = [None] * (n // 2 + 1)
    for r in range(n // 4 + 1):
        (er, ei), (tr, ti) = even[r], odd[r]
        if r == 0:
            out[0] = (er + tr, None)
            out[n // 2] = (er - tr, None)
        elif r == n // 4:
            out[r] = (er, -tr)
        else:
            tr, ti = times_phase((tr, ti), -r, n)
            out[r] = (er + tr, ei + ti)
            out[n // 2 - r] = (er - tr, ti - ei)
    return out


def real_inverse(spectrum):
    n = 2 * (len(spectrum) - 1)
    if n == 2:
        a, b = spectrum[0][0], spectrum[1][0]
        return [a + b, a - b]
    even, odd = [None] * (n // 4 + 1), [None] * (n // 4 + 1)
    for r in range(n // 4 + 1):
        (ar, ai), (br, bi) = spectrum[r], spectrum[n // 2 - r]
        if r == 0:
            even[0] = (ar + br, None)
            odd[0] = (ar - br, None)
        elif r == n // 4:
            even[r] = (ar + ar, None)
            odd[r] = (-(ai + ai), None)
        else:
            even[r] = (ar + br, ai - bi)
            odd[r] = times_phase((ar - br, ai + bi), r, n)
    out = [None] * n
    out[0::2] = real_inverse(even)
    out[1::2] = real_inverse(odd)
    return out


def four(values, sign):
    (ar, ai), (br, bi), (cr, ci), (dr, di) = values
    pr, pi, mr, mi = ar + cr, ai + ci, ar - cr, ai - ci
    qr, qi, nr, ni = br + dr, bi + di, br - dr, bi - di
    if sign > 0:
        nr, ni = -nr, -ni
    return [(pr + qr, pi + qi), (mr + ni, mi - nr), (pr - qr, pi - qi), (mr - ni, mi + nr)]


def half_dft(x):
    out = [None] * 9
    out[0::2] = real_dft(x)
    odd = four([times_phase((x[v], -x[v + 4]), -v, 16) for v in range(4)], -1)
    out[1], out[5] = odd[0], odd[1]
    out[7] = (odd[2][0], -odd[2][1])
    out[3] = (odd[3][0], -odd[3][1])
    return out


def half_inverse(w):
    even = real_inverse(w[0::2])
    odd = four([w[1], w[5], (w[7][0], -w[7][1]), (w[3][0], -w[3][1])], 1)
    odd = [times_phase(value, v, 16) for v, value in enumerate(odd)]
    return [even[v] + odd[v][0] for v in range(4)] + [even[v + 4] - odd[v][1] for v in range(4)]


def split(value):
    high = value.astype(jnp.bfloat16)
    return high, (value - high.astype(jnp.float32)).astype(jnp.bfloat16)


def product(left, table_high, table_low, side):
    high, low = split(left)

    def dot(x, y):
        return lax.dot_general(x, y, (((1,), (side,)), ((), ())), preferred_element_type=jnp.float32)

    return dot(high, table_high) + (dot(high, table_low) + dot(low, table_high))


def spans(columns, width):
    return [slice(start, min(start + width, columns)) for start in range(0, columns, width)]


def is_cap(lat):
    count = lax.axis_size("lat")
    return (lat < count // 4) | (lat >= count - count // 4)


def flux_of(face_speed, south, north):
    return jnp.maximum(face_speed, 0.0) * south + jnp.minimum(face_speed, 0.0) * north


def near_is_north():
    return lax.rem(lax.axis_index("lat"), 2) == 0


def begin_kernel(
    cells_hbm, speed_hbm, mine_ref, send_ref, near_ref, far_ref, near_part_ref, far_part_ref,
    cells_ref, speed_ref, sems,
):
    tracer_count, levels, row_count, columns = cells_ref.shape
    share = tracer_count // PAIR
    core = lax.rem(lax.axis_index("lon"), PAIR)
    north = near_is_north()
    copies = [pltpu.make_async_copy(speed_hbm, speed_ref, sems.at[tracer_count])]
    copies += [
        pltpu.make_async_copy(cells_hbm.at[t], cells_ref.at[t], sems.at[t]) for t in range(tracer_count)
    ]
    for copy in copies:
        copy.start()
    for copy in copies:
        copy.wait()
    for lanes in spans(columns, 2 * LANES):
        speed = [speed_ref[:, j, lanes] for j in range(row_count)]
        near_ref[tracer_count * levels :, lanes] = speed[0]
        far_ref[tracer_count * levels :, lanes] = speed[0]
        for which, out_ref in enumerate([mine_ref, send_ref]):
            for i in range(share):
                t = lax.rem(core + which, PAIR) * share + i
                place = pl.ds(pl.multiple_of(t * levels, levels), levels)
                x = [cells_ref[t, :, j, lanes] for j in range(row_count)]
                flux = [flux_of(speed[j], x[j - 1], x[j]) for j in range(1, row_count)]
                for j in range(1, row_count - 1):
                    out_ref[i, j - 1, :, lanes] = x[j] + flux[j - 1] - flux[j]
                near_ref[place, lanes] = jnp.where(north, x[-1], x[0])
                far_ref[place, lanes] = jnp.where(north, x[0], x[-1])
                south_part, north_part = x[0] - flux[0], x[-1] + flux[-1]
                near_part_ref[t, :, lanes] = jnp.where(north, north_part, south_part)
                far_part_ref[t, :, lanes] = jnp.where(north, south_part, north_part)


def edge_kernel(is_near, own_ref, got_ref, part_ref, after_ref, mine_ref, send_ref):
    tracer_count, levels, columns = part_ref.shape
    share = tracer_count // PAIR
    total = tracer_count * levels
    core = lax.rem(lax.axis_index("lon"), PAIR)
    lat = lax.axis_index("lat")
    north = near_is_north() if is_near else jnp.logical_not(near_is_north())
    wall = jnp.where(north, lat == lax.axis_size("lat") - 1, lat == 0)
    for lanes in spans(columns, 3 * LANES):
        speed = jnp.where(north, got_ref[total:, lanes], own_ref[total:, lanes])
        speed = jnp.where(wall, 0.0, speed)
        for which, out_ref in enumerate([mine_ref, send_ref]):
            for i in range(share):
                t = lax.rem(core + which, PAIR) * share + i
                place = pl.ds(pl.multiple_of(t * levels, levels), levels)
                own, got = own_ref[place, lanes], got_ref[place, lanes]
                flux = flux_of(speed, jnp.where(north, own, got), jnp.where(north, got, own))
                out_ref[i, 0, :, lanes] = part_ref[t, :, lanes] + jnp.where(north, -flux, flux)


def forward_kernel(
    mine_ref, theirs_ref, phase_ref, high_ref, low_ref, after_ref, message_ref, held_ref, stack_ref
):
    share, number, levels, columns = mine_ref.shape
    piece = columns * PAIR // HALF
    padded = stack_ref.shape[1]
    modes = high_ref.shape[1] // 2
    group = levels * 2 * (HALF + 1)
    core = lax.rem(lax.axis_index("lon"), PAIR)
    count = share * number
    for n in range(count):
        i, j = divmod(n, number)
        held_ref[core, n, :, :columns] = mine_ref[i, j]
        held_ref[1 - core, n, :, :columns] = theirs_ref[i, j]
        for pos in range(PAIR):
            held_ref[pos, n, :, columns:] = jnp.zeros((levels, held_ref.shape[3] - columns), jnp.float32)
        message_ref[n, :, 2 * MODES :] = held_ref[PAIR - 1, n, :, columns - LANES : columns]

    @pl.when(is_cap(lax.axis_index("lat")))
    def _():
        for n in range(count):
            for tile in range(0, padded, LANES):
                lanes = slice(tile, tile + LANES)
                x = []
                for u in range(HALF):
                    pos, start = divmod(u * piece, columns)
                    x.append(held_ref[pos, n, :, start + tile : start + tile + LANES])
                for r, (re, im) in enumerate(half_dft(x)):
                    base = n * group + 2 * r * levels
                    if r == 0:
                        im = jnp.zeros_like(re)
                    else:
                        c, s = phase_ref[2 * r : 2 * r + 1, lanes], phase_ref[2 * r + 1 : 2 * r + 2, lanes]
                        if im is None:
                            re, im = re * c, -(re * s)
                        else:
                            re, im = re * c + im * s, im * c - re * s
                    stack_ref[base : base + levels, lanes] = re
                    stack_ref[base + levels : base + 2 * levels, lanes] = im
        coeffs = product(stack_ref[...], high_ref[...], low_ref[...], 0)
        upper = lax.broadcasted_iota(jnp.int32, (levels, modes), 1) >= modes // 2
        for n in range(count):
            first = None
            for r in [0, HALF] + list(range(1, HALF)):
                base = n * group + 2 * r * levels
                re, im = coeffs[base : base + levels], coeffs[base + levels : base + 2 * levels]
                x_re = re[:, :modes] + im[:, modes:]
                x_im = im[:, :modes] - re[:, modes:]
                if r == 0:
                    first = x_re, x_im
                    continue
                slot = r
                if r == HALF:
                    x_re = jnp.where(upper, first[0], pltpu.roll(x_re, modes // 2, 1))
                    x_im = jnp.where(upper, first[1], pltpu.roll(x_im, modes // 2, 1))
                    slot = 0
                message_ref[n, :, 2 * slot * modes : (2 * slot + 1) * modes] = x_re
                message_ref[n, :, (2 * slot + 1) * modes : (2 * slot + 2) * modes] = x_im


def row_vector(ref, row, levels):
    level = lax.broadcasted_iota(jnp.int32, (levels, LANES), 0)
    out = jnp.full((levels, LANES), ref[row, 0])
    for i in range(1, levels):
        out = jnp.where(level == i, ref[row, i], out)
    return out


def displaced(tiles, distance, share):
    lane = lax.broadcasted_iota(jnp.int32, distance.shape, 1)

    def moved(steps):
        index = (lane - steps) & (LANES - 1)
        turned = [jnp.take_along_axis(v, index, axis=1, mode="promise_in_bounds") for v in tiles]
        from_left = lane < steps
        return [jnp.where(from_left, a, b) for a, b in zip(turned, turned[1:])]

    pairs = zip(moved(distance), moved(distance + 1))
    return [(1.0 - share) * here + share * earlier for here, earlier in pairs]


def rows_of(which, row_count):
    if which == "inner":
        return list(range(1, row_count - 1))
    north = near_is_north() if which == "near" else jnp.logical_not(near_is_north())
    return [jnp.where(north, row_count - 1, 0)]


def wave_angle(steps, lon_cells):
    steps = lax.rem(steps, lon_cells)
    return steps.astype(jnp.float32) * (2.0 * math.pi / lon_cells)


def row_kernel(
    columns, shift_ref, fraction_ref, cutoff_ref, damping_ref, wave_ref, after_ref,
    distance_ref, share_ref, keep_ref, gain_ref,
):
    row_count, levels = shift_ref.shape
    lon_cells = columns * PAIR * PAIR
    modes = gain_ref.shape[3]
    lat = lax.axis_index("lat")
    for row in range(row_count):
        distance_ref[row] = row_vector(shift_ref, row, levels).astype(jnp.float32)
        share_ref[row] = row_vector(fraction_ref, row, levels)
        keep_ref[row] = jnp.full((levels, LANES), damping_ref[lat * row_count + row])

    @pl.when(is_cap(lat))
    def _():
        lane = lax.broadcasted_iota(jnp.int32, (levels, modes), 1)
        mode = lane - modes // 2
        for row in range(row_count):
            distance = distance_ref[row].astype(jnp.int32)
            share = share_ref[row]
            limit = cutoff_ref[lat * row_count + row]
            wide = wave_angle(RADIX * mode * distance, lon_cells)
            wide_re, wide_im = jnp.cos(wide), -jnp.sin(wide)
            fine = wave_angle(lane * distance, lon_cells)
            fine_re, fine_im = jnp.cos(fine), -jnp.sin(fine)
            for r in range(HALF + 1):
                wavenumber = RADIX * mode + r
                kept = jnp.abs(wavenumber) <= limit
                if r in (0, HALF):
                    kept = kept & (wavenumber >= 0)
                once = r % 2 == 0 and r not in (0, HALF)
                weight = jnp.full((levels, modes), (1.0 if once else 2.0) / lon_cells)
                if r == 0:
                    weight = jnp.where(wavenumber == 0, 1.0 / lon_cells, weight)
                weight = jnp.where(kept, weight, 0.0)
                mix_re = (1.0 - share) + share * wave_ref[2 * r : 2 * r + 1]
                mix_im = -share * wave_ref[2 * r + 1 : 2 * r + 2]
                turn_re, turn_im = fine_re[:, r : r + 1], fine_im[:, r : r + 1]
                re, im = wide_re * turn_re - wide_im * turn_im, wide_re * turn_im + wide_im * turn_re
                gain_ref[row, 2 * r] = (re * mix_re - im * mix_im) * weight
                gain_ref[row, 2 * r + 1] = (re * mix_im + im * mix_re) * weight


def shift_kernel(which, columns, distance_ref, share_ref, held_ref, after_ref, *refs):
    if which == "inner":
        source_ref, moved_ref, relay_ref = refs
        relay_ref[...] = source_ref[...]
    else:
        (moved_ref,) = refs
    _, count, levels, padded = held_ref.shape
    rows = rows_of(which, share_ref.shape[0])
    number = len(rows)
    for j, row in enumerate(rows):
        distance, share = distance_ref[row].astype(jnp.int32), share_ref[row]
        for n in range(j, count, number):
            for pos in range(PAIR):
                tiles = [held_ref[PAIR - 1 - pos, n, :, columns - LANES : columns]]
                tiles += [held_ref[pos, n, :, lanes] for lanes in spans(padded, LANES)]
                for lanes, tile in zip(spans(padded, LANES), displaced(tiles, distance, share)):
                    moved_ref[n, pos, :, lanes] = tile


def inverse_kernel(
    which, columns, distance_ref, share_ref, keep_ref, gain_ref, phase_ref, high_ref, low_ref,
    held_ref, moved_ref, own_ref, other_ref, after_ref, mine_ref, send_ref,
    stack_ref, back_ref, pair_ref,
):
    _, count, levels, _ = held_ref.shape
    rows = rows_of(which, share_ref.shape[0])
    number = len(rows)
    piece = columns * PAIR // HALF
    padded = stack_ref.shape[1]
    modes = gain_ref.shape[3]
    group = levels * 2 * (HALF + 1)
    core = lax.rem(lax.axis_index("lon"), PAIR)
    cap = is_cap(lax.axis_index("lat"))
    for j, row in enumerate(rows):
        distance, share = distance_ref[row].astype(jnp.int32), share_ref[row]
        for n in range(j, count, number):
            tiles = [other_ref[n, :, 2 * MODES :], held_ref[0, n, :, :LANES]]
            (moved_ref[n, 0, :, :LANES],) = displaced(tiles, distance, share)

    @pl.when(jnp.logical_not(cap))
    def _():
        for n in range(count):
            i, j = divmod(n, number)
            mine_ref[i, j] = moved_ref[n, core, :, :columns]
            send_ref[i, j] = moved_ref[n, 1 - core, :, :columns]

    @pl.when(cap)
    def _():
        for n in range(count):
            row = rows[n % number]
            for r in range(HALF + 1):
                slot = r % HALF
                ours, theirs = (
                    [ref[n, :, (2 * slot + part) * modes : (2 * slot + part + 1) * modes] for part in range(2)]
                    for ref in (own_ref, other_ref)
                )
                if r % 2:
                    re, im = ours[0] - theirs[0], ours[1] - theirs[1]
                else:
                    re, im = ours[0] + theirs[0], ours[1] + theirs[1]
                if r == HALF:
                    re, im = pltpu.roll(re, modes // 2, 1), pltpu.roll(im, modes // 2, 1)
                g_re, g_im = gain_ref[row, 2 * r], gain_ref[row, 2 * r + 1]
                re, im = re * g_re - im * g_im, re * g_im + im * g_re
                base = n * group + 2 * r * levels
                back_ref[base : base + levels, :modes] = re
                back_ref[base : base + levels, modes:] = -im
                back_ref[base + levels : base + 2 * levels, :modes] = im
                back_ref[base + levels : base + 2 * levels, modes:] = re
        stack_ref[...] = product(back_ref[...], high_ref[...], low_ref[...], 1)
        for n in range(count):
            i, j = divmod(n, number)
            keep = keep_ref[rows[j]]
            for tile in range(0, padded, LANES):
                lanes = slice(tile, tile + LANES)
                spectrum = []
                for r in range(HALF + 1):
                    base = n * group + 2 * r * levels
                    re = stack_ref[base : base + levels, lanes]
                    im = stack_ref[base + levels : base + 2 * levels, lanes]
                    if r > 0:
                        c, s = phase_ref[2 * r : 2 * r + 1, lanes], phase_ref[2 * r + 1 : 2 * r + 2, lanes]
                        re, im = re * c - im * s, re * s + im * c
                    spectrum.append((re, im))
                width = min(LANES, piece - tile)
                for u, value in enumerate(half_inverse(spectrum)):
                    pos, start = divmod(u * piece, columns)
                    start += tile
                    shifted = moved_ref[n, pos, :, start : start + LANES]
                    result = keep * shifted + (1.0 - keep) * value
                    pair_ref[pos, n, :, start : start + width] = result[:, :width]
        for n in range(count):
            i, j = divmod(n, number)
            mine_ref[i, j] = pair_ref[core, n, :, :columns]
            send_ref[i, j] = pair_ref[1 - core, n, :, :columns]


def end_kernel(*refs):
    *refs, out_hbm, out_ref, sems = refs
    tracer_count, levels, row_count, columns = out_ref.shape
    share = tracer_count // PAIR
    core = lax.rem(lax.axis_index("lon"), PAIR)
    north = near_is_north()
    copies = []
    for place, (inner, near, far) in enumerate([refs[:3], refs[3:]]):
        for i in range(share):
            slot = place * share + i
            for lanes in spans(columns, 4 * LANES):
                a, b = near[i, 0, :, lanes], far[i, 0, :, lanes]
                out_ref[slot, :, 0, lanes] = jnp.where(north, b, a)
                out_ref[slot, :, row_count - 1, lanes] = jnp.where(north, a, b)
                for j in range(1, row_count - 1):
                    out_ref[slot, :, j, lanes] = inner[i, j - 1, :, lanes]
            t = lax.rem(core + place, PAIR) * share + i
            copies.append(pltpu.make_async_copy(out_ref.at[slot], out_hbm.at[t], sems.at[slot]))
            copies[-1].start()
    for copy in copies:
        copy.wait()


def filter_tables(lon_cells):
    piece = lon_cells // RADIX
    padded = -(-piece // LANES) * LANES
    modes = 2 * MODES // RADIX
    q = np.arange(modes) - modes // 2
    angle = 2 * np.pi * (np.arange(piece)[:, None] * q[None, :] % piece) / piece
    table = np.zeros((padded, 2 * modes))
    table[:piece, :modes] = np.cos(angle)
    table[:piece, modes:] = np.sin(angle)
    high = table.astype(jnp.bfloat16)
    low = (table - high.astype(np.float64)).astype(jnp.bfloat16)
    r = np.arange(HALF + 1)[:, None]

    def waves(steps):
        angle = 2 * np.pi * steps / lon_cells
        pairs = np.stack([np.cos(angle), np.sin(angle)], axis=1)
        return pairs.reshape(-1, steps.shape[1]).astype(np.float32)

    phase = waves(r * np.arange(padded)[None, :])
    wave = waves(RADIX * q[None, :] + r)
    return phase, wave, high, low


SMALL, WHOLE, UNREAD = pltpu.SMEM, pltpu.VMEM, pl.ANY


def call(kernel, outs, operands, scratch=(), sems=0, place=None):
    return pl.pallas_call(
        kernel,
        out_shape=[jax.ShapeDtypeStruct(shape, jnp.float32) for shape in outs],
        in_specs=[pl.BlockSpec(memory_space=place) for _, place in operands],
        out_specs=[pl.BlockSpec(memory_space=place or WHOLE)] * len(outs),
        scratch_shapes=[pltpu.VMEM(shape, jnp.float32) for shape in scratch]
        + ([pltpu.SemaphoreType.DMA((sems,))] if sems else []),
        compiler_params=pltpu.CompilerParams(vmem_limit_bytes=24 << 20),
        cost_estimate=pl.CostEstimate(flops=1, bytes_accessed=1, transcendentals=0),
    )(*[v for v, _ in operands])


def whole(*values):
    return [(v, WHOLE) for v in values]


def body(tracers, merid_courant, zonal_shift, zonal_fraction, cutoff, damping):
    tracer_count, level_count, row_count, column_count = tracers.shape
    lat_count = lax.axis_size("lat")
    lon_count = lax.axis_size("lon")
    assert lon_count == PAIR * PAIR and tracer_count % PAIR == 0 and row_count > 2
    share = tracer_count // PAIR
    lon_cells = column_count * lon_count
    phase, wave, high, low = [jnp.asarray(t) for t in filter_tables(lon_cells)]
    padded, double = high.shape
    width = -(-column_count // LANES) * LANES
    assert column_count - lon_cells // RADIX + padded <= width
    group = level_count * 2 * (HALF + 1)
    shift_rows, fraction_rows = zonal_shift.T, zonal_fraction.T

    def swap_core(value):
        return lax.ppermute(value, "lon", [(p, p ^ 1) for p in range(lon_count)])

    def swap_half(value):
        return lax.ppermute(value, "lon", [(p, p ^ 2) for p in range(lon_count)])

    def swap_band(value, first):
        pairs = []
        for b in range(first, lat_count - 1, 2):
            pairs += [(b, b + 1), (b + 1, b)]
        return lax.ppermute(value, "lat", pairs)

    def set_shape(number):
        return (share, number, level_count, column_count)

    def forward(mine, theirs, after):
        count = mine.shape[0] * mine.shape[1]
        return call(
            forward_kernel,
            [(count, level_count, 2 * MODES + LANES), (PAIR, count, level_count, width)],
            whole(mine, theirs, phase, high, low) + [(after, UNREAD)],
            [(count * group, padded)],
        )

    def shifted(which, held, after, *relay):
        count = held.shape[1]
        return call(
            functools.partial(shift_kernel, which, column_count),
            [(count, PAIR, level_count, width)] + [v.shape for v in relay],
            whole(distance, fraction, held) + [(after, UNREAD)] + whole(*relay),
        )

    def inverse(which, held, moved, own, other, after):
        count = held.shape[1]
        return call(
            functools.partial(inverse_kernel, which, column_count),
            [set_shape(count // share)] * 2,
            whole(distance, fraction, keep, gain, phase, high, low, held, moved, own, other)
            + [(after, UNREAD)],
            [(count * group, padded), (count * group, double), (PAIR, count, level_count, width)],
        )

    edge_shape = ((tracer_count + 1) * level_count, column_count)
    part_shape = (tracer_count, level_count, column_count)
    inner_mine, inner_send, near_edge, far_edge, near_part, far_part = call(
        begin_kernel,
        [set_shape(row_count - 2)] * 2 + [edge_shape] * 2 + [part_shape] * 2,
        [(pltpu.with_memory_space_constraint(v, pltpu.HBM), pltpu.HBM) for v in (tracers, merid_courant)],
        [tracers.shape, merid_courant.shape],
        tracer_count + 1,
    )
    inner_theirs = swap_core(inner_send)
    near_got = swap_band(near_edge, 0)
    inner_own, inner_held = forward(inner_mine, inner_theirs, near_part)
    inner_other = swap_half(inner_own)
    row_shape = (row_count, level_count, LANES)
    distance, fraction, keep, gain = call(
        functools.partial(row_kernel, column_count),
        [row_shape] * 3 + [(row_count, 2 * (HALF + 1), level_count, double // 2)],
        [(v, SMALL) for v in (shift_rows, fraction_rows, cutoff, damping)]
        + whole(wave)
        + [(inner_own, UNREAD)],
    )
    inner_moved, far_relay = shifted("inner", inner_held, inner_own, far_edge)
    far_got = swap_band(far_relay, 1)

    near_mine, near_send = call(
        functools.partial(edge_kernel, True),
        [set_shape(1)] * 2,
        whole(near_edge, near_got, near_part) + [(inner_moved, UNREAD)],
    )
    near_theirs = swap_core(near_send)
    near_own, near_held = forward(near_mine, near_theirs, inner_moved)
    near_other = swap_half(near_own)
    (near_moved,) = shifted("near", near_held, near_own)
    inner = inverse("inner", inner_held, inner_moved, inner_own, inner_other, near_moved)
    inner_back = swap_core(inner[1])

    far_mine, far_send = call(
        functools.partial(edge_kernel, False),
        [set_shape(1)] * 2,
        whole(far_edge, far_got, far_part) + [(inner[0], UNREAD)],
    )
    far_theirs = swap_core(far_send)
    near = inverse("near", near_held, near_moved, near_own, near_other, far_mine)
    near_back = swap_core(near[1])
    far_own, far_held = forward(far_mine, far_theirs, near[0])
    far_other = swap_half(far_own)
    (far_moved,) = shifted("far", far_held, far_own)
    far = inverse("far", far_held, far_moved, far_own, far_other, far_moved)
    far_back = swap_core(far[1])
    (result,) = call(
        end_kernel,
        [tracers.shape],
        whole(inner[0], near[0], far[0], inner_back, near_back, far_back),
        [tracers.shape],
        tracer_count,
        pltpu.HBM,
    )
    return result


def solution(mesh):
    placed = (
        P(None, None, "lat", "lon"),
        P(None, "lat", "lon"),
        P(None, "lat"),
        P(None, "lat"),
        P(),
        P(),
    )
    return jax.shard_map(
        body, mesh=mesh, in_specs=placed, out_specs=P(None, None, "lat", "lon"), check_vma=False
    )
```

```python
import functools
import math

import jax
import jax.numpy as jnp
import numpy as np
from jax import lax
from jax.experimental import pallas as pl
from jax.experimental.pallas import tpu as pltpu
from jax.sharding import PartitionSpec as P

MODES = 1024
SMAX = 64
RADIX = 16
HALF = RADIX // 2
LANES = 128
PAIR = 2


def times_phase(value, numerator, denominator):
    re, im = value
    eighth = (8 * numerator % (8 * denominator)) / denominator
    if eighth == 0:
        return re, im
    if eighth == 2:
        return -im, re
    if eighth == 4:
        return -re, -im
    if eighth == 6:
        return im, -re
    c = math.cos(2 * math.pi * numerator / denominator)
    s = math.sin(2 * math.pi * numerator / denominator)
    if eighth == 7:
        return (re + im) * c, (im - re) * c
    if eighth == 1:
        return (re - im) * c, (re + im) * c
    return re * c - im * s, re * s + im * c


def real_dft(values):
    n = len(values)
    if n == 2:
        return [(values[0] + values[1], None), (values[0] - values[1], None)]
    even, odd = real_dft(values[0::2]), real_dft(values[1::2])
    out = [None] * (n // 2 + 1)
    for r in range(n // 4 + 1):
        (er, ei), (tr, ti) = even[r], odd[r]
        if r == 0:
            out[0] = (er + tr, None)
            out[n // 2] = (er - tr, None)
        elif r == n // 4:
            out[r] = (er, -tr)
        else:
            tr, ti = times_phase((tr, ti), -r, n)
            out[r] = (er + tr, ei + ti)
            out[n // 2 - r] = (er - tr, ti - ei)
    return out


def real_inverse(spectrum):
    n = 2 * (len(spectrum) - 1)
    if n == 2:
        a, b = spectrum[0][0], spectrum[1][0]
        return [a + b, a - b]
    even, odd = [None] * (n // 4 + 1), [None] * (n // 4 + 1)
    for r in range(n // 4 + 1):
        (ar, ai), (br, bi) = spectrum[r], spectrum[n // 2 - r]
        if r == 0:
            even[0] = (ar + br, None)
            odd[0] = (ar - br, None)
        elif r == n // 4:
            even[r] = (ar + ar, None)
            odd[r] = (-(ai + ai), None)
        else:
            even[r] = (ar + br, ai - bi)
            odd[r] = times_phase((ar - br, ai + bi), r, n)
    out = [None] * n
    out[0::2] = real_inverse(even)
    out[1::2] = real_inverse(odd)
    return out


def four(values, sign):
    (ar, ai), (br, bi), (cr, ci), (dr, di) = values
    pr, pi, mr, mi = ar + cr, ai + ci, ar - cr, ai - ci
    qr, qi, nr, ni = br + dr, bi + di, br - dr, bi - di
    if sign > 0:
        nr, ni = -nr, -ni
    return [(pr + qr, pi + qi), (mr + ni, mi - nr), (pr - qr, pi - qi), (mr - ni, mi + nr)]


def half_dft(x):
    out = [None] * 9
    out[0::2] = real_dft(x)
    odd = four([times_phase((x[v], -x[v + 4]), -v, 16) for v in range(4)], -1)
    out[1], out[5] = odd[0], odd[1]
    out[7] = (odd[2][0], -odd[2][1])
    out[3] = (odd[3][0], -odd[3][1])
    return out


def half_inverse(w):
    even = real_inverse(w[0::2])
    odd = four([w[1], w[5], (w[7][0], -w[7][1]), (w[3][0], -w[3][1])], 1)
    odd = [times_phase(value, v, 16) for v, value in enumerate(odd)]
    return [even[v] + odd[v][0] for v in range(4)] + [even[v + 4] - odd[v][1] for v in range(4)]


def split(value):
    high = value.astype(jnp.bfloat16)
    return high, (value - high.astype(jnp.float32)).astype(jnp.bfloat16)


def product(left, table_high, table_low, side):
    high, low = split(left)

    def dot(x, y):
        return lax.dot_general(x, y, (((1,), (side,)), ((), ())), preferred_element_type=jnp.float32)

    return dot(high, table_high) + (dot(high, table_low) + dot(low, table_high))


def spans(columns, width):
    return [slice(start, min(start + width, columns)) for start in range(0, columns, width)]


def is_cap(lat):
    count = lax.axis_size("lat")
    return (lat < count // 4) | (lat >= count - count // 4)


def flux_of(face_speed, south, north):
    return jnp.maximum(face_speed, 0.0) * south + jnp.minimum(face_speed, 0.0) * north


def near_is_north():
    return lax.rem(lax.axis_index("lat"), 2) == 0


def begin_kernel(
    cells_hbm, speed_hbm, mine_ref, send_ref, near_ref, far_ref, near_part_ref, far_part_ref,
    cells_ref, speed_ref, sems,
):
    tracer_count, levels, row_count, columns = cells_ref.shape
    share = tracer_count // PAIR
    core = lax.rem(lax.axis_index("lon"), PAIR)
    north = near_is_north()
    copies = [pltpu.make_async_copy(speed_hbm, speed_ref, sems.at[tracer_count])]
    copies += [
        pltpu.make_async_copy(cells_hbm.at[t], cells_ref.at[t], sems.at[t]) for t in range(tracer_count)
    ]
    for copy in copies:
        copy.start()
    for copy in copies:
        copy.wait()
    for lanes in spans(columns, 2 * LANES):
        speed = [speed_ref[:, j, lanes] for j in range(row_count)]
        near_ref[tracer_count * levels :, lanes] = speed[0]
        far_ref[tracer_count * levels :, lanes] = speed[0]
        for which, out_ref in enumerate([mine_ref, send_ref]):
            for i in range(share):
                t = lax.rem(core + which, PAIR) * share + i
                place = pl.ds(pl.multiple_of(t * levels, levels), levels)
                x = [cells_ref[t, :, j, lanes] for j in range(row_count)]
                flux = [flux_of(speed[j], x[j - 1], x[j]) for j in range(1, row_count)]
                for j in range(1, row_count - 1):
                    out_ref[i, j - 1, :, lanes] = x[j] + flux[j - 1] - flux[j]
                near_ref[place, lanes] = jnp.where(north, x[-1], x[0])
                far_ref[place, lanes] = jnp.where(north, x[0], x[-1])
                south_part, north_part = x[0] - flux[0], x[-1] + flux[-1]
                near_part_ref[t, :, lanes] = jnp.where(north, north_part, south_part)
                far_part_ref[t, :, lanes] = jnp.where(north, south_part, north_part)


def edge_kernel(is_near, own_ref, got_ref, part_ref, after_ref, mine_ref, send_ref):
    tracer_count, levels, columns = part_ref.shape
    share = tracer_count // PAIR
    total = tracer_count * levels
    core = lax.rem(lax.axis_index("lon"), PAIR)
    lat = lax.axis_index("lat")
    north = near_is_north() if is_near else jnp.logical_not(near_is_north())
    wall = jnp.where(north, lat == lax.axis_size("lat") - 1, lat == 0)
    for lanes in spans(columns, 3 * LANES):
        speed = jnp.where(north, got_ref[total:, lanes], own_ref[total:, lanes])
        speed = jnp.where(wall, 0.0, speed)
        for which, out_ref in enumerate([mine_ref, send_ref]):
            for i in range(share):
                t = lax.rem(core + which, PAIR) * share + i
                place = pl.ds(pl.multiple_of(t * levels, levels), levels)
                own, got = own_ref[place, lanes], got_ref[place, lanes]
                flux = flux_of(speed, jnp.where(north, own, got), jnp.where(north, got, own))
                out_ref[i, 0, :, lanes] = part_ref[t, :, lanes] + jnp.where(north, -flux, flux)


def forward_kernel(
    mine_ref, theirs_ref, phase_ref, high_ref, low_ref, after_ref, message_ref, held_ref, stack_ref
):
    share, number, levels, columns = mine_ref.shape
    piece = columns * PAIR // HALF
    padded = stack_ref.shape[1]
    modes = high_ref.shape[1] // 2
    group = levels * 2 * (HALF + 1)
    core = lax.rem(lax.axis_index("lon"), PAIR)
    count = share * number
    for n in range(count):
        i, j = divmod(n, number)
        held_ref[core, n, :, :columns] = mine_ref[i, j]
        held_ref[1 - core, n, :, :columns] = theirs_ref[i, j]
        for pos in range(PAIR):
            held_ref[pos, n, :, columns:] = jnp.zeros((levels, held_ref.shape[3] - columns), jnp.float32)
        message_ref[n, :, 2 * MODES :] = held_ref[PAIR - 1, n, :, columns - LANES : columns]

    @pl.when(is_cap(lax.axis_index("lat")))
    def _():
        for n in range(count):
            for tile in range(0, padded, LANES):
                lanes = slice(tile, tile + LANES)
                x = []
                for u in range(HALF):
                    pos, start = divmod(u * piece, columns)
                    x.append(held_ref[pos, n, :, start + tile : start + tile + LANES])
                for r, (re, im) in enumerate(half_dft(x)):
                    base = n * group + 2 * r * levels
                    if r == 0:
                        im = jnp.zeros_like(re)
                    else:
                        c, s = phase_ref[2 * r : 2 * r + 1, lanes], phase_ref[2 * r + 1 : 2 * r + 2, lanes]
                        if im is None:
                            re, im = re * c, -(re * s)
                        else:
                            re, im = re * c + im * s, im * c - re * s
                    stack_ref[base : base + levels, lanes] = re
                    stack_ref[base + levels : base + 2 * levels, lanes] = im
        coeffs = product(stack_ref[...], high_ref[...], low_ref[...], 0)
        upper = lax.broadcasted_iota(jnp.int32, (levels, modes), 1) >= modes // 2
        for n in range(count):
            first = None
            for r in [0, HALF] + list(range(1, HALF)):
                base = n * group + 2 * r * levels
                re, im = coeffs[base : base + levels], coeffs[base + levels : base + 2 * levels]
                x_re = re[:, :modes] + im[:, modes:]
                x_im = im[:, :modes] - re[:, modes:]
                if r == 0:
                    first = x_re, x_im
                    continue
                slot = r
                if r == HALF:
                    x_re = jnp.where(upper, first[0], pltpu.roll(x_re, modes // 2, 1))
                    x_im = jnp.where(upper, first[1], pltpu.roll(x_im, modes // 2, 1))
                    slot = 0
                message_ref[n, :, 2 * slot * modes : (2 * slot + 1) * modes] = x_re
                message_ref[n, :, (2 * slot + 1) * modes : (2 * slot + 2) * modes] = x_im


def row_vector(ref, row, levels):
    level = lax.broadcasted_iota(jnp.int32, (levels, LANES), 0)
    out = jnp.full((levels, LANES), ref[row, 0])
    for i in range(1, levels):
        out = jnp.where(level == i, ref[row, i], out)
    return out


def displaced(tiles, distance, share):
    lane = lax.broadcasted_iota(jnp.int32, distance.shape, 1)

    def moved(steps):
        index = (lane - steps) & (LANES - 1)
        turned = [jnp.take_along_axis(v, index, axis=1, mode="promise_in_bounds") for v in tiles]
        from_left = lane < steps
        return [jnp.where(from_left, a, b) for a, b in zip(turned, turned[1:])]

    pairs = zip(moved(distance), moved(distance + 1))
    return [(1.0 - share) * here + share * earlier for here, earlier in pairs]


def rows_of(which, row_count):
    if which == "inner":
        return list(range(1, row_count - 1))
    north = near_is_north() if which == "near" else jnp.logical_not(near_is_north())
    return [jnp.where(north, row_count - 1, 0)]


def wave_angle(steps, lon_cells):
    steps = lax.rem(steps, lon_cells)
    return steps.astype(jnp.float32) * (2.0 * math.pi / lon_cells)


def row_kernel(
    columns, shift_ref, fraction_ref, cutoff_ref, damping_ref, wave_ref, after_ref,
    distance_ref, share_ref, keep_ref, gain_ref,
):
    row_count, levels = shift_ref.shape
    lon_cells = columns * PAIR * PAIR
    modes = gain_ref.shape[3]
    lat = lax.axis_index("lat")
    for row in range(row_count):
        distance_ref[row] = row_vector(shift_ref, row, levels).astype(jnp.float32)
        share_ref[row] = row_vector(fraction_ref, row, levels)
        keep_ref[row] = jnp.full((levels, LANES), damping_ref[lat * row_count + row])

    @pl.when(is_cap(lat))
    def _():
        lane = lax.broadcasted_iota(jnp.int32, (levels, modes), 1)
        mode = lane - modes // 2
        for row in range(row_count):
            distance = distance_ref[row].astype(jnp.int32)
            share = share_ref[row]
            limit = cutoff_ref[lat * row_count + row]
            wide = wave_angle(RADIX * mode * distance, lon_cells)
            wide_re, wide_im = jnp.cos(wide), -jnp.sin(wide)
            fine = wave_angle(lane * distance, lon_cells)
            fine_re, fine_im = jnp.cos(fine), -jnp.sin(fine)
            for r in range(HALF + 1):
                wavenumber = RADIX * mode + r
                kept = jnp.abs(wavenumber) <= limit
                if r in (0, HALF):
                    kept = kept & (wavenumber >= 0)
                once = r % 2 == 0 and r not in (0, HALF)
                weight = jnp.full((levels, modes), (1.0 if once else 2.0) / lon_cells)
                if r == 0:
                    weight = jnp.where(wavenumber == 0, 1.0 / lon_cells, weight)
                weight = jnp.where(kept, weight, 0.0)
                mix_re = (1.0 - share) + share * wave_ref[2 * r : 2 * r + 1]
                mix_im = -share * wave_ref[2 * r + 1 : 2 * r + 2]
                turn_re, turn_im = fine_re[:, r : r + 1], fine_im[:, r : r + 1]
                re, im = wide_re * turn_re - wide_im * turn_im, wide_re * turn_im + wide_im * turn_re
                gain_ref[row, 2 * r] = (re * mix_re - im * mix_im) * weight
                gain_ref[row, 2 * r + 1] = (re * mix_im + im * mix_re) * weight


def shift_kernel(which, columns, distance_ref, share_ref, held_ref, after_ref, moved_ref):
    _, count, levels, padded = held_ref.shape
    rows = rows_of(which, share_ref.shape[0])
    number = len(rows)
    for j, row in enumerate(rows):
        distance, share = distance_ref[row].astype(jnp.int32), share_ref[row]
        for n in range(j, count, number):
            for pos in range(PAIR):
                tiles = [held_ref[PAIR - 1 - pos, n, :, columns - LANES : columns]]
                tiles += [held_ref[pos, n, :, lanes] for lanes in spans(padded, LANES)]
                for lanes, tile in zip(spans(padded, LANES), displaced(tiles, distance, share)):
                    moved_ref[n, pos, :, lanes] = tile


def inverse_kernel(
    which, columns, distance_ref, share_ref, keep_ref, gain_ref, phase_ref, high_ref, low_ref,
    held_ref, moved_ref, own_ref, other_ref, after_ref, mine_ref, send_ref,
    stack_ref, back_ref, pair_ref,
):
    _, count, levels, _ = held_ref.shape
    rows = rows_of(which, share_ref.shape[0])
    number = len(rows)
    piece = columns * PAIR // HALF
    padded = stack_ref.shape[1]
    modes = gain_ref.shape[3]
    group = levels * 2 * (HALF + 1)
    core = lax.rem(lax.axis_index("lon"), PAIR)
    cap = is_cap(lax.axis_index("lat"))
    for j, row in enumerate(rows):
        distance, share = distance_ref[row].astype(jnp.int32), share_ref[row]
        for n in range(j, count, number):
            tiles = [other_ref[n, :, 2 * MODES :], held_ref[0, n, :, :LANES]]
            (moved_ref[n, 0, :, :LANES],) = displaced(tiles, distance, share)

    @pl.when(jnp.logical_not(cap))
    def _():
        for n in range(count):
            i, j = divmod(n, number)
            mine_ref[i, j] = moved_ref[n, core, :, :columns]
            send_ref[i, j] = moved_ref[n, 1 - core, :, :columns]

    @pl.when(cap)
    def _():
        for n in range(count):
            row = rows[n % number]
            for r in range(HALF + 1):
                slot = r % HALF
                ours, theirs = (
                    [ref[n, :, (2 * slot + part) * modes : (2 * slot + part + 1) * modes] for part in range(2)]
                    for ref in (own_ref, other_ref)
                )
                if r % 2:
                    re, im = ours[0] - theirs[0], ours[1] - theirs[1]
                else:
                    re, im = ours[0] + theirs[0], ours[1] + theirs[1]
                if r == HALF:
                    re, im = pltpu.roll(re, modes // 2, 1), pltpu.roll(im, modes // 2, 1)
                g_re, g_im = gain_ref[row, 2 * r], gain_ref[row, 2 * r + 1]
                re, im = re * g_re - im * g_im, re * g_im + im * g_re
                base = n * group + 2 * r * levels
                back_ref[base : base + levels, :modes] = re
                back_ref[base : base + levels, modes:] = -im
                back_ref[base + levels : base + 2 * levels, :modes] = im
                back_ref[base + levels : base + 2 * levels, modes:] = re
        stack_ref[...] = product(back_ref[...], high_ref[...], low_ref[...], 1)
        for n in range(count):
            i, j = divmod(n, number)
            keep = keep_ref[rows[j]]
            for tile in range(0, padded, LANES):
                lanes = slice(tile, tile + LANES)
                spectrum = []
                for r in range(HALF + 1):
                    base = n * group + 2 * r * levels
                    re = stack_ref[base : base + levels, lanes]
                    im = stack_ref[base + levels : base + 2 * levels, lanes]
                    if r > 0:
                        c, s = phase_ref[2 * r : 2 * r + 1, lanes], phase_ref[2 * r + 1 : 2 * r + 2, lanes]
                        re, im = re * c - im * s, re * s + im * c
                    spectrum.append((re, im))
                width = min(LANES, piece - tile)
                for u, value in enumerate(half_inverse(spectrum)):
                    pos, start = divmod(u * piece, columns)
                    start += tile
                    shifted = moved_ref[n, pos, :, start : start + LANES]
                    result = keep * shifted + (1.0 - keep) * value
                    pair_ref[pos, n, :, start : start + width] = result[:, :width]
        for n in range(count):
            i, j = divmod(n, number)
            mine_ref[i, j] = pair_ref[core, n, :, :columns]
            send_ref[i, j] = pair_ref[1 - core, n, :, :columns]


def end_kernel(*refs):
    *refs, out_hbm, out_ref, sems = refs
    tracer_count, levels, row_count, columns = out_ref.shape
    share = tracer_count // PAIR
    core = lax.rem(lax.axis_index("lon"), PAIR)
    north = near_is_north()
    copies = []
    for place, (inner, near, far) in enumerate([refs[:3], refs[3:]]):
        for i in range(share):
            slot = place * share + i
            for lanes in spans(columns, 4 * LANES):
                a, b = near[i, 0, :, lanes], far[i, 0, :, lanes]
                out_ref[slot, :, 0, lanes] = jnp.where(north, b, a)
                out_ref[slot, :, row_count - 1, lanes] = jnp.where(north, a, b)
                for j in range(1, row_count - 1):
                    out_ref[slot, :, j, lanes] = inner[i, j - 1, :, lanes]
            t = lax.rem(core + place, PAIR) * share + i
            copies.append(pltpu.make_async_copy(out_ref.at[slot], out_hbm.at[t], sems.at[slot]))
            copies[-1].start()
    for copy in copies:
        copy.wait()


def filter_tables(lon_cells):
    piece = lon_cells // RADIX
    padded = -(-piece // LANES) * LANES
    modes = 2 * MODES // RADIX
    q = np.arange(modes) - modes // 2
    angle = 2 * np.pi * (np.arange(piece)[:, None] * q[None, :] % piece) / piece
    table = np.zeros((padded, 2 * modes))
    table[:piece, :modes] = np.cos(angle)
    table[:piece, modes:] = np.sin(angle)
    high = table.astype(jnp.bfloat16)
    low = (table - high.astype(np.float64)).astype(jnp.bfloat16)
    r = np.arange(HALF + 1)[:, None]

    def waves(steps):
        angle = 2 * np.pi * steps / lon_cells
        pairs = np.stack([np.cos(angle), np.sin(angle)], axis=1)
        return pairs.reshape(-1, steps.shape[1]).astype(np.float32)

    phase = waves(r * np.arange(padded)[None, :])
    wave = waves(RADIX * q[None, :] + r)
    return phase, wave, high, low


SMALL, WHOLE, UNREAD = pltpu.SMEM, pltpu.VMEM, pl.ANY


def call(kernel, outs, operands, scratch=(), sems=0, place=None):
    return pl.pallas_call(
        kernel,
        out_shape=[jax.ShapeDtypeStruct(shape, jnp.float32) for shape in outs],
        in_specs=[pl.BlockSpec(memory_space=place) for _, place in operands],
        out_specs=[pl.BlockSpec(memory_space=place or WHOLE)] * len(outs),
        scratch_shapes=[pltpu.VMEM(shape, jnp.float32) for shape in scratch]
        + ([pltpu.SemaphoreType.DMA((sems,))] if sems else []),
        compiler_params=pltpu.CompilerParams(vmem_limit_bytes=24 << 20),
        cost_estimate=pl.CostEstimate(flops=1, bytes_accessed=1, transcendentals=0),
    )(*[v for v, _ in operands])


def whole(*values):
    return [(v, WHOLE) for v in values]


def body(tracers, merid_courant, zonal_shift, zonal_fraction, cutoff, damping):
    tracer_count, level_count, row_count, column_count = tracers.shape
    lat_count = lax.axis_size("lat")
    lon_count = lax.axis_size("lon")
    assert lon_count == PAIR * PAIR and tracer_count % PAIR == 0 and row_count > 2
    share = tracer_count // PAIR
    lon_cells = column_count * lon_count
    phase, wave, high, low = [jnp.asarray(t) for t in filter_tables(lon_cells)]
    padded, double = high.shape
    width = -(-column_count // LANES) * LANES
    assert column_count - lon_cells // RADIX + padded <= width
    group = level_count * 2 * (HALF + 1)
    shift_rows, fraction_rows = zonal_shift.T, zonal_fraction.T

    def swap_core(value):
        return lax.ppermute(value, "lon", [(p, p ^ 1) for p in range(lon_count)])

    def swap_half(value):
        return lax.ppermute(value, "lon", [(p, p ^ 2) for p in range(lon_count)])

    def swap_band(value, first):
        pairs = []
        for b in range(first, lat_count - 1, 2):
            pairs += [(b, b + 1), (b + 1, b)]
        return lax.ppermute(value, "lat", pairs)

    def set_shape(number):
        return (share, number, level_count, column_count)

    def forward(mine, theirs, after):
        count = mine.shape[0] * mine.shape[1]
        return call(
            forward_kernel,
            [(count, level_count, 2 * MODES + LANES), (PAIR, count, level_count, width)],
            whole(mine, theirs, phase, high, low) + [(after, UNREAD)],
            [(count * group, padded)],
        )

    def shifted(which, held, after):
        count = held.shape[1]
        return call(
            functools.partial(shift_kernel, which, column_count),
            [(count, PAIR, level_count, width)],
            whole(distance, fraction, held) + [(after, UNREAD)],
        )

    def inverse(which, held, moved, own, other, after):
        count = held.shape[1]
        return call(
            functools.partial(inverse_kernel, which, column_count),
            [set_shape(count // share)] * 2,
            whole(distance, fraction, keep, gain, phase, high, low, held, moved, own, other)
            + [(after, UNREAD)],
            [(count * group, padded), (count * group, double), (PAIR, count, level_count, width)],
        )

    edge_shape = ((tracer_count + 1) * level_count, column_count)
    part_shape = (tracer_count, level_count, column_count)
    inner_mine, inner_send, near_edge, far_edge, near_part, far_part = call(
        begin_kernel,
        [set_shape(row_count - 2)] * 2 + [edge_shape] * 2 + [part_shape] * 2,
        [(pltpu.with_memory_space_constraint(v, pltpu.HBM), pltpu.HBM) for v in (tracers, merid_courant)],
        [tracers.shape, merid_courant.shape],
        tracer_count + 1,
    )
    inner_theirs = swap_core(inner_send)
    far_got = swap_band(far_edge, 1)
    inner_own, inner_held = forward(inner_mine, inner_theirs, near_part)
    inner_other = swap_half(inner_own)
    row_shape = (row_count, level_count, LANES)
    distance, fraction, keep, gain = call(
        functools.partial(row_kernel, column_count),
        [row_shape] * 3 + [(row_count, 2 * (HALF + 1), level_count, double // 2)],
        [(v, SMALL) for v in (shift_rows, fraction_rows, cutoff, damping)]
        + whole(wave)
        + [(inner_own, UNREAD)],
    )
    (inner_moved,) = shifted("inner", inner_held, inner_own)
    near_got = swap_band(near_edge, 0)

    far_mine, far_send = call(
        functools.partial(edge_kernel, False),
        [set_shape(1)] * 2,
        whole(far_edge, far_got, far_part) + [(inner_moved, UNREAD)],
    )
    far_theirs = swap_core(far_send)
    far_own, far_held = forward(far_mine, far_theirs, inner_moved)
    far_other = swap_half(far_own)
    (far_moved,) = shifted("far", far_held, far_own)
    inner = inverse("inner", inner_held, inner_moved, inner_own, inner_other, far_moved)
    inner_back = swap_core(inner[1])

    near_mine, near_send = call(
        functools.partial(edge_kernel, True),
        [set_shape(1)] * 2,
        whole(near_edge, near_got, near_part) + [(inner[0], UNREAD)],
    )
    near_theirs = swap_core(near_send)
    near_own, near_held = forward(near_mine, near_theirs, inner[0])
    near_other = swap_half(near_own)
    (near_moved,) = shifted("near", near_held, near_own)
    far = inverse("far", far_held, far_moved, far_own, far_other, near_moved)
    far_back = swap_core(far[1])
    near = inverse("near", near_held, near_moved, near_own, near_other, far[0])
    near_back = swap_core(near[1])
    (result,) = call(
        end_kernel,
        [tracers.shape],
        whole(inner[0], near[0], far[0], inner_back, near_back, far_back),
        [tracers.shape],
        tracer_count,
        pltpu.HBM,
    )
    return result


def solution(mesh):
    placed = (
        P(None, None, "lat", "lon"),
        P(None, "lat", "lon"),
        P(None, "lat"),
        P(None, "lat"),
        P(),
        P(),
    )
    return jax.shard_map(
        body, mesh=mesh, in_specs=placed, out_specs=P(None, None, "lat", "lon"), check_vma=False
    )
```

```python
import functools
import math

import jax
import jax.numpy as jnp
import numpy as np
from jax import lax
from jax.experimental import pallas as pl
from jax.experimental.pallas import tpu as pltpu
from jax.sharding import PartitionSpec as P

MODES = 1024
SMAX = 64
RADIX = 16
HALF = RADIX // 2
LANES = 128
PAIR = 2


def times_phase(value, numerator, denominator):
    re, im = value
    eighth = (8 * numerator % (8 * denominator)) / denominator
    if eighth == 0:
        return re, im
    if eighth == 2:
        return -im, re
    if eighth == 4:
        return -re, -im
    if eighth == 6:
        return im, -re
    c = math.cos(2 * math.pi * numerator / denominator)
    s = math.sin(2 * math.pi * numerator / denominator)
    if eighth == 7:
        return (re + im) * c, (im - re) * c
    if eighth == 1:
        return (re - im) * c, (re + im) * c
    return re * c - im * s, re * s + im * c


def real_dft(values):
    n = len(values)
    if n == 2:
        return [(values[0] + values[1], None), (values[0] - values[1], None)]
    even, odd = real_dft(values[0::2]), real_dft(values[1::2])
    out = [None] * (n // 2 + 1)
    for r in range(n // 4 + 1):
        (er, ei), (tr, ti) = even[r], odd[r]
        if r == 0:
            out[0] = (er + tr, None)
            out[n // 2] = (er - tr, None)
        elif r == n // 4:
            out[r] = (er, -tr)
        else:
            tr, ti = times_phase((tr, ti), -r, n)
            out[r] = (er + tr, ei + ti)
            out[n // 2 - r] = (er - tr, ti - ei)
    return out


def real_inverse(spectrum):
    n = 2 * (len(spectrum) - 1)
    if n == 2:
        a, b = spectrum[0][0], spectrum[1][0]
        return [a + b, a - b]
    even, odd = [None] * (n // 4 + 1), [None] * (n // 4 + 1)
    for r in range(n // 4 + 1):
        (ar, ai), (br, bi) = spectrum[r], spectrum[n // 2 - r]
        if r == 0:
            even[0] = (ar + br, None)
            odd[0] = (ar - br, None)
        elif r == n // 4:
            even[r] = (ar + ar, None)
            odd[r] = (-(ai + ai), None)
        else:
            even[r] = (ar + br, ai - bi)
            odd[r] = times_phase((ar - br, ai + bi), r, n)
    out = [None] * n
    out[0::2] = real_inverse(even)
    out[1::2] = real_inverse(odd)
    return out


def four(values, sign):
    (ar, ai), (br, bi), (cr, ci), (dr, di) = values
    pr, pi, mr, mi = ar + cr, ai + ci, ar - cr, ai - ci
    qr, qi, nr, ni = br + dr, bi + di, br - dr, bi - di
    if sign > 0:
        nr, ni = -nr, -ni
    return [(pr + qr, pi + qi), (mr + ni, mi - nr), (pr - qr, pi - qi), (mr - ni, mi + nr)]


def half_dft(x):
    out = [None] * 9
    out[0::2] = real_dft(x)
    odd = four([times_phase((x[v], -x[v + 4]), -v, 16) for v in range(4)], -1)
    out[1], out[5] = odd[0], odd[1]
    out[7] = (odd[2][0], -odd[2][1])
    out[3] = (odd[3][0], -odd[3][1])
    return out


def half_inverse(w):
    even = real_inverse(w[0::2])
    odd = four([w[1], w[5], (w[7][0], -w[7][1]), (w[3][0], -w[3][1])], 1)
    odd = [times_phase(value, v, 16) for v, value in enumerate(odd)]
    return [even[v] + odd[v][0] for v in range(4)] + [even[v + 4] - odd[v][1] for v in range(4)]


def split(value):
    high = value.astype(jnp.bfloat16)
    return high, (value - high.astype(jnp.float32)).astype(jnp.bfloat16)


def product(left, table_high, table_low, side):
    high, low = split(left)

    def dot(x, y):
        return lax.dot_general(x, y, (((1,), (side,)), ((), ())), preferred_element_type=jnp.float32)

    return dot(high, table_high) + (dot(high, table_low) + dot(low, table_high))


def spans(columns, width):
    return [slice(start, min(start + width, columns)) for start in range(0, columns, width)]


def is_cap(lat):
    count = lax.axis_size("lat")
    return (lat < count // 4) | (lat >= count - count // 4)


def flux_of(face_speed, south, north):
    return jnp.maximum(face_speed, 0.0) * south + jnp.minimum(face_speed, 0.0) * north


def near_is_north():
    return lax.rem(lax.axis_index("lat"), 2) == 0


def begin_kernel(
    cells_hbm, speed_hbm, mine_ref, send_ref, near_ref, far_ref, near_part_ref, far_part_ref,
    cells_ref, speed_ref, sems,
):
    tracer_count, levels, row_count, columns = cells_ref.shape
    share = tracer_count // PAIR
    core = lax.rem(lax.axis_index("lon"), PAIR)
    north = near_is_north()
    copies = [pltpu.make_async_copy(speed_hbm, speed_ref, sems.at[tracer_count])]
    copies += [
        pltpu.make_async_copy(cells_hbm.at[t], cells_ref.at[t], sems.at[t]) for t in range(tracer_count)
    ]
    for copy in copies:
        copy.start()
    for copy in copies:
        copy.wait()
    for lanes in spans(columns, 2 * LANES):
        speed = [speed_ref[:, j, lanes] for j in range(row_count)]
        near_ref[tracer_count * levels :, lanes] = speed[0]
        far_ref[tracer_count * levels :, lanes] = speed[0]
        for which, out_ref in enumerate([mine_ref, send_ref]):
            for i in range(share):
                t = lax.rem(core + which, PAIR) * share + i
                place = pl.ds(pl.multiple_of(t * levels, levels), levels)
                x = [cells_ref[t, :, j, lanes] for j in range(row_count)]
                flux = [flux_of(speed[j], x[j - 1], x[j]) for j in range(1, row_count)]
                for j in range(1, row_count - 1):
                    out_ref[i, j - 1, :, lanes] = x[j] + flux[j - 1] - flux[j]
                near_ref[place, lanes] = jnp.where(north, x[-1], x[0])
                far_ref[place, lanes] = jnp.where(north, x[0], x[-1])
                south_part, north_part = x[0] - flux[0], x[-1] + flux[-1]
                near_part_ref[t, :, lanes] = jnp.where(north, north_part, south_part)
                far_part_ref[t, :, lanes] = jnp.where(north, south_part, north_part)


def edge_kernel(is_near, own_ref, got_ref, part_ref, after_ref, mine_ref, send_ref):
    tracer_count, levels, columns = part_ref.shape
    share = tracer_count // PAIR
    total = tracer_count * levels
    core = lax.rem(lax.axis_index("lon"), PAIR)
    lat = lax.axis_index("lat")
    north = near_is_north() if is_near else jnp.logical_not(near_is_north())
    wall = jnp.where(north, lat == lax.axis_size("lat") - 1, lat == 0)
    for lanes in spans(columns, 3 * LANES):
        speed = jnp.where(north, got_ref[total:, lanes], own_ref[total:, lanes])
        speed = jnp.where(wall, 0.0, speed)
        for which, out_ref in enumerate([mine_ref, send_ref]):
            for i in range(share):
                t = lax.rem(core + which, PAIR) * share + i
                place = pl.ds(pl.multiple_of(t * levels, levels), levels)
                own, got = own_ref[place, lanes], got_ref[place, lanes]
                flux = flux_of(speed, jnp.where(north, own, got), jnp.where(north, got, own))
                out_ref[i, 0, :, lanes] = part_ref[t, :, lanes] + jnp.where(north, -flux, flux)


def forward_kernel(
    mine_ref, theirs_ref, phase_ref, high_ref, low_ref, after_ref, message_ref, held_ref, stack_ref
):
    share, number, levels, columns = mine_ref.shape
    piece = columns * PAIR // HALF
    padded = stack_ref.shape[1]
    modes = high_ref.shape[1] // 2
    group = levels * 2 * (HALF + 1)
    core = lax.rem(lax.axis_index("lon"), PAIR)
    count = share * number
    for n in range(count):
        i, j = divmod(n, number)
        held_ref[core, n, :, :columns] = mine_ref[i, j]
        held_ref[1 - core, n, :, :columns] = theirs_ref[i, j]
        for pos in range(PAIR):
            held_ref[pos, n, :, columns:] = jnp.zeros((levels, held_ref.shape[3] - columns), jnp.float32)
        message_ref[n, :, 2 * MODES :] = held_ref[PAIR - 1, n, :, columns - LANES : columns]

    @pl.when(is_cap(lax.axis_index("lat")))
    def _():
        for n in range(count):
            for tile in range(0, padded, LANES):
                lanes = slice(tile, tile + LANES)
                x = []
                for u in range(HALF):
                    pos, start = divmod(u * piece, columns)
                    x.append(held_ref[pos, n, :, start + tile : start + tile + LANES])
                for r, (re, im) in enumerate(half_dft(x)):
                    base = n * group + 2 * r * levels
                    if r == 0:
                        im = jnp.zeros_like(re)
                    else:
                        c, s = phase_ref[2 * r : 2 * r + 1, lanes], phase_ref[2 * r + 1 : 2 * r + 2, lanes]
                        if im is None:
                            re, im = re * c, -(re * s)
                        else:
                            re, im = re * c + im * s, im * c - re * s
                    stack_ref[base : base + levels, lanes] = re
                    stack_ref[base + levels : base + 2 * levels, lanes] = im
        coeffs = product(stack_ref[...], high_ref[...], low_ref[...], 0)
        upper = lax.broadcasted_iota(jnp.int32, (levels, modes), 1) >= modes // 2
        for n in range(count):
            first = None
            for r in [0, HALF] + list(range(1, HALF)):
                base = n * group + 2 * r * levels
                re, im = coeffs[base : base + levels], coeffs[base + levels : base + 2 * levels]
                x_re = re[:, :modes] + im[:, modes:]
                x_im = im[:, :modes] - re[:, modes:]
                if r == 0:
                    first = x_re, x_im
                    continue
                slot = r
                if r == HALF:
                    x_re = jnp.where(upper, first[0], pltpu.roll(x_re, modes // 2, 1))
                    x_im = jnp.where(upper, first[1], pltpu.roll(x_im, modes // 2, 1))
                    slot = 0
                message_ref[n, :, 2 * slot * modes : (2 * slot + 1) * modes] = x_re
                message_ref[n, :, (2 * slot + 1) * modes : (2 * slot + 2) * modes] = x_im


def row_vector(ref, row, levels):
    level = lax.broadcasted_iota(jnp.int32, (levels, LANES), 0)
    out = jnp.full((levels, LANES), ref[row, 0])
    for i in range(1, levels):
        out = jnp.where(level == i, ref[row, i], out)
    return out


def displaced(tiles, distance, share):
    lane = lax.broadcasted_iota(jnp.int32, distance.shape, 1)

    def moved(steps):
        index = (lane - steps) & (LANES - 1)
        turned = [jnp.take_along_axis(v, index, axis=1, mode="promise_in_bounds") for v in tiles]
        from_left = lane < steps
        return [jnp.where(from_left, a, b) for a, b in zip(turned, turned[1:])]

    pairs = zip(moved(distance), moved(distance + 1))
    return [(1.0 - share) * here + share * earlier for here, earlier in pairs]


def rows_of(which, row_count):
    if which == "inner":
        return list(range(1, row_count - 1))
    north = near_is_north() if which == "near" else jnp.logical_not(near_is_north())
    return [jnp.where(north, row_count - 1, 0)]


def wave_angle(steps, lon_cells):
    steps = lax.rem(steps, lon_cells)
    return steps.astype(jnp.float32) * (2.0 * math.pi / lon_cells)


def row_kernel(
    columns, shift_ref, fraction_ref, cutoff_ref, damping_ref, wave_ref, after_ref,
    distance_ref, share_ref, keep_ref, gain_ref,
):
    row_count, levels = shift_ref.shape
    lon_cells = columns * PAIR * PAIR
    modes = gain_ref.shape[3]
    lat = lax.axis_index("lat")
    for row in range(row_count):
        distance_ref[row] = row_vector(shift_ref, row, levels).astype(jnp.float32)
        share_ref[row] = row_vector(fraction_ref, row, levels)
        keep_ref[row] = jnp.full((levels, LANES), damping_ref[lat * row_count + row])

    @pl.when(is_cap(lat))
    def _():
        lane = lax.broadcasted_iota(jnp.int32, (levels, modes), 1)
        mode = lane - modes // 2
        for row in range(row_count):
            distance = distance_ref[row].astype(jnp.int32)
            share = share_ref[row]
            limit = cutoff_ref[lat * row_count + row]
            wide = wave_angle(RADIX * mode * distance, lon_cells)
            wide_re, wide_im = jnp.cos(wide), -jnp.sin(wide)
            fine = wave_angle(lane * distance, lon_cells)
            fine_re, fine_im = jnp.cos(fine), -jnp.sin(fine)
            for r in range(HALF + 1):
                wavenumber = RADIX * mode + r
                kept = jnp.abs(wavenumber) <= limit
                if r in (0, HALF):
                    kept = kept & (wavenumber >= 0)
                once = r % 2 == 0 and r not in (0, HALF)
                weight = jnp.full((levels, modes), (1.0 if once else 2.0) / lon_cells)
                if r == 0:
                    weight = jnp.where(wavenumber == 0, 1.0 / lon_cells, weight)
                weight = jnp.where(kept, weight, 0.0)
                mix_re = (1.0 - share) + share * wave_ref[2 * r : 2 * r + 1]
                mix_im = -share * wave_ref[2 * r + 1 : 2 * r + 2]
                turn_re, turn_im = fine_re[:, r : r + 1], fine_im[:, r : r + 1]
                re, im = wide_re * turn_re - wide_im * turn_im, wide_re * turn_im + wide_im * turn_re
                gain_ref[row, 2 * r] = (re * mix_re - im * mix_im) * weight
                gain_ref[row, 2 * r + 1] = (re * mix_im + im * mix_re) * weight


def shift_kernel(which, columns, distance_ref, share_ref, held_ref, after_ref, moved_ref):
    _, count, levels, padded = held_ref.shape
    rows = rows_of(which, share_ref.shape[0])
    number = len(rows)
    for j, row in enumerate(rows):
        distance, share = distance_ref[row].astype(jnp.int32), share_ref[row]
        for n in range(j, count, number):
            for pos in range(PAIR):
                tiles = [held_ref[PAIR - 1 - pos, n, :, columns - LANES : columns]]
                tiles += [held_ref[pos, n, :, lanes] for lanes in spans(padded, LANES)]
                for lanes, tile in zip(spans(padded, LANES), displaced(tiles, distance, share)):
                    moved_ref[n, pos, :, lanes] = tile


def inverse_kernel(
    which, columns, distance_ref, share_ref, keep_ref, gain_ref, phase_ref, high_ref, low_ref,
    held_ref, moved_ref, own_ref, other_ref, after_ref, mine_ref, send_ref,
    stack_ref, back_ref, pair_ref,
):
    _, count, levels, _ = held_ref.shape
    rows = rows_of(which, share_ref.shape[0])
    number = len(rows)
    piece = columns * PAIR // HALF
    padded = stack_ref.shape[1]
    modes = gain_ref.shape[3]
    group = levels * 2 * (HALF + 1)
    core = lax.rem(lax.axis_index("lon"), PAIR)
    cap = is_cap(lax.axis_index("lat"))
    for j, row in enumerate(rows):
        distance, share = distance_ref[row].astype(jnp.int32), share_ref[row]
        for n in range(j, count, number):
            tiles = [other_ref[n, :, 2 * MODES :], held_ref[0, n, :, :LANES]]
            (moved_ref[n, 0, :, :LANES],) = displaced(tiles, distance, share)

    @pl.when(jnp.logical_not(cap))
    def _():
        for n in range(count):
            i, j = divmod(n, number)
            mine_ref[i, j] = moved_ref[n, core, :, :columns]
            send_ref[i, j] = moved_ref[n, 1 - core, :, :columns]

    @pl.when(cap)
    def _():
        for n in range(count):
            row = rows[n % number]
            for r in range(HALF + 1):
                slot = r % HALF
                ours, theirs = (
                    [ref[n, :, (2 * slot + part) * modes : (2 * slot + part + 1) * modes] for part in range(2)]
                    for ref in (own_ref, other_ref)
                )
                if r % 2:
                    re, im = ours[0] - theirs[0], ours[1] - theirs[1]
                else:
                    re, im = ours[0] + theirs[0], ours[1] + theirs[1]
                if r == HALF:
                    re, im = pltpu.roll(re, modes // 2, 1), pltpu.roll(im, modes // 2, 1)
                g_re, g_im = gain_ref[row, 2 * r], gain_ref[row, 2 * r + 1]
                re, im = re * g_re - im * g_im, re * g_im + im * g_re
                base = n * group + 2 * r * levels
                back_ref[base : base + levels, :modes] = re
                back_ref[base : base + levels, modes:] = -im
                back_ref[base + levels : base + 2 * levels, :modes] = im
                back_ref[base + levels : base + 2 * levels, modes:] = re
        stack_ref[...] = product(back_ref[...], high_ref[...], low_ref[...], 1)
        for n in range(count):
            i, j = divmod(n, number)
            keep = keep_ref[rows[j]]
            for tile in range(0, padded, LANES):
                lanes = slice(tile, tile + LANES)
                spectrum = []
                for r in range(HALF + 1):
                    base = n * group + 2 * r * levels
                    re = stack_ref[base : base + levels, lanes]
                    im = stack_ref[base + levels : base + 2 * levels, lanes]
                    if r > 0:
                        c, s = phase_ref[2 * r : 2 * r + 1, lanes], phase_ref[2 * r + 1 : 2 * r + 2, lanes]
                        re, im = re * c - im * s, re * s + im * c
                    spectrum.append((re, im))
                width = min(LANES, piece - tile)
                for u, value in enumerate(half_inverse(spectrum)):
                    pos, start = divmod(u * piece, columns)
                    start += tile
                    shifted = moved_ref[n, pos, :, start : start + LANES]
                    result = keep * shifted + (1.0 - keep) * value
                    pair_ref[pos, n, :, start : start + width] = result[:, :width]
        for n in range(count):
            i, j = divmod(n, number)
            mine_ref[i, j] = pair_ref[core, n, :, :columns]
            send_ref[i, j] = pair_ref[1 - core, n, :, :columns]


def end_kernel(*refs):
    *refs, out_hbm, out_ref, sems = refs
    tracer_count, levels, row_count, columns = out_ref.shape
    share = tracer_count // PAIR
    core = lax.rem(lax.axis_index("lon"), PAIR)
    north = near_is_north()
    copies = []
    for place, (inner, near, far) in enumerate([refs[:3], refs[3:]]):
        for i in range(share):
            slot = place * share + i
            for lanes in spans(columns, 4 * LANES):
                a, b = near[i, 0, :, lanes], far[i, 0, :, lanes]
                out_ref[slot, :, 0, lanes] = jnp.where(north, b, a)
                out_ref[slot, :, row_count - 1, lanes] = jnp.where(north, a, b)
                for j in range(1, row_count - 1):
                    out_ref[slot, :, j, lanes] = inner[i, j - 1, :, lanes]
            t = lax.rem(core + place, PAIR) * share + i
            copies.append(pltpu.make_async_copy(out_ref.at[slot], out_hbm.at[t], sems.at[slot]))
            copies[-1].start()
    for copy in copies:
        copy.wait()


def filter_tables(lon_cells):
    piece = lon_cells // RADIX
    padded = -(-piece // LANES) * LANES
    modes = 2 * MODES // RADIX
    q = np.arange(modes) - modes // 2
    angle = 2 * np.pi * (np.arange(piece)[:, None] * q[None, :] % piece) / piece
    table = np.zeros((padded, 2 * modes))
    table[:piece, :modes] = np.cos(angle)
    table[:piece, modes:] = np.sin(angle)
    high = table.astype(jnp.bfloat16)
    low = (table - high.astype(np.float64)).astype(jnp.bfloat16)
    r = np.arange(HALF + 1)[:, None]

    def waves(steps):
        angle = 2 * np.pi * steps / lon_cells
        pairs = np.stack([np.cos(angle), np.sin(angle)], axis=1)
        return pairs.reshape(-1, steps.shape[1]).astype(np.float32)

    phase = waves(r * np.arange(padded)[None, :])
    wave = waves(RADIX * q[None, :] + r)
    return phase, wave, high, low


SMALL, WHOLE, UNREAD = pltpu.SMEM, pltpu.VMEM, pl.ANY


def call(kernel, outs, operands, scratch=(), sems=0, place=None):
    return pl.pallas_call(
        kernel,
        out_shape=[jax.ShapeDtypeStruct(shape, jnp.float32) for shape in outs],
        in_specs=[pl.BlockSpec(memory_space=place) for _, place in operands],
        out_specs=[pl.BlockSpec(memory_space=place or WHOLE)] * len(outs),
        scratch_shapes=[pltpu.VMEM(shape, jnp.float32) for shape in scratch]
        + ([pltpu.SemaphoreType.DMA((sems,))] if sems else []),
        compiler_params=pltpu.CompilerParams(vmem_limit_bytes=24 << 20),
        cost_estimate=pl.CostEstimate(flops=1, bytes_accessed=1, transcendentals=0),
    )(*[v for v, _ in operands])


def whole(*values):
    return [(v, WHOLE) for v in values]


def body(tracers, merid_courant, zonal_shift, zonal_fraction, cutoff, damping):
    tracer_count, level_count, row_count, column_count = tracers.shape
    lat_count = lax.axis_size("lat")
    lon_count = lax.axis_size("lon")
    assert lon_count == PAIR * PAIR and tracer_count % PAIR == 0 and row_count > 2
    share = tracer_count // PAIR
    lon_cells = column_count * lon_count
    phase, wave, high, low = [jnp.asarray(t) for t in filter_tables(lon_cells)]
    padded, double = high.shape
    width = -(-column_count // LANES) * LANES
    assert column_count - lon_cells // RADIX + padded <= width
    group = level_count * 2 * (HALF + 1)
    shift_rows, fraction_rows = zonal_shift.T, zonal_fraction.T

    def swap_core(value):
        return lax.ppermute(value, "lon", [(p, p ^ 1) for p in range(lon_count)])

    def swap_half(value):
        return lax.ppermute(value, "lon", [(p, p ^ 2) for p in range(lon_count)])

    def swap_band(value, first):
        pairs = []
        for b in range(first, lat_count - 1, 2):
            pairs += [(b, b + 1), (b + 1, b)]
        return lax.ppermute(value, "lat", pairs)

    def set_shape(number):
        return (share, number, level_count, column_count)

    def forward(mine, theirs, after):
        count = mine.shape[0] * mine.shape[1]
        return call(
            forward_kernel,
            [(count, level_count, 2 * MODES + LANES), (PAIR, count, level_count, width)],
            whole(mine, theirs, phase, high, low) + [(after, UNREAD)],
            [(count * group, padded)],
        )

    def shifted(which, held, after):
        count = held.shape[1]
        return call(
            functools.partial(shift_kernel, which, column_count),
            [(count, PAIR, level_count, width)],
            whole(distance, fraction, held) + [(after, UNREAD)],
        )

    def inverse(which, held, moved, own, other, after):
        count = held.shape[1]
        return call(
            functools.partial(inverse_kernel, which, column_count),
            [set_shape(count // share)] * 2,
            whole(distance, fraction, keep, gain, phase, high, low, held, moved, own, other)
            + [(after, UNREAD)],
            [(count * group, padded), (count * group, double), (PAIR, count, level_count, width)],
        )

    edge_shape = ((tracer_count + 1) * level_count, column_count)
    part_shape = (tracer_count, level_count, column_count)
    inner_mine, inner_send, near_edge, far_edge, near_part, far_part = call(
        begin_kernel,
        [set_shape(row_count - 2)] * 2 + [edge_shape] * 2 + [part_shape] * 2,
        [(pltpu.with_memory_space_constraint(v, pltpu.HBM), pltpu.HBM) for v in (tracers, merid_courant)],
        [tracers.shape, merid_courant.shape],
        tracer_count + 1,
    )
    inner_theirs = swap_core(inner_send)
    far_got = swap_band(far_edge, 1)
    inner_own, inner_held = forward(inner_mine, inner_theirs, near_part)
    inner_other = swap_half(inner_own)
    row_shape = (row_count, level_count, LANES)
    distance, fraction, keep, gain = call(
        functools.partial(row_kernel, column_count),
        [row_shape] * 3 + [(row_count, 2 * (HALF + 1), level_count, double // 2)],
        [(v, SMALL) for v in (shift_rows, fraction_rows, cutoff, damping)]
        + whole(wave)
        + [(inner_own, UNREAD)],
    )
    (inner_moved,) = shifted("inner", inner_held, inner_own)
    near_got = swap_band(near_edge, 0)

    far_mine, far_send = call(
        functools.partial(edge_kernel, False),
        [set_shape(1)] * 2,
        whole(far_edge, far_got, far_part) + [(inner_moved, UNREAD)],
    )
    far_theirs = swap_core(far_send)
    far_own, far_held = forward(far_mine, far_theirs, inner_moved)
    far_other = swap_half(far_own)
    (far_moved,) = shifted("far", far_held, far_own)
    inner = inverse("inner", inner_held, inner_moved, inner_own, inner_other, far_moved)
    inner_back = swap_core(inner[1])

    near_mine, near_send = call(
        functools.partial(edge_kernel, True),
        [set_shape(1)] * 2,
        whole(near_edge, near_got, near_part) + [(inner[0], UNREAD)],
    )
    near_theirs = swap_core(near_send)
    far = inverse("far", far_held, far_moved, far_own, far_other, near_mine)
    far_back = swap_core(far[1])
    near_own, near_held = forward(near_mine, near_theirs, far[0])
    near_other = swap_half(near_own)
    (near_moved,) = shifted("near", near_held, near_own)
    near = inverse("near", near_held, near_moved, near_own, near_other, far[0])
    near_back = swap_core(near[1])
    (result,) = call(
        end_kernel,
        [tracers.shape],
        whole(inner[0], near[0], far[0], inner_back, near_back, far_back),
        [tracers.shape],
        tracer_count,
        pltpu.HBM,
    )
    return result


def solution(mesh):
    placed = (
        P(None, None, "lat", "lon"),
        P(None, "lat", "lon"),
        P(None, "lat"),
        P(None, "lat"),
        P(),
        P(),
    )
    return jax.shard_map(
        body, mesh=mesh, in_specs=placed, out_specs=P(None, None, "lat", "lon"), check_vma=False
    )
```

```python
import functools
import math

import jax
import jax.numpy as jnp
import numpy as np
from jax import lax
from jax.experimental import pallas as pl
from jax.experimental.pallas import tpu as pltpu
from jax.sharding import PartitionSpec as P

MODES = 1024
SMAX = 64
RADIX = 16
HALF = RADIX // 2
LANES = 128
PAIR = 2


def times_phase(value, numerator, denominator):
    re, im = value
    eighth = (8 * numerator % (8 * denominator)) / denominator
    if eighth == 0:
        return re, im
    if eighth == 2:
        return -im, re
    if eighth == 4:
        return -re, -im
    if eighth == 6:
        return im, -re
    c = math.cos(2 * math.pi * numerator / denominator)
    s = math.sin(2 * math.pi * numerator / denominator)
    if eighth == 7:
        return (re + im) * c, (im - re) * c
    if eighth == 1:
        return (re - im) * c, (re + im) * c
    return re * c - im * s, re * s + im * c


def real_dft(values):
    n = len(values)
    if n == 2:
        return [(values[0] + values[1], None), (values[0] - values[1], None)]
    even, odd = real_dft(values[0::2]), real_dft(values[1::2])
    out = [None] * (n // 2 + 1)
    for r in range(n // 4 + 1):
        (er, ei), (tr, ti) = even[r], odd[r]
        if r == 0:
            out[0] = (er + tr, None)
            out[n // 2] = (er - tr, None)
        elif r == n // 4:
            out[r] = (er, -tr)
        else:
            tr, ti = times_phase((tr, ti), -r, n)
            out[r] = (er + tr, ei + ti)
            out[n // 2 - r] = (er - tr, ti - ei)
    return out


def real_inverse(spectrum):
    n = 2 * (len(spectrum) - 1)
    if n == 2:
        a, b = spectrum[0][0], spectrum[1][0]
        return [a + b, a - b]
    even, odd = [None] * (n // 4 + 1), [None] * (n // 4 + 1)
    for r in range(n // 4 + 1):
        (ar, ai), (br, bi) = spectrum[r], spectrum[n // 2 - r]
        if r == 0:
            even[0] = (ar + br, None)
            odd[0] = (ar - br, None)
        elif r == n // 4:
            even[r] = (ar + ar, None)
            odd[r] = (-(ai + ai), None)
        else:
            even[r] = (ar + br, ai - bi)
            odd[r] = times_phase((ar - br, ai + bi), r, n)
    out = [None] * n
    out[0::2] = real_inverse(even)
    out[1::2] = real_inverse(odd)
    return out


def four(values, sign):
    (ar, ai), (br, bi), (cr, ci), (dr, di) = values
    pr, pi, mr, mi = ar + cr, ai + ci, ar - cr, ai - ci
    qr, qi, nr, ni = br + dr, bi + di, br - dr, bi - di
    if sign > 0:
        nr, ni = -nr, -ni
    return [(pr + qr, pi + qi), (mr + ni, mi - nr), (pr - qr, pi - qi), (mr - ni, mi + nr)]


def half_dft(x):
    out = [None] * 9
    out[0::2] = real_dft(x)
    odd = four([times_phase((x[v], -x[v + 4]), -v, 16) for v in range(4)], -1)
    out[1], out[5] = odd[0], odd[1]
    out[7] = (odd[2][0], -odd[2][1])
    out[3] = (odd[3][0], -odd[3][1])
    return out


def half_inverse(w):
    even = real_inverse(w[0::2])
    odd = four([w[1], w[5], (w[7][0], -w[7][1]), (w[3][0], -w[3][1])], 1)
    odd = [times_phase(value, v, 16) for v, value in enumerate(odd)]
    return [even[v] + odd[v][0] for v in range(4)] + [even[v + 4] - odd[v][1] for v in range(4)]


def split(value):
    high = value.astype(jnp.bfloat16)
    return high, (value - high.astype(jnp.float32)).astype(jnp.bfloat16)


def product(left, table_high, table_low, side):
    high, low = split(left)

    def dot(x, y):
        return lax.dot_general(x, y, (((1,), (side,)), ((), ())), preferred_element_type=jnp.float32)

    return dot(high, table_high) + (dot(high, table_low) + dot(low, table_high))


def spans(columns, width):
    return [slice(start, min(start + width, columns)) for start in range(0, columns, width)]


def is_cap(lat):
    count = lax.axis_size("lat")
    return (lat < count // 4) | (lat >= count - count // 4)


def flux_of(face_speed, south, north):
    return jnp.maximum(face_speed, 0.0) * south + jnp.minimum(face_speed, 0.0) * north


def near_is_north():
    return lax.rem(lax.axis_index("lat"), 2) == 0


def begin_kernel(
    cells_hbm, speed_hbm, mine_ref, send_ref, near_ref, far_ref, near_part_ref, far_part_ref,
    cells_ref, speed_ref, sems,
):
    tracer_count, levels, row_count, columns = cells_ref.shape
    share = tracer_count // PAIR
    core = lax.rem(lax.axis_index("lon"), PAIR)
    north = near_is_north()
    copies = [pltpu.make_async_copy(speed_hbm, speed_ref, sems.at[tracer_count])]
    copies += [
        pltpu.make_async_copy(cells_hbm.at[t], cells_ref.at[t], sems.at[t]) for t in range(tracer_count)
    ]
    for copy in copies:
        copy.start()
    for copy in copies:
        copy.wait()
    for lanes in spans(columns, 2 * LANES):
        speed = [speed_ref[:, j, lanes] for j in range(row_count)]
        near_ref[tracer_count * levels :, lanes] = speed[0]
        far_ref[tracer_count * levels :, lanes] = speed[0]
        for which, out_ref in enumerate([mine_ref, send_ref]):
            for i in range(share):
                t = lax.rem(core + which, PAIR) * share + i
                place = pl.ds(pl.multiple_of(t * levels, levels), levels)
                x = [cells_ref[t, :, j, lanes] for j in range(row_count)]
                flux = [flux_of(speed[j], x[j - 1], x[j]) for j in range(1, row_count)]
                for j in range(1, row_count - 1):
                    out_ref[i, j - 1, :, lanes] = x[j] + flux[j - 1] - flux[j]
                near_ref[place, lanes] = jnp.where(north, x[-1], x[0])
                far_ref[place, lanes] = jnp.where(north, x[0], x[-1])
                south_part, north_part = x[0] - flux[0], x[-1] + flux[-1]
                near_part_ref[t, :, lanes] = jnp.where(north, north_part, south_part)
                far_part_ref[t, :, lanes] = jnp.where(north, south_part, north_part)


def edge_kernel(is_near, own_ref, got_ref, later_ref, part_ref, after_ref, mine_ref, send_ref):
    tracer_count, levels, columns = part_ref.shape
    share = tracer_count // PAIR
    total = tracer_count * levels
    core = lax.rem(lax.axis_index("lon"), PAIR)
    lat = lax.axis_index("lat")
    north = near_is_north() if is_near else jnp.logical_not(near_is_north())
    wall = jnp.where(north, lat == lax.axis_size("lat") - 1, lat == 0)
    urgent = is_cap(lat) | is_cap(jnp.where(north, lat + 1, lat - 1))

    def got(place, lanes):
        if not is_near:
            return got_ref[place, lanes]
        return jnp.where(urgent, got_ref[place, lanes], later_ref[place, lanes])

    for lanes in spans(columns, 3 * LANES):
        speed = jnp.where(north, got(slice(total, total + levels), lanes), own_ref[total:, lanes])
        speed = jnp.where(wall, 0.0, speed)
        for which, out_ref in enumerate([mine_ref, send_ref]):
            for i in range(share):
                t = lax.rem(core + which, PAIR) * share + i
                place = pl.ds(pl.multiple_of(t * levels, levels), levels)
                own, other = own_ref[place, lanes], got(place, lanes)
                flux = flux_of(speed, jnp.where(north, own, other), jnp.where(north, other, own))
                out_ref[i, 0, :, lanes] = part_ref[t, :, lanes] + jnp.where(north, -flux, flux)


def forward_kernel(
    mine_ref, theirs_ref, phase_ref, high_ref, low_ref, after_ref, message_ref, held_ref, stack_ref
):
    share, number, levels, columns = mine_ref.shape
    piece = columns * PAIR // HALF
    padded = stack_ref.shape[1]
    modes = high_ref.shape[1] // 2
    group = levels * 2 * (HALF + 1)
    core = lax.rem(lax.axis_index("lon"), PAIR)
    count = share * number
    for n in range(count):
        i, j = divmod(n, number)
        held_ref[core, n, :, :columns] = mine_ref[i, j]
        held_ref[1 - core, n, :, :columns] = theirs_ref[i, j]
        for pos in range(PAIR):
            held_ref[pos, n, :, columns:] = jnp.zeros((levels, held_ref.shape[3] - columns), jnp.float32)
        message_ref[n, :, 2 * MODES :] = held_ref[PAIR - 1, n, :, columns - LANES : columns]

    @pl.when(is_cap(lax.axis_index("lat")))
    def _():
        for n in range(count):
            for tile in range(0, padded, LANES):
                lanes = slice(tile, tile + LANES)
                x = []
                for u in range(HALF):
                    pos, start = divmod(u * piece, columns)
                    x.append(held_ref[pos, n, :, start + tile : start + tile + LANES])
                for r, (re, im) in enumerate(half_dft(x)):
                    base = n * group + 2 * r * levels
                    if r == 0:
                        im = jnp.zeros_like(re)
                    else:
                        c, s = phase_ref[2 * r : 2 * r + 1, lanes], phase_ref[2 * r + 1 : 2 * r + 2, lanes]
                        if im is None:
                            re, im = re * c, -(re * s)
                        else:
                            re, im = re * c + im * s, im * c - re * s
                    stack_ref[base : base + levels, lanes] = re
                    stack_ref[base + levels : base + 2 * levels, lanes] = im
        coeffs = product(stack_ref[...], high_ref[...], low_ref[...], 0)
        upper = lax.broadcasted_iota(jnp.int32, (levels, modes), 1) >= modes // 2
        for n in range(count):
            first = None
            for r in [0, HALF] + list(range(1, HALF)):
                base = n * group + 2 * r * levels
                re, im = coeffs[base : base + levels], coeffs[base + levels : base + 2 * levels]
                x_re = re[:, :modes] + im[:, modes:]
                x_im = im[:, :modes] - re[:, modes:]
                if r == 0:
                    first = x_re, x_im
                    continue
                slot = r
                if r == HALF:
                    x_re = jnp.where(upper, first[0], pltpu.roll(x_re, modes // 2, 1))
                    x_im = jnp.where(upper, first[1], pltpu.roll(x_im, modes // 2, 1))
                    slot = 0
                message_ref[n, :, 2 * slot * modes : (2 * slot + 1) * modes] = x_re
                message_ref[n, :, (2 * slot + 1) * modes : (2 * slot + 2) * modes] = x_im


def row_vector(ref, row, levels):
    level = lax.broadcasted_iota(jnp.int32, (levels, LANES), 0)
    out = jnp.full((levels, LANES), ref[row, 0])
    for i in range(1, levels):
        out = jnp.where(level == i, ref[row, i], out)
    return out


def displaced(tiles, distance, share):
    lane = lax.broadcasted_iota(jnp.int32, distance.shape, 1)

    def moved(steps):
        index = (lane - steps) & (LANES - 1)
        turned = [jnp.take_along_axis(v, index, axis=1, mode="promise_in_bounds") for v in tiles]
        from_left = lane < steps
        return [jnp.where(from_left, a, b) for a, b in zip(turned, turned[1:])]

    pairs = zip(moved(distance), moved(distance + 1))
    return [(1.0 - share) * here + share * earlier for here, earlier in pairs]


def rows_of(which, row_count):
    if which == "inner":
        return list(range(1, row_count - 1))
    north = near_is_north() if which == "near" else jnp.logical_not(near_is_north())
    return [jnp.where(north, row_count - 1, 0)]


def wave_angle(steps, lon_cells):
    steps = lax.rem(steps, lon_cells)
    return steps.astype(jnp.float32) * (2.0 * math.pi / lon_cells)


def row_kernel(
    columns, shift_ref, fraction_ref, cutoff_ref, damping_ref, wave_ref, after_ref,
    distance_ref, share_ref, keep_ref, gain_ref,
):
    row_count, levels = shift_ref.shape
    lon_cells = columns * PAIR * PAIR
    modes = gain_ref.shape[3]
    lat = lax.axis_index("lat")
    for row in range(row_count):
        distance_ref[row] = row_vector(shift_ref, row, levels).astype(jnp.float32)
        share_ref[row] = row_vector(fraction_ref, row, levels)
        keep_ref[row] = jnp.full((levels, LANES), damping_ref[lat * row_count + row])

    @pl.when(is_cap(lat))
    def _():
        lane = lax.broadcasted_iota(jnp.int32, (levels, modes), 1)
        mode = lane - modes // 2
        for row in range(row_count):
            distance = distance_ref[row].astype(jnp.int32)
            share = share_ref[row]
            limit = cutoff_ref[lat * row_count + row]
            wide = wave_angle(RADIX * mode * distance, lon_cells)
            wide_re, wide_im = jnp.cos(wide), -jnp.sin(wide)
            fine = wave_angle(lane * distance, lon_cells)
            fine_re, fine_im = jnp.cos(fine), -jnp.sin(fine)
            for r in range(HALF + 1):
                wavenumber = RADIX * mode + r
                kept = jnp.abs(wavenumber) <= limit
                if r in (0, HALF):
                    kept = kept & (wavenumber >= 0)
                once = r % 2 == 0 and r not in (0, HALF)
                weight = jnp.full((levels, modes), (1.0 if once else 2.0) / lon_cells)
                if r == 0:
                    weight = jnp.where(wavenumber == 0, 1.0 / lon_cells, weight)
                weight = jnp.where(kept, weight, 0.0)
                mix_re = (1.0 - share) + share * wave_ref[2 * r : 2 * r + 1]
                mix_im = -share * wave_ref[2 * r + 1 : 2 * r + 2]
                turn_re, turn_im = fine_re[:, r : r + 1], fine_im[:, r : r + 1]
                re, im = wide_re * turn_re - wide_im * turn_im, wide_re * turn_im + wide_im * turn_re
                gain_ref[row, 2 * r] = (re * mix_re - im * mix_im) * weight
                gain_ref[row, 2 * r + 1] = (re * mix_im + im * mix_re) * weight


def shift_kernel(which, columns, distance_ref, share_ref, held_ref, after_ref, *refs):
    relays = len(refs) // 2
    moved_ref = refs[relays]
    for source_ref, relay_ref in zip(refs[:relays], refs[relays + 1 :]):
        relay_ref[...] = source_ref[...]
    _, count, levels, padded = held_ref.shape
    rows = rows_of(which, share_ref.shape[0])
    number = len(rows)
    for j, row in enumerate(rows):
        distance, share = distance_ref[row].astype(jnp.int32), share_ref[row]
        for n in range(j, count, number):
            for pos in range(PAIR):
                tiles = [held_ref[PAIR - 1 - pos, n, :, columns - LANES : columns]]
                tiles += [held_ref[pos, n, :, lanes] for lanes in spans(padded, LANES)]
                for lanes, tile in zip(spans(padded, LANES), displaced(tiles, distance, share)):
                    moved_ref[n, pos, :, lanes] = tile


def inverse_kernel(
    which, columns, distance_ref, share_ref, keep_ref, gain_ref, phase_ref, high_ref, low_ref,
    held_ref, moved_ref, own_ref, other_ref, after_ref, mine_ref, send_ref,
    stack_ref, back_ref, pair_ref,
):
    _, count, levels, _ = held_ref.shape
    rows = rows_of(which, share_ref.shape[0])
    number = len(rows)
    piece = columns * PAIR // HALF
    padded = stack_ref.shape[1]
    modes = gain_ref.shape[3]
    group = levels * 2 * (HALF + 1)
    core = lax.rem(lax.axis_index("lon"), PAIR)
    cap = is_cap(lax.axis_index("lat"))
    for j, row in enumerate(rows):
        distance, share = distance_ref[row].astype(jnp.int32), share_ref[row]
        for n in range(j, count, number):
            tiles = [other_ref[n, :, 2 * MODES :], held_ref[0, n, :, :LANES]]
            (moved_ref[n, 0, :, :LANES],) = displaced(tiles, distance, share)

    @pl.when(jnp.logical_not(cap))
    def _():
        for n in range(count):
            i, j = divmod(n, number)
            mine_ref[i, j] = moved_ref[n, core, :, :columns]
            send_ref[i, j] = moved_ref[n, 1 - core, :, :columns]

    @pl.when(cap)
    def _():
        for n in range(count):
            row = rows[n % number]
            for r in range(HALF + 1):
                slot = r % HALF
                ours, theirs = (
                    [ref[n, :, (2 * slot + part) * modes : (2 * slot + part + 1) * modes] for part in range(2)]
                    for ref in (own_ref, other_ref)
                )
                if r % 2:
                    re, im = ours[0] - theirs[0], ours[1] - theirs[1]
                else:
                    re, im = ours[0] + theirs[0], ours[1] + theirs[1]
                if r == HALF:
                    re, im = pltpu.roll(re, modes // 2, 1), pltpu.roll(im, modes // 2, 1)
                g_re, g_im = gain_ref[row, 2 * r], gain_ref[row, 2 * r + 1]
                re, im = re * g_re - im * g_im, re * g_im + im * g_re
                base = n * group + 2 * r * levels
                back_ref[base : base + levels, :modes] = re
                back_ref[base : base + levels, modes:] = -im
                back_ref[base + levels : base + 2 * levels, :modes] = im
                back_ref[base + levels : base + 2 * levels, modes:] = re
        stack_ref[...] = product(back_ref[...], high_ref[...], low_ref[...], 1)
        for n in range(count):
            i, j = divmod(n, number)
            keep = keep_ref[rows[j]]
            for tile in range(0, padded, LANES):
                lanes = slice(tile, tile + LANES)
                spectrum = []
                for r in range(HALF + 1):
                    base = n * group + 2 * r * levels
                    re = stack_ref[base : base + levels, lanes]
                    im = stack_ref[base + levels : base + 2 * levels, lanes]
                    if r > 0:
                        c, s = phase_ref[2 * r : 2 * r + 1, lanes], phase_ref[2 * r + 1 : 2 * r + 2, lanes]
                        re, im = re * c - im * s, re * s + im * c
                    spectrum.append((re, im))
                width = min(LANES, piece - tile)
                for u, value in enumerate(half_inverse(spectrum)):
                    pos, start = divmod(u * piece, columns)
                    start += tile
                    shifted = moved_ref[n, pos, :, start : start + LANES]
                    result = keep * shifted + (1.0 - keep) * value
                    pair_ref[pos, n, :, start : start + width] = result[:, :width]
        for n in range(count):
            i, j = divmod(n, number)
            mine_ref[i, j] = pair_ref[core, n, :, :columns]
            send_ref[i, j] = pair_ref[1 - core, n, :, :columns]


def end_kernel(*refs):
    *refs, out_hbm, out_ref, sems = refs
    tracer_count, levels, row_count, columns = out_ref.shape
    share = tracer_count // PAIR
    core = lax.rem(lax.axis_index("lon"), PAIR)
    north = near_is_north()
    copies = []
    for place, (inner, near, far) in enumerate([refs[:3], refs[3:]]):
        for i in range(share):
            slot = place * share + i
            for lanes in spans(columns, 4 * LANES):
                a, b = near[i, 0, :, lanes], far[i, 0, :, lanes]
                out_ref[slot, :, 0, lanes] = jnp.where(north, b, a)
                out_ref[slot, :, row_count - 1, lanes] = jnp.where(north, a, b)
                for j in range(1, row_count - 1):
                    out_ref[slot, :, j, lanes] = inner[i, j - 1, :, lanes]
            t = lax.rem(core + place, PAIR) * share + i
            copies.append(pltpu.make_async_copy(out_ref.at[slot], out_hbm.at[t], sems.at[slot]))
            copies[-1].start()
    for copy in copies:
        copy.wait()


def filter_tables(lon_cells):
    piece = lon_cells // RADIX
    padded = -(-piece // LANES) * LANES
    modes = 2 * MODES // RADIX
    q = np.arange(modes) - modes // 2
    angle = 2 * np.pi * (np.arange(piece)[:, None] * q[None, :] % piece) / piece
    table = np.zeros((padded, 2 * modes))
    table[:piece, :modes] = np.cos(angle)
    table[:piece, modes:] = np.sin(angle)
    high = table.astype(jnp.bfloat16)
    low = (table - high.astype(np.float64)).astype(jnp.bfloat16)
    r = np.arange(HALF + 1)[:, None]

    def waves(steps):
        angle = 2 * np.pi * steps / lon_cells
        pairs = np.stack([np.cos(angle), np.sin(angle)], axis=1)
        return pairs.reshape(-1, steps.shape[1]).astype(np.float32)

    phase = waves(r * np.arange(padded)[None, :])
    wave = waves(RADIX * q[None, :] + r)
    return phase, wave, high, low


SMALL, WHOLE, UNREAD = pltpu.SMEM, pltpu.VMEM, pl.ANY


def call(kernel, outs, operands, scratch=(), sems=0, place=None):
    return pl.pallas_call(
        kernel,
        out_shape=[jax.ShapeDtypeStruct(shape, jnp.float32) for shape in outs],
        in_specs=[pl.BlockSpec(memory_space=place) for _, place in operands],
        out_specs=[pl.BlockSpec(memory_space=place or WHOLE)] * len(outs),
        scratch_shapes=[pltpu.VMEM(shape, jnp.float32) for shape in scratch]
        + ([pltpu.SemaphoreType.DMA((sems,))] if sems else []),
        compiler_params=pltpu.CompilerParams(vmem_limit_bytes=24 << 20),
        cost_estimate=pl.CostEstimate(flops=1, bytes_accessed=1, transcendentals=0),
    )(*[v for v, _ in operands])


def whole(*values):
    return [(v, WHOLE) for v in values]


def body(tracers, merid_courant, zonal_shift, zonal_fraction, cutoff, damping):
    tracer_count, level_count, row_count, column_count = tracers.shape
    lat_count = lax.axis_size("lat")
    lon_count = lax.axis_size("lon")
    assert lon_count == PAIR * PAIR and tracer_count % PAIR == 0 and row_count > 2
    share = tracer_count // PAIR
    lon_cells = column_count * lon_count
    phase, wave, high, low = [jnp.asarray(t) for t in filter_tables(lon_cells)]
    padded, double = high.shape
    width = -(-column_count // LANES) * LANES
    assert column_count - lon_cells // RADIX + padded <= width
    group = level_count * 2 * (HALF + 1)
    shift_rows, fraction_rows = zonal_shift.T, zonal_fraction.T

    def swap_core(value):
        return lax.ppermute(value, "lon", [(p, p ^ 1) for p in range(lon_count)])

    def swap_half(value):
        return lax.ppermute(value, "lon", [(p, p ^ 2) for p in range(lon_count)])

    caps = [b for b in range(lat_count) if b < lat_count // 4 or b >= lat_count - lat_count // 4]

    def swap_band(value, first, urgent=None):
        pairs = []
        for b in range(first, lat_count - 1, 2):
            if urgent is None or (b in caps or b + 1 in caps) == urgent:
                pairs += [(b, b + 1), (b + 1, b)]
        return lax.ppermute(value, "lat", pairs)

    def set_shape(number):
        return (share, number, level_count, column_count)

    def forward(mine, theirs, after):
        count = mine.shape[0] * mine.shape[1]
        return call(
            forward_kernel,
            [(count, level_count, 2 * MODES + LANES), (PAIR, count, level_count, width)],
            whole(mine, theirs, phase, high, low) + [(after, UNREAD)],
            [(count * group, padded)],
        )

    def shifted(which, held, after, *relay):
        count = held.shape[1]
        return call(
            functools.partial(shift_kernel, which, column_count),
            [(count, PAIR, level_count, width)] + [v.shape for v in relay],
            whole(distance, fraction, held) + [(after, UNREAD)] + whole(*relay),
        )

    def inverse(which, held, moved, own, other, after):
        count = held.shape[1]
        return call(
            functools.partial(inverse_kernel, which, column_count),
            [set_shape(count // share)] * 2,
            whole(distance, fraction, keep, gain, phase, high, low, held, moved, own, other)
            + [(after, UNREAD)],
            [(count * group, padded), (count * group, double), (PAIR, count, level_count, width)],
        )

    edge_shape = ((tracer_count + 1) * level_count, column_count)
    part_shape = (tracer_count, level_count, column_count)
    inner_mine, inner_send, near_edge, far_edge, near_part, far_part = call(
        begin_kernel,
        [set_shape(row_count - 2)] * 2 + [edge_shape] * 2 + [part_shape] * 2,
        [(pltpu.with_memory_space_constraint(v, pltpu.HBM), pltpu.HBM) for v in (tracers, merid_courant)],
        [tracers.shape, merid_courant.shape],
        tracer_count + 1,
    )
    inner_theirs = swap_core(inner_send)
    far_got = swap_band(far_edge, 1)
    inner_own, inner_held = forward(inner_mine, inner_theirs, near_part)
    inner_other = swap_half(inner_own)
    row_shape = (row_count, level_count, LANES)
    distance, fraction, keep, gain = call(
        functools.partial(row_kernel, column_count),
        [row_shape] * 3 + [(row_count, 2 * (HALF + 1), level_count, double // 2)],
        [(v, SMALL) for v in (shift_rows, fraction_rows, cutoff, damping)]
        + whole(wave)
        + [(inner_own, UNREAD)],
    )
    near_got = swap_band(near_edge, 0, True)
    inner_moved, near_relay = shifted("inner", inner_held, inner_own, near_edge)
    near_later = swap_band(near_relay, 0, False)

    far_mine, far_send = call(
        functools.partial(edge_kernel, False),
        [set_shape(1)] * 2,
        whole(far_edge, far_got) + [(far_edge, UNREAD)] + whole(far_part) + [(inner_moved, UNREAD)],
    )
    far_theirs = swap_core(far_send)
    far_own, far_held = forward(far_mine, far_theirs, inner_moved)
    far_other = swap_half(far_own)
    (far_moved,) = shifted("far", far_held, far_own)
    inner = inverse("inner", inner_held, inner_moved, inner_own, inner_other, far_moved)
    inner_back = swap_core(inner[1])

    near_mine, near_send = call(
        functools.partial(edge_kernel, True),
        [set_shape(1)] * 2,
        whole(near_edge, near_got, near_later, near_part) + [(inner[0], UNREAD)],
    )
    near_theirs = swap_core(near_send)
    near_own, near_held = forward(near_mine, near_theirs, inner[0])
    near_other = swap_half(near_own)
    (near_moved,) = shifted("near", near_held, near_own)
    far = inverse("far", far_held, far_moved, far_own, far_other, near_moved)
    far_back = swap_core(far[1])
    near = inverse("near", near_held, near_moved, near_own, near_other, far[0])
    near_back = swap_core(near[1])
    (result,) = call(
        end_kernel,
        [tracers.shape],
        whole(inner[0], near[0], far[0], inner_back, near_back, far_back),
        [tracers.shape],
        tracer_count,
        pltpu.HBM,
    )
    return result


def solution(mesh):
    placed = (
        P(None, None, "lat", "lon"),
        P(None, "lat", "lon"),
        P(None, "lat"),
        P(None, "lat"),
        P(),
        P(),
    )
    return jax.shard_map(
        body, mesh=mesh, in_specs=placed, out_specs=P(None, None, "lat", "lon"), check_vma=False
    )
```

```python
import functools
import math

import jax
import jax.numpy as jnp
import numpy as np
from jax import lax
from jax.experimental import pallas as pl
from jax.experimental.pallas import tpu as pltpu
from jax.sharding import PartitionSpec as P

MODES = 1024
SMAX = 64
RADIX = 16
HALF = RADIX // 2
LANES = 128
PAIR = 2


def times_phase(value, numerator, denominator):
    re, im = value
    eighth = (8 * numerator % (8 * denominator)) / denominator
    if eighth == 0:
        return re, im
    if eighth == 2:
        return -im, re
    if eighth == 4:
        return -re, -im
    if eighth == 6:
        return im, -re
    c = math.cos(2 * math.pi * numerator / denominator)
    s = math.sin(2 * math.pi * numerator / denominator)
    if eighth == 7:
        return (re + im) * c, (im - re) * c
    if eighth == 1:
        return (re - im) * c, (re + im) * c
    return re * c - im * s, re * s + im * c


def real_dft(values):
    n = len(values)
    if n == 2:
        return [(values[0] + values[1], None), (values[0] - values[1], None)]
    even, odd = real_dft(values[0::2]), real_dft(values[1::2])
    out = [None] * (n // 2 + 1)
    for r in range(n // 4 + 1):
        (er, ei), (tr, ti) = even[r], odd[r]
        if r == 0:
            out[0] = (er + tr, None)
            out[n // 2] = (er - tr, None)
        elif r == n // 4:
            out[r] = (er, -tr)
        else:
            tr, ti = times_phase((tr, ti), -r, n)
            out[r] = (er + tr, ei + ti)
            out[n // 2 - r] = (er - tr, ti - ei)
    return out


def real_inverse(spectrum):
    n = 2 * (len(spectrum) - 1)
    if n == 2:
        a, b = spectrum[0][0], spectrum[1][0]
        return [a + b, a - b]
    even, odd = [None] * (n // 4 + 1), [None] * (n // 4 + 1)
    for r in range(n // 4 + 1):
        (ar, ai), (br, bi) = spectrum[r], spectrum[n // 2 - r]
        if r == 0:
            even[0] = (ar + br, None)
            odd[0] = (ar - br, None)
        elif r == n // 4:
            even[r] = (ar + ar, None)
            odd[r] = (-(ai + ai), None)
        else:
            even[r] = (ar + br, ai - bi)
            odd[r] = times_phase((ar - br, ai + bi), r, n)
    out = [None] * n
    out[0::2] = real_inverse(even)
    out[1::2] = real_inverse(odd)
    return out


def four(values, sign):
    (ar, ai), (br, bi), (cr, ci), (dr, di) = values
    pr, pi, mr, mi = ar + cr, ai + ci, ar - cr, ai - ci
    qr, qi, nr, ni = br + dr, bi + di, br - dr, bi - di
    if sign > 0:
        nr, ni = -nr, -ni
    return [(pr + qr, pi + qi), (mr + ni, mi - nr), (pr - qr, pi - qi), (mr - ni, mi + nr)]


def half_dft(x):
    out = [None] * 9
    out[0::2] = real_dft(x)
    odd = four([times_phase((x[v], -x[v + 4]), -v, 16) for v in range(4)], -1)
    out[1], out[5] = odd[0], odd[1]
    out[7] = (odd[2][0], -odd[2][1])
    out[3] = (odd[3][0], -odd[3][1])
    return out


def half_inverse(w):
    even = real_inverse(w[0::2])
    odd = four([w[1], w[5], (w[7][0], -w[7][1]), (w[3][0], -w[3][1])], 1)
    odd = [times_phase(value, v, 16) for v, value in enumerate(odd)]
    return [even[v] + odd[v][0] for v in range(4)] + [even[v + 4] - odd[v][1] for v in range(4)]


def split(value):
    high = value.astype(jnp.bfloat16)
    return high, (value - high.astype(jnp.float32)).astype(jnp.bfloat16)


def product(left, table_high, table_low, side):
    high, low = split(left)

    def dot(x, y):
        return lax.dot_general(x, y, (((1,), (side,)), ((), ())), preferred_element_type=jnp.float32)

    return dot(high, table_high) + (dot(high, table_low) + dot(low, table_high))


def spans(columns, width):
    return [slice(start, min(start + width, columns)) for start in range(0, columns, width)]


def is_cap(lat):
    count = lax.axis_size("lat")
    return (lat < count // 4) | (lat >= count - count // 4)


def flux_of(face_speed, south, north):
    return jnp.maximum(face_speed, 0.0) * south + jnp.minimum(face_speed, 0.0) * north


def near_is_north():
    return lax.rem(lax.axis_index("lat"), 2) == 0


def begin_kernel(
    cells_hbm, speed_hbm, mine_ref, send_ref, near_ref, far_ref, near_part_ref, far_part_ref,
    cells_ref, speed_ref, sems,
):
    tracer_count, levels, row_count, columns = cells_ref.shape
    share = tracer_count // PAIR
    core = lax.rem(lax.axis_index("lon"), PAIR)
    north = near_is_north()
    loads = [pltpu.make_async_copy(speed_hbm, speed_ref, sems.at[tracer_count])]
    owners = []
    for slot in range(tracer_count):
        place, i = divmod(slot, share)
        owners.append(lax.rem(core + place, PAIR) * share + i)
        loads.append(pltpu.make_async_copy(cells_hbm.at[owners[-1]], cells_ref.at[slot], sems.at[slot]))
    for load in loads:
        load.start()
    loads[0].wait()
    near_ref[tracer_count * levels :] = speed_ref[:, 0]
    far_ref[tracer_count * levels :] = speed_ref[:, 0]
    for slot, t in enumerate(owners):
        loads[slot + 1].wait()
        out_ref, i = (mine_ref, send_ref)[slot // share], slot % share
        place = pl.ds(pl.multiple_of(t * levels, levels), levels)
        for lanes in spans(columns, 3 * LANES):
            speed = [speed_ref[:, j, lanes] for j in range(row_count)]
            x = [cells_ref[slot, :, j, lanes] for j in range(row_count)]
            flux = [flux_of(speed[j], x[j - 1], x[j]) for j in range(1, row_count)]
            for j in range(1, row_count - 1):
                out_ref[i, j - 1, :, lanes] = x[j] + flux[j - 1] - flux[j]
            near_ref[place, lanes] = jnp.where(north, x[-1], x[0])
            far_ref[place, lanes] = jnp.where(north, x[0], x[-1])
            south_part, north_part = x[0] - flux[0], x[-1] + flux[-1]
            near_part_ref[t, :, lanes] = jnp.where(north, north_part, south_part)
            far_part_ref[t, :, lanes] = jnp.where(north, south_part, north_part)


def edge_kernel(is_near, own_ref, got_ref, part_ref, after_ref, mine_ref, send_ref):
    tracer_count, levels, columns = part_ref.shape
    share = tracer_count // PAIR
    total = tracer_count * levels
    core = lax.rem(lax.axis_index("lon"), PAIR)
    lat = lax.axis_index("lat")
    north = near_is_north() if is_near else jnp.logical_not(near_is_north())
    wall = jnp.where(north, lat == lax.axis_size("lat") - 1, lat == 0)
    for lanes in spans(columns, 3 * LANES):
        speed = jnp.where(north, got_ref[total:, lanes], own_ref[total:, lanes])
        speed = jnp.where(wall, 0.0, speed)
        for which, out_ref in enumerate([mine_ref, send_ref]):
            for i in range(share):
                t = lax.rem(core + which, PAIR) * share + i
                place = pl.ds(pl.multiple_of(t * levels, levels), levels)
                own, got = own_ref[place, lanes], got_ref[place, lanes]
                flux = flux_of(speed, jnp.where(north, own, got), jnp.where(north, got, own))
                out_ref[i, 0, :, lanes] = part_ref[t, :, lanes] + jnp.where(north, -flux, flux)


def forward_kernel(
    mine_ref, theirs_ref, phase_ref, high_ref, low_ref, after_ref, *refs
):
    *refs, stack_ref = refs
    relays = len(refs) // 3
    message_ref, held_ref = refs[relays : relays + 2]
    for source_ref, relay_ref in zip(refs[:relays], refs[relays + 2 :]):
        relay_ref[...] = source_ref[...]
    share, number, levels, columns = mine_ref.shape
    piece = columns * PAIR // HALF
    padded = stack_ref.shape[1]
    modes = high_ref.shape[1] // 2
    group = levels * 2 * (HALF + 1)
    core = lax.rem(lax.axis_index("lon"), PAIR)
    count = share * number
    for n in range(count):
        i, j = divmod(n, number)
        held_ref[core, n, :, :columns] = mine_ref[i, j]
        held_ref[1 - core, n, :, :columns] = theirs_ref[i, j]
        for pos in range(PAIR):
            held_ref[pos, n, :, columns:] = jnp.zeros((levels, held_ref.shape[3] - columns), jnp.float32)
        message_ref[n, :, 2 * MODES :] = held_ref[PAIR - 1, n, :, columns - LANES : columns]

    @pl.when(is_cap(lax.axis_index("lat")))
    def _():
        for n in range(count):
            for tile in range(0, padded, LANES):
                lanes = slice(tile, tile + LANES)
                x = []
                for u in range(HALF):
                    pos, start = divmod(u * piece, columns)
                    x.append(held_ref[pos, n, :, start + tile : start + tile + LANES])
                for r, (re, im) in enumerate(half_dft(x)):
                    base = n * group + 2 * r * levels
                    if r == 0:
                        im = jnp.zeros_like(re)
                    else:
                        c, s = phase_ref[2 * r : 2 * r + 1, lanes], phase_ref[2 * r + 1 : 2 * r + 2, lanes]
                        if im is None:
                            re, im = re * c, -(re * s)
                        else:
                            re, im = re * c + im * s, im * c - re * s
                    stack_ref[base : base + levels, lanes] = re
                    stack_ref[base + levels : base + 2 * levels, lanes] = im
        coeffs = product(stack_ref[...], high_ref[...], low_ref[...], 0)
        upper = lax.broadcasted_iota(jnp.int32, (levels, modes), 1) >= modes // 2
        for n in range(count):
            first = None
            for r in [0, HALF] + list(range(1, HALF)):
                base = n * group + 2 * r * levels
                re, im = coeffs[base : base + levels], coeffs[base + levels : base + 2 * levels]
                x_re = re[:, :modes] + im[:, modes:]
                x_im = im[:, :modes] - re[:, modes:]
                if r == 0:
                    first = x_re, x_im
                    continue
                slot = r
                if r == HALF:
                    x_re = jnp.where(upper, first[0], pltpu.roll(x_re, modes // 2, 1))
                    x_im = jnp.where(upper, first[1], pltpu.roll(x_im, modes // 2, 1))
                    slot = 0
                message_ref[n, :, 2 * slot * modes : (2 * slot + 1) * modes] = x_re
                message_ref[n, :, (2 * slot + 1) * modes : (2 * slot + 2) * modes] = x_im


def row_vector(ref, row, levels):
    level = lax.broadcasted_iota(jnp.int32, (levels, LANES), 0)
    out = jnp.full((levels, LANES), ref[row, 0])
    for i in range(1, levels):
        out = jnp.where(level == i, ref[row, i], out)
    return out


def displaced(tiles, distance, share):
    lane = lax.broadcasted_iota(jnp.int32, distance.shape, 1)

    def moved(steps):
        index = (lane - steps) & (LANES - 1)
        turned = [jnp.take_along_axis(v, index, axis=1, mode="promise_in_bounds") for v in tiles]
        from_left = lane < steps
        return [jnp.where(from_left, a, b) for a, b in zip(turned, turned[1:])]

    pairs = zip(moved(distance), moved(distance + 1))
    return [(1.0 - share) * here + share * earlier for here, earlier in pairs]


def rows_of(which, row_count):
    if which == "inner":
        return list(range(1, row_count - 1))
    north = near_is_north() if which == "near" else jnp.logical_not(near_is_north())
    return [jnp.where(north, row_count - 1, 0)]


def wave_angle(steps, lon_cells):
    steps = lax.rem(steps, lon_cells)
    return steps.astype(jnp.float32) * (2.0 * math.pi / lon_cells)


def row_kernel(
    columns, shift_ref, fraction_ref, cutoff_ref, damping_ref, wave_ref, after_ref,
    distance_ref, share_ref, keep_ref, gain_ref,
):
    row_count, levels = shift_ref.shape
    lon_cells = columns * PAIR * PAIR
    modes = gain_ref.shape[3]
    lat = lax.axis_index("lat")
    for row in range(row_count):
        distance_ref[row] = row_vector(shift_ref, row, levels).astype(jnp.float32)
        share_ref[row] = row_vector(fraction_ref, row, levels)
        keep_ref[row] = jnp.full((levels, LANES), damping_ref[lat * row_count + row])

    @pl.when(is_cap(lat))
    def _():
        lane = lax.broadcasted_iota(jnp.int32, (levels, modes), 1)
        mode = lane - modes // 2
        for row in range(row_count):
            distance = distance_ref[row].astype(jnp.int32)
            share = share_ref[row]
            limit = cutoff_ref[lat * row_count + row]
            wide = wave_angle(RADIX * mode * distance, lon_cells)
            wide_re, wide_im = jnp.cos(wide), -jnp.sin(wide)
            fine = wave_angle(lane * distance, lon_cells)
            fine_re, fine_im = jnp.cos(fine), -jnp.sin(fine)
            for r in range(HALF + 1):
                wavenumber = RADIX * mode + r
                kept = jnp.abs(wavenumber) <= limit
                if r in (0, HALF):
                    kept = kept & (wavenumber >= 0)
                once = r % 2 == 0 and r not in (0, HALF)
                weight = jnp.full((levels, modes), (1.0 if once else 2.0) / lon_cells)
                if r == 0:
                    weight = jnp.where(wavenumber == 0, 1.0 / lon_cells, weight)
                weight = jnp.where(kept, weight, 0.0)
                mix_re = (1.0 - share) + share * wave_ref[2 * r : 2 * r + 1]
                mix_im = -share * wave_ref[2 * r + 1 : 2 * r + 2]
                turn_re, turn_im = fine_re[:, r : r + 1], fine_im[:, r : r + 1]
                re, im = wide_re * turn_re - wide_im * turn_im, wide_re * turn_im + wide_im * turn_re
                gain_ref[row, 2 * r] = (re * mix_re - im * mix_im) * weight
                gain_ref[row, 2 * r + 1] = (re * mix_im + im * mix_re) * weight


def shift_kernel(which, columns, distance_ref, share_ref, held_ref, after_ref, moved_ref):
    _, count, levels, padded = held_ref.shape
    rows = rows_of(which, share_ref.shape[0])
    number = len(rows)
    for j, row in enumerate(rows):
        distance, share = distance_ref[row].astype(jnp.int32), share_ref[row]
        for n in range(j, count, number):
            for pos in range(PAIR):
                tiles = [held_ref[PAIR - 1 - pos, n, :, columns - LANES : columns]]
                tiles += [held_ref[pos, n, :, lanes] for lanes in spans(padded, LANES)]
                for lanes, tile in zip(spans(padded, LANES), displaced(tiles, distance, share)):
                    moved_ref[n, pos, :, lanes] = tile


def inverse_kernel(
    which, columns, distance_ref, share_ref, keep_ref, gain_ref, phase_ref, high_ref, low_ref,
    held_ref, moved_ref, own_ref, other_ref, after_ref, mine_ref, send_ref,
    stack_ref, back_ref, pair_ref,
):
    _, count, levels, _ = held_ref.shape
    rows = rows_of(which, share_ref.shape[0])
    number = len(rows)
    piece = columns * PAIR // HALF
    padded = stack_ref.shape[1]
    modes = gain_ref.shape[3]
    group = levels * 2 * (HALF + 1)
    core = lax.rem(lax.axis_index("lon"), PAIR)
    cap = is_cap(lax.axis_index("lat"))
    for j, row in enumerate(rows):
        distance, share = distance_ref[row].astype(jnp.int32), share_ref[row]
        for n in range(j, count, number):
            tiles = [other_ref[n, :, 2 * MODES :], held_ref[0, n, :, :LANES]]
            (moved_ref[n, 0, :, :LANES],) = displaced(tiles, distance, share)

    @pl.when(jnp.logical_not(cap))
    def _():
        for n in range(count):
            i, j = divmod(n, number)
            mine_ref[i, j] = moved_ref[n, core, :, :columns]
            send_ref[i, j] = moved_ref[n, 1 - core, :, :columns]

    @pl.when(cap)
    def _():
        for n in range(count):
            row = rows[n % number]
            for r in range(HALF + 1):
                slot = r % HALF
                ours, theirs = (
                    [ref[n, :, (2 * slot + part) * modes : (2 * slot + part + 1) * modes] for part in range(2)]
                    for ref in (own_ref, other_ref)
                )
                if r % 2:
                    re, im = ours[0] - theirs[0], ours[1] - theirs[1]
                else:
                    re, im = ours[0] + theirs[0], ours[1] + theirs[1]
                if r == HALF:
                    re, im = pltpu.roll(re, modes // 2, 1), pltpu.roll(im, modes // 2, 1)
                g_re, g_im = gain_ref[row, 2 * r], gain_ref[row, 2 * r + 1]
                re, im = re * g_re - im * g_im, re * g_im + im * g_re
                base = n * group + 2 * r * levels
                back_ref[base : base + levels, :modes] = re
                back_ref[base : base + levels, modes:] = -im
                back_ref[base + levels : base + 2 * levels, :modes] = im
                back_ref[base + levels : base + 2 * levels, modes:] = re
        stack_ref[...] = product(back_ref[...], high_ref[...], low_ref[...], 1)
        for n in range(count):
            i, j = divmod(n, number)
            keep = keep_ref[rows[j]]
            for tile in range(0, padded, LANES):
                lanes = slice(tile, tile + LANES)
                spectrum = []
                for r in range(HALF + 1):
                    base = n * group + 2 * r * levels
                    re = stack_ref[base : base + levels, lanes]
                    im = stack_ref[base + levels : base + 2 * levels, lanes]
                    if r > 0:
                        c, s = phase_ref[2 * r : 2 * r + 1, lanes], phase_ref[2 * r + 1 : 2 * r + 2, lanes]
                        re, im = re * c - im * s, re * s + im * c
                    spectrum.append((re, im))
                width = min(LANES, piece - tile)
                for u, value in enumerate(half_inverse(spectrum)):
                    pos, start = divmod(u * piece, columns)
                    start += tile
                    shifted = moved_ref[n, pos, :, start : start + LANES]
                    result = keep * shifted + (1.0 - keep) * value
                    pair_ref[pos, n, :, start : start + width] = result[:, :width]
        for n in range(count):
            i, j = divmod(n, number)
            mine_ref[i, j] = pair_ref[core, n, :, :columns]
            send_ref[i, j] = pair_ref[1 - core, n, :, :columns]


def end_kernel(place, inner, near, far, *refs):
    out_hbm, out_ref, sems = refs[-3:]
    share, levels, row_count, columns = out_ref.shape
    core = lax.rem(lax.axis_index("lon"), PAIR)
    north = near_is_north()
    copies = []
    for i in range(share):
        for lanes in spans(columns, 4 * LANES):
            a, b = near[i, 0, :, lanes], far[i, 0, :, lanes]
            out_ref[i, :, 0, lanes] = jnp.where(north, b, a)
            out_ref[i, :, row_count - 1, lanes] = jnp.where(north, a, b)
            for j in range(1, row_count - 1):
                out_ref[i, :, j, lanes] = inner[i, j - 1, :, lanes]
        t = lax.rem(core + place, PAIR) * share + i
        copies.append(pltpu.make_async_copy(out_ref.at[i], out_hbm.at[t], sems.at[i]))
        copies[-1].start()
    for copy in copies:
        copy.wait()


def filter_tables(lon_cells):
    piece = lon_cells // RADIX
    padded = -(-piece // LANES) * LANES
    modes = 2 * MODES // RADIX
    q = np.arange(modes) - modes // 2
    angle = 2 * np.pi * (np.arange(piece)[:, None] * q[None, :] % piece) / piece
    table = np.zeros((padded, 2 * modes))
    table[:piece, :modes] = np.cos(angle)
    table[:piece, modes:] = np.sin(angle)
    high = table.astype(jnp.bfloat16)
    low = (table - high.astype(np.float64)).astype(jnp.bfloat16)
    r = np.arange(HALF + 1)[:, None]

    def waves(steps):
        angle = 2 * np.pi * steps / lon_cells
        pairs = np.stack([np.cos(angle), np.sin(angle)], axis=1)
        return pairs.reshape(-1, steps.shape[1]).astype(np.float32)

    phase = waves(r * np.arange(padded)[None, :])
    wave = waves(RADIX * q[None, :] + r)
    return phase, wave, high, low


SMALL, WHOLE, UNREAD = pltpu.SMEM, pltpu.VMEM, pl.ANY


def call(kernel, outs, operands, scratch=(), sems=0, place=None, aliases=None):
    return pl.pallas_call(
        kernel,
        out_shape=[jax.ShapeDtypeStruct(shape, jnp.float32) for shape in outs],
        in_specs=[pl.BlockSpec(memory_space=place) for _, place in operands],
        out_specs=[pl.BlockSpec(memory_space=place or WHOLE)] * len(outs),
        input_output_aliases=aliases or {},
        scratch_shapes=[pltpu.VMEM(shape, jnp.float32) for shape in scratch]
        + ([pltpu.SemaphoreType.DMA((sems,))] if sems else []),
        compiler_params=pltpu.CompilerParams(vmem_limit_bytes=24 << 20),
        cost_estimate=pl.CostEstimate(flops=1, bytes_accessed=1, transcendentals=0),
    )(*[v for v, _ in operands])


def whole(*values):
    return [(v, WHOLE) for v in values]


def body(tracers, merid_courant, zonal_shift, zonal_fraction, cutoff, damping):
    tracer_count, level_count, row_count, column_count = tracers.shape
    lat_count = lax.axis_size("lat")
    lon_count = lax.axis_size("lon")
    assert lon_count == PAIR * PAIR and tracer_count % PAIR == 0 and row_count > 2
    share = tracer_count // PAIR
    lon_cells = column_count * lon_count
    phase, wave, high, low = [jnp.asarray(t) for t in filter_tables(lon_cells)]
    padded, double = high.shape
    width = -(-column_count // LANES) * LANES
    assert column_count - lon_cells // RADIX + padded <= width
    group = level_count * 2 * (HALF + 1)
    shift_rows, fraction_rows = zonal_shift.T, zonal_fraction.T

    def swap_core(value):
        return lax.ppermute(value, "lon", [(p, p ^ 1) for p in range(lon_count)])

    def swap_half(value):
        return lax.ppermute(value, "lon", [(p, p ^ 2) for p in range(lon_count)])

    def swap_band(value, first):
        pairs = []
        for b in range(first, lat_count - 1, 2):
            pairs += [(b, b + 1), (b + 1, b)]
        return lax.ppermute(value, "lat", pairs)

    def set_shape(number):
        return (share, number, level_count, column_count)

    def forward(mine, theirs, after, *relay):
        count = mine.shape[0] * mine.shape[1]
        message_shape = (count, level_count, 2 * MODES + LANES)
        return call(
            forward_kernel,
            [message_shape, (PAIR, count, level_count, width)] + [v.shape for v in relay],
            whole(mine, theirs, phase, high, low) + [(after, UNREAD)] + whole(*relay),
            [(count * group, padded)],
        )

    def shifted(which, held, after):
        count = held.shape[1]
        return call(
            functools.partial(shift_kernel, which, column_count),
            [(count, PAIR, level_count, width)],
            whole(distance, fraction, held) + [(after, UNREAD)],
        )

    def inverse(which, held, moved, own, other, after):
        count = held.shape[1]
        return call(
            functools.partial(inverse_kernel, which, column_count),
            [set_shape(count // share)] * 2,
            whole(distance, fraction, keep, gain, phase, high, low, held, moved, own, other)
            + [(after, UNREAD)],
            [(count * group, padded), (count * group, double), (PAIR, count, level_count, width)],
        )

    edge_shape = ((tracer_count + 1) * level_count, column_count)
    part_shape = (tracer_count, level_count, column_count)
    inner_mine, inner_send, near_edge, far_edge, near_part, far_part = call(
        begin_kernel,
        [set_shape(row_count - 2)] * 2 + [edge_shape] * 2 + [part_shape] * 2,
        [(pltpu.with_memory_space_constraint(v, pltpu.HBM), pltpu.HBM) for v in (tracers, merid_courant)],
        [tracers.shape, merid_courant.shape],
        tracer_count + 1,
    )
    inner_theirs = swap_core(inner_send)
    near_got = swap_band(near_edge, 0)
    inner_own, inner_held, far_relay = forward(inner_mine, inner_theirs, near_part, far_edge)
    far_got = swap_band(far_relay, 1)
    inner_other = swap_half(inner_own)
    row_shape = (row_count, level_count, LANES)
    distance, fraction, keep, gain = call(
        functools.partial(row_kernel, column_count),
        [row_shape] * 3 + [(row_count, 2 * (HALF + 1), level_count, double // 2)],
        [(v, SMALL) for v in (shift_rows, fraction_rows, cutoff, damping)]
        + whole(wave)
        + [(inner_own, UNREAD)],
    )
    (inner_moved,) = shifted("inner", inner_held, inner_own)

    near_mine, near_send = call(
        functools.partial(edge_kernel, True),
        [set_shape(1)] * 2,
        whole(near_edge, near_got, near_part) + [(inner_moved, UNREAD)],
    )
    near_theirs = swap_core(near_send)
    near_own, near_held = forward(near_mine, near_theirs, inner_moved)
    near_other = swap_half(near_own)
    (near_moved,) = shifted("near", near_held, near_own)
    inner = inverse("inner", inner_held, inner_moved, inner_own, inner_other, near_moved)
    inner_back = swap_core(inner[1])

    far_mine, far_send = call(
        functools.partial(edge_kernel, False),
        [set_shape(1)] * 2,
        whole(far_edge, far_got, far_part) + [(inner[0], UNREAD)],
    )
    far_theirs = swap_core(far_send)
    near = inverse("near", near_held, near_moved, near_own, near_other, far_mine)
    near_back = swap_core(near[1])
    far_own, far_held = forward(far_mine, far_theirs, near[0])
    far_other = swap_half(far_own)
    (far_moved,) = shifted("far", far_held, far_own)
    far = inverse("far", far_held, far_moved, far_own, far_other, far_moved)
    far_back = swap_core(far[1])
    (half_done,) = call(
        functools.partial(end_kernel, 0),
        [tracers.shape],
        whole(inner[0], near[0], far[0]),
        [(share,) + tracers.shape[1:]],
        share,
        pltpu.HBM,
    )
    (result,) = call(
        functools.partial(end_kernel, 1),
        [tracers.shape],
        whole(inner_back, near_back, far_back) + [(half_done, pltpu.HBM)],
        [(share,) + tracers.shape[1:]],
        share,
        pltpu.HBM,
        {3: 0},
    )
    return result


def solution(mesh):
    placed = (
        P(None, None, "lat", "lon"),
        P(None, "lat", "lon"),
        P(None, "lat"),
        P(None, "lat"),
        P(),
        P(),
    )
    return jax.shard_map(
        body, mesh=mesh, in_specs=placed, out_specs=P(None, None, "lat", "lon"), check_vma=False
    )
```

```python
import functools
import math

import jax
import jax.numpy as jnp
import numpy as np
from jax import lax
from jax.experimental import pallas as pl
from jax.experimental.pallas import tpu as pltpu
from jax.sharding import PartitionSpec as P

MODES = 1024
SMAX = 64
RADIX = 16
HALF = RADIX // 2
LANES = 128
PAIR = 2


def times_phase(value, numerator, denominator):
    re, im = value
    eighth = (8 * numerator % (8 * denominator)) / denominator
    if eighth == 0:
        return re, im
    if eighth == 2:
        return -im, re
    if eighth == 4:
        return -re, -im
    if eighth == 6:
        return im, -re
    c = math.cos(2 * math.pi * numerator / denominator)
    s = math.sin(2 * math.pi * numerator / denominator)
    if eighth == 7:
        return (re + im) * c, (im - re) * c
    if eighth == 1:
        return (re - im) * c, (re + im) * c
    return re * c - im * s, re * s + im * c


def real_dft(values):
    n = len(values)
    if n == 2:
        return [(values[0] + values[1], None), (values[0] - values[1], None)]
    even, odd = real_dft(values[0::2]), real_dft(values[1::2])
    out = [None] * (n // 2 + 1)
    for r in range(n // 4 + 1):
        (er, ei), (tr, ti) = even[r], odd[r]
        if r == 0:
            out[0] = (er + tr, None)
            out[n // 2] = (er - tr, None)
        elif r == n // 4:
            out[r] = (er, -tr)
        else:
            tr, ti = times_phase((tr, ti), -r, n)
            out[r] = (er + tr, ei + ti)
            out[n // 2 - r] = (er - tr, ti - ei)
    return out


def real_inverse(spectrum):
    n = 2 * (len(spectrum) - 1)
    if n == 2:
        a, b = spectrum[0][0], spectrum[1][0]
        return [a + b, a - b]
    even, odd = [None] * (n // 4 + 1), [None] * (n // 4 + 1)
    for r in range(n // 4 + 1):
        (ar, ai), (br, bi) = spectrum[r], spectrum[n // 2 - r]
        if r == 0:
            even[0] = (ar + br, None)
            odd[0] = (ar - br, None)
        elif r == n // 4:
            even[r] = (ar + ar, None)
            odd[r] = (-(ai + ai), None)
        else:
            even[r] = (ar + br, ai - bi)
            odd[r] = times_phase((ar - br, ai + bi), r, n)
    out = [None] * n
    out[0::2] = real_inverse(even)
    out[1::2] = real_inverse(odd)
    return out


def four(values, sign):
    (ar, ai), (br, bi), (cr, ci), (dr, di) = values
    pr, pi, mr, mi = ar + cr, ai + ci, ar - cr, ai - ci
    qr, qi, nr, ni = br + dr, bi + di, br - dr, bi - di
    if sign > 0:
        nr, ni = -nr, -ni
    return [(pr + qr, pi + qi), (mr + ni, mi - nr), (pr - qr, pi - qi), (mr - ni, mi + nr)]


def half_dft(x):
    out = [None] * 9
    out[0::2] = real_dft(x)
    odd = four([times_phase((x[v], -x[v + 4]), -v, 16) for v in range(4)], -1)
    out[1], out[5] = odd[0], odd[1]
    out[7] = (odd[2][0], -odd[2][1])
    out[3] = (odd[3][0], -odd[3][1])
    return out


def half_inverse(w):
    even = real_inverse(w[0::2])
    odd = four([w[1], w[5], (w[7][0], -w[7][1]), (w[3][0], -w[3][1])], 1)
    odd = [times_phase(value, v, 16) for v, value in enumerate(odd)]
    return [even[v] + odd[v][0] for v in range(4)] + [even[v + 4] - odd[v][1] for v in range(4)]


def split(value):
    high = value.astype(jnp.bfloat16)
    return high, (value - high.astype(jnp.float32)).astype(jnp.bfloat16)


def product(left, table_high, table_low, side):
    high, low = split(left)

    def dot(x, y):
        return lax.dot_general(x, y, (((1,), (side,)), ((), ())), preferred_element_type=jnp.float32)

    return dot(high, table_high) + (dot(high, table_low) + dot(low, table_high))


def spans(columns, width):
    return [slice(start, min(start + width, columns)) for start in range(0, columns, width)]


def is_cap(lat):
    count = lax.axis_size("lat")
    return (lat < count // 4) | (lat >= count - count // 4)


def flux_of(face_speed, south, north):
    return jnp.maximum(face_speed, 0.0) * south + jnp.minimum(face_speed, 0.0) * north


def near_is_north():
    return lax.rem(lax.axis_index("lat"), 2) == 0


def begin_kernel(
    cells_hbm, speed_hbm, mine_ref, send_ref, near_ref, far_ref, near_part_ref, far_part_ref,
    cells_ref, speed_ref, sems,
):
    tracer_count, levels, row_count, columns = cells_ref.shape
    share = tracer_count // PAIR
    core = lax.rem(lax.axis_index("lon"), PAIR)
    north = near_is_north()
    loads = [pltpu.make_async_copy(speed_hbm, speed_ref, sems.at[tracer_count])]
    owners = []
    for slot in range(tracer_count):
        place, i = divmod(slot, share)
        owners.append(lax.rem(core + place, PAIR) * share + i)
        loads.append(pltpu.make_async_copy(cells_hbm.at[owners[-1]], cells_ref.at[slot], sems.at[slot]))
    for load in loads:
        load.start()
    loads[0].wait()
    near_ref[tracer_count * levels :] = speed_ref[:, 0]
    far_ref[tracer_count * levels :] = speed_ref[:, 0]
    for slot, t in enumerate(owners):
        loads[slot + 1].wait()
        out_ref, i = (mine_ref, send_ref)[slot // share], slot % share
        place = pl.ds(pl.multiple_of(t * levels, levels), levels)
        for lanes in spans(columns, 3 * LANES):
            speed = [speed_ref[:, j, lanes] for j in range(row_count)]
            x = [cells_ref[slot, :, j, lanes] for j in range(row_count)]
            flux = [flux_of(speed[j], x[j - 1], x[j]) for j in range(1, row_count)]
            for j in range(1, row_count - 1):
                out_ref[i, j - 1, :, lanes] = x[j] + flux[j - 1] - flux[j]
            near_ref[place, lanes] = jnp.where(north, x[-1], x[0])
            far_ref[place, lanes] = jnp.where(north, x[0], x[-1])
            south_part, north_part = x[0] - flux[0], x[-1] + flux[-1]
            near_part_ref[t, :, lanes] = jnp.where(north, north_part, south_part)
            far_part_ref[t, :, lanes] = jnp.where(north, south_part, north_part)


def edge_kernel(is_near, own_ref, got_ref, part_ref, after_ref, mine_ref, send_ref):
    tracer_count, levels, columns = part_ref.shape
    share = tracer_count // PAIR
    total = tracer_count * levels
    core = lax.rem(lax.axis_index("lon"), PAIR)
    lat = lax.axis_index("lat")
    north = near_is_north() if is_near else jnp.logical_not(near_is_north())
    wall = jnp.where(north, lat == lax.axis_size("lat") - 1, lat == 0)
    for lanes in spans(columns, 3 * LANES):
        speed = jnp.where(north, got_ref[total:, lanes], own_ref[total:, lanes])
        speed = jnp.where(wall, 0.0, speed)
        for which, out_ref in enumerate([mine_ref, send_ref]):
            for i in range(share):
                t = lax.rem(core + which, PAIR) * share + i
                place = pl.ds(pl.multiple_of(t * levels, levels), levels)
                own, got = own_ref[place, lanes], got_ref[place, lanes]
                flux = flux_of(speed, jnp.where(north, own, got), jnp.where(north, got, own))
                out_ref[i, 0, :, lanes] = part_ref[t, :, lanes] + jnp.where(north, -flux, flux)


def forward_kernel(
    mine_ref, theirs_ref, phase_ref, high_ref, low_ref, after_ref, *refs
):
    *refs, stack_ref = refs
    relays = (len(refs) - 3) // 2
    message_ref, held_ref, rim_ref = refs[relays : relays + 3]
    for source_ref, relay_ref in zip(refs[:relays], refs[relays + 3 :]):
        relay_ref[...] = source_ref[...]
    share, number, levels, columns = mine_ref.shape
    piece = columns * PAIR // HALF
    padded = stack_ref.shape[1]
    modes = high_ref.shape[1] // 2
    group = levels * 2 * (HALF + 1)
    core = lax.rem(lax.axis_index("lon"), PAIR)
    count = share * number
    for n in range(count):
        i, j = divmod(n, number)
        held_ref[core, n, :, :columns] = mine_ref[i, j]
        held_ref[1 - core, n, :, :columns] = theirs_ref[i, j]
        for pos in range(PAIR):
            held_ref[pos, n, :, columns:] = jnp.zeros((levels, held_ref.shape[3] - columns), jnp.float32)
        rim_ref[n] = held_ref[PAIR - 1, n, :, columns - LANES : columns]
        message_ref[n, :, 2 * MODES :] = rim_ref[n]

    @pl.when(is_cap(lax.axis_index("lat")))
    def _():
        for n in range(count):
            for tile in range(0, padded, LANES):
                lanes = slice(tile, tile + LANES)
                x = []
                for u in range(HALF):
                    pos, start = divmod(u * piece, columns)
                    x.append(held_ref[pos, n, :, start + tile : start + tile + LANES])
                for r, (re, im) in enumerate(half_dft(x)):
                    base = n * group + 2 * r * levels
                    if r == 0:
                        im = jnp.zeros_like(re)
                    else:
                        c, s = phase_ref[2 * r : 2 * r + 1, lanes], phase_ref[2 * r + 1 : 2 * r + 2, lanes]
                        if im is None:
                            re, im = re * c, -(re * s)
                        else:
                            re, im = re * c + im * s, im * c - re * s
                    stack_ref[base : base + levels, lanes] = re
                    stack_ref[base + levels : base + 2 * levels, lanes] = im
        coeffs = product(stack_ref[...], high_ref[...], low_ref[...], 0)
        upper = lax.broadcasted_iota(jnp.int32, (levels, modes), 1) >= modes // 2
        for n in range(count):
            first = None
            for r in [0, HALF] + list(range(1, HALF)):
                base = n * group + 2 * r * levels
                re, im = coeffs[base : base + levels], coeffs[base + levels : base + 2 * levels]
                x_re = re[:, :modes] + im[:, modes:]
                x_im = im[:, :modes] - re[:, modes:]
                if r == 0:
                    first = x_re, x_im
                    continue
                slot = r
                if r == HALF:
                    x_re = jnp.where(upper, first[0], pltpu.roll(x_re, modes // 2, 1))
                    x_im = jnp.where(upper, first[1], pltpu.roll(x_im, modes // 2, 1))
                    slot = 0
                message_ref[n, :, 2 * slot * modes : (2 * slot + 1) * modes] = x_re
                message_ref[n, :, (2 * slot + 1) * modes : (2 * slot + 2) * modes] = x_im


def row_vector(ref, row, levels):
    level = lax.broadcasted_iota(jnp.int32, (levels, LANES), 0)
    out = jnp.full((levels, LANES), ref[row, 0])
    for i in range(1, levels):
        out = jnp.where(level == i, ref[row, i], out)
    return out


def displaced(tiles, distance, share):
    lane = lax.broadcasted_iota(jnp.int32, distance.shape, 1)

    def moved(steps):
        index = (lane - steps) & (LANES - 1)
        turned = [jnp.take_along_axis(v, index, axis=1, mode="promise_in_bounds") for v in tiles]
        from_left = lane < steps
        return [jnp.where(from_left, a, b) for a, b in zip(turned, turned[1:])]

    pairs = zip(moved(distance), moved(distance + 1))
    return [(1.0 - share) * here + share * earlier for here, earlier in pairs]


def rows_of(which, row_count):
    if which == "inner":
        return list(range(1, row_count - 1))
    north = near_is_north() if which == "near" else jnp.logical_not(near_is_north())
    return [jnp.where(north, row_count - 1, 0)]


def wave_angle(steps, lon_cells):
    steps = lax.rem(steps, lon_cells)
    return steps.astype(jnp.float32) * (2.0 * math.pi / lon_cells)


def row_kernel(
    columns, shift_ref, fraction_ref, cutoff_ref, damping_ref, wave_ref, after_ref,
    distance_ref, share_ref, keep_ref, gain_ref,
):
    row_count, levels = shift_ref.shape
    lon_cells = columns * PAIR * PAIR
    modes = gain_ref.shape[3]
    lat = lax.axis_index("lat")
    for row in range(row_count):
        distance_ref[row] = row_vector(shift_ref, row, levels).astype(jnp.float32)
        share_ref[row] = row_vector(fraction_ref, row, levels)
        keep_ref[row] = jnp.full((levels, LANES), damping_ref[lat * row_count + row])

    @pl.when(is_cap(lat))
    def _():
        lane = lax.broadcasted_iota(jnp.int32, (levels, modes), 1)
        mode = lane - modes // 2
        for row in range(row_count):
            distance = distance_ref[row].astype(jnp.int32)
            share = share_ref[row]
            limit = cutoff_ref[lat * row_count + row]
            wide = wave_angle(RADIX * mode * distance, lon_cells)
            wide_re, wide_im = jnp.cos(wide), -jnp.sin(wide)
            fine = wave_angle(lane * distance, lon_cells)
            fine_re, fine_im = jnp.cos(fine), -jnp.sin(fine)
            for r in range(HALF + 1):
                wavenumber = RADIX * mode + r
                kept = jnp.abs(wavenumber) <= limit
                if r in (0, HALF):
                    kept = kept & (wavenumber >= 0)
                once = r % 2 == 0 and r not in (0, HALF)
                weight = jnp.full((levels, modes), (1.0 if once else 2.0) / lon_cells)
                if r == 0:
                    weight = jnp.where(wavenumber == 0, 1.0 / lon_cells, weight)
                weight = jnp.where(kept, weight, 0.0)
                mix_re = (1.0 - share) + share * wave_ref[2 * r : 2 * r + 1]
                mix_im = -share * wave_ref[2 * r + 1 : 2 * r + 2]
                turn_re, turn_im = fine_re[:, r : r + 1], fine_im[:, r : r + 1]
                re, im = wide_re * turn_re - wide_im * turn_im, wide_re * turn_im + wide_im * turn_re
                gain_ref[row, 2 * r] = (re * mix_re - im * mix_im) * weight
                gain_ref[row, 2 * r + 1] = (re * mix_im + im * mix_re) * weight


def shift_kernel(which, columns, distance_ref, share_ref, held_ref, after_ref, moved_ref):
    _, count, levels, padded = held_ref.shape
    rows = rows_of(which, share_ref.shape[0])
    number = len(rows)
    for j, row in enumerate(rows):
        distance, share = distance_ref[row].astype(jnp.int32), share_ref[row]
        for n in range(j, count, number):
            for pos in range(PAIR):
                tiles = [held_ref[PAIR - 1 - pos, n, :, columns - LANES : columns]]
                tiles += [held_ref[pos, n, :, lanes] for lanes in spans(padded, LANES)]
                for lanes, tile in zip(spans(padded, LANES), displaced(tiles, distance, share)):
                    moved_ref[n, pos, :, lanes] = tile


def inverse_kernel(
    which, columns, distance_ref, share_ref, keep_ref, gain_ref, phase_ref, high_ref, low_ref,
    held_ref, moved_ref, own_ref, other_ref, rim_ref, after_ref, mine_ref, send_ref,
    stack_ref, back_ref, pair_ref,
):
    _, count, levels, _ = held_ref.shape
    rows = rows_of(which, share_ref.shape[0])
    number = len(rows)
    piece = columns * PAIR // HALF
    padded = stack_ref.shape[1]
    modes = gain_ref.shape[3]
    group = levels * 2 * (HALF + 1)
    core = lax.rem(lax.axis_index("lon"), PAIR)
    cap = is_cap(lax.axis_index("lat"))
    for j, row in enumerate(rows):
        distance, share = distance_ref[row].astype(jnp.int32), share_ref[row]
        for n in range(j, count, number):
            rim = jnp.where(cap, other_ref[n, :, 2 * MODES :], rim_ref[n])
            tiles = [rim, held_ref[0, n, :, :LANES]]
            (moved_ref[n, 0, :, :LANES],) = displaced(tiles, distance, share)

    @pl.when(jnp.logical_not(cap))
    def _():
        for n in range(count):
            i, j = divmod(n, number)
            mine_ref[i, j] = moved_ref[n, core, :, :columns]
            send_ref[i, j] = moved_ref[n, 1 - core, :, :columns]

    @pl.when(cap)
    def _():
        for n in range(count):
            row = rows[n % number]
            for r in range(HALF + 1):
                slot = r % HALF
                ours, theirs = (
                    [ref[n, :, (2 * slot + part) * modes : (2 * slot + part + 1) * modes] for part in range(2)]
                    for ref in (own_ref, other_ref)
                )
                if r % 2:
                    re, im = ours[0] - theirs[0], ours[1] - theirs[1]
                else:
                    re, im = ours[0] + theirs[0], ours[1] + theirs[1]
                if r == HALF:
                    re, im = pltpu.roll(re, modes // 2, 1), pltpu.roll(im, modes // 2, 1)
                g_re, g_im = gain_ref[row, 2 * r], gain_ref[row, 2 * r + 1]
                re, im = re * g_re - im * g_im, re * g_im + im * g_re
                base = n * group + 2 * r * levels
                back_ref[base : base + levels, :modes] = re
                back_ref[base : base + levels, modes:] = -im
                back_ref[base + levels : base + 2 * levels, :modes] = im
                back_ref[base + levels : base + 2 * levels, modes:] = re
        stack_ref[...] = product(back_ref[...], high_ref[...], low_ref[...], 1)
        for n in range(count):
            i, j = divmod(n, number)
            keep = keep_ref[rows[j]]
            for tile in range(0, padded, LANES):
                lanes = slice(tile, tile + LANES)
                spectrum = []
                for r in range(HALF + 1):
                    base = n * group + 2 * r * levels
                    re = stack_ref[base : base + levels, lanes]
                    im = stack_ref[base + levels : base + 2 * levels, lanes]
                    if r > 0:
                        c, s = phase_ref[2 * r : 2 * r + 1, lanes], phase_ref[2 * r + 1 : 2 * r + 2, lanes]
                        re, im = re * c - im * s, re * s + im * c
                    spectrum.append((re, im))
                width = min(LANES, piece - tile)
                for u, value in enumerate(half_inverse(spectrum)):
                    pos, start = divmod(u * piece, columns)
                    start += tile
                    shifted = moved_ref[n, pos, :, start : start + LANES]
                    result = keep * shifted + (1.0 - keep) * value
                    pair_ref[pos, n, :, start : start + width] = result[:, :width]
        for n in range(count):
            i, j = divmod(n, number)
            mine_ref[i, j] = pair_ref[core, n, :, :columns]
            send_ref[i, j] = pair_ref[1 - core, n, :, :columns]


def end_kernel(place, inner, near, far, *refs):
    out_hbm, out_ref, sems = refs[-3:]
    share, levels, row_count, columns = out_ref.shape
    core = lax.rem(lax.axis_index("lon"), PAIR)
    north = near_is_north()
    copies = []
    for i in range(share):
        for lanes in spans(columns, 4 * LANES):
            a, b = near[i, 0, :, lanes], far[i, 0, :, lanes]
            out_ref[i, :, 0, lanes] = jnp.where(north, b, a)
            out_ref[i, :, row_count - 1, lanes] = jnp.where(north, a, b)
            for j in range(1, row_count - 1):
                out_ref[i, :, j, lanes] = inner[i, j - 1, :, lanes]
        t = lax.rem(core + place, PAIR) * share + i
        copies.append(pltpu.make_async_copy(out_ref.at[i], out_hbm.at[t], sems.at[i]))
        copies[-1].start()
    for copy in copies:
        copy.wait()


def filter_tables(lon_cells):
    piece = lon_cells // RADIX
    padded = -(-piece // LANES) * LANES
    modes = 2 * MODES // RADIX
    q = np.arange(modes) - modes // 2
    angle = 2 * np.pi * (np.arange(piece)[:, None] * q[None, :] % piece) / piece
    table = np.zeros((padded, 2 * modes))
    table[:piece, :modes] = np.cos(angle)
    table[:piece, modes:] = np.sin(angle)
    high = table.astype(jnp.bfloat16)
    low = (table - high.astype(np.float64)).astype(jnp.bfloat16)
    r = np.arange(HALF + 1)[:, None]

    def waves(steps):
        angle = 2 * np.pi * steps / lon_cells
        pairs = np.stack([np.cos(angle), np.sin(angle)], axis=1)
        return pairs.reshape(-1, steps.shape[1]).astype(np.float32)

    phase = waves(r * np.arange(padded)[None, :])
    wave = waves(RADIX * q[None, :] + r)
    return phase, wave, high, low


SMALL, WHOLE, UNREAD = pltpu.SMEM, pltpu.VMEM, pl.ANY


def call(kernel, outs, operands, scratch=(), sems=0, place=None, aliases=None):
    return pl.pallas_call(
        kernel,
        out_shape=[jax.ShapeDtypeStruct(shape, jnp.float32) for shape in outs],
        in_specs=[pl.BlockSpec(memory_space=place) for _, place in operands],
        out_specs=[pl.BlockSpec(memory_space=place or WHOLE)] * len(outs),
        input_output_aliases=aliases or {},
        scratch_shapes=[pltpu.VMEM(shape, jnp.float32) for shape in scratch]
        + ([pltpu.SemaphoreType.DMA((sems,))] if sems else []),
        compiler_params=pltpu.CompilerParams(vmem_limit_bytes=24 << 20),
        cost_estimate=pl.CostEstimate(flops=1, bytes_accessed=1, transcendentals=0),
    )(*[v for v, _ in operands])


def whole(*values):
    return [(v, WHOLE) for v in values]


def body(tracers, merid_courant, zonal_shift, zonal_fraction, cutoff, damping):
    tracer_count, level_count, row_count, column_count = tracers.shape
    lat_count = lax.axis_size("lat")
    lon_count = lax.axis_size("lon")
    assert lon_count == PAIR * PAIR and tracer_count % PAIR == 0 and row_count > 2
    share = tracer_count // PAIR
    lon_cells = column_count * lon_count
    phase, wave, high, low = [jnp.asarray(t) for t in filter_tables(lon_cells)]
    padded, double = high.shape
    width = -(-column_count // LANES) * LANES
    assert column_count - lon_cells // RADIX + padded <= width
    group = level_count * 2 * (HALF + 1)
    shift_rows, fraction_rows = zonal_shift.T, zonal_fraction.T

    def swap_core(value):
        return lax.ppermute(value, "lon", [(p, p ^ 1) for p in range(lon_count)])

    quarter = lat_count // 4
    caps = [b for b in range(lat_count) if b < quarter or b >= lat_count - quarter]

    def swap_half(message, rim):
        def pairs(bands):
            return [(b * lon_count + p, b * lon_count + (p ^ 2)) for b in bands for p in range(lon_count)]

        others = [b for b in range(lat_count) if b not in caps]
        axes = ("lat", "lon")
        return lax.ppermute(message, axes, pairs(caps)), lax.ppermute(rim, axes, pairs(others))

    def swap_band(value, first):
        pairs = []
        for b in range(first, lat_count - 1, 2):
            pairs += [(b, b + 1), (b + 1, b)]
        return lax.ppermute(value, "lat", pairs)

    def set_shape(number):
        return (share, number, level_count, column_count)

    def forward(mine, theirs, after, *relay):
        count = mine.shape[0] * mine.shape[1]
        message_shape = (count, level_count, 2 * MODES + LANES)
        return call(
            forward_kernel,
            [message_shape, (PAIR, count, level_count, width), (count, level_count, LANES)]
            + [v.shape for v in relay],
            whole(mine, theirs, phase, high, low) + [(after, UNREAD)] + whole(*relay),
            [(count * group, padded)],
        )

    def shifted(which, held, after):
        count = held.shape[1]
        return call(
            functools.partial(shift_kernel, which, column_count),
            [(count, PAIR, level_count, width)],
            whole(distance, fraction, held) + [(after, UNREAD)],
        )

    def inverse(which, held, moved, own, others, after):
        count = held.shape[1]
        return call(
            functools.partial(inverse_kernel, which, column_count),
            [set_shape(count // share)] * 2,
            whole(distance, fraction, keep, gain, phase, high, low, held, moved, own, *others)
            + [(after, UNREAD)],
            [(count * group, padded), (count * group, double), (PAIR, count, level_count, width)],
        )

    edge_shape = ((tracer_count + 1) * level_count, column_count)
    part_shape = (tracer_count, level_count, column_count)
    inner_mine, inner_send, near_edge, far_edge, near_part, far_part = call(
        begin_kernel,
        [set_shape(row_count - 2)] * 2 + [edge_shape] * 2 + [part_shape] * 2,
        [(pltpu.with_memory_space_constraint(v, pltpu.HBM), pltpu.HBM) for v in (tracers, merid_courant)],
        [tracers.shape, merid_courant.shape],
        tracer_count + 1,
    )
    inner_theirs = swap_core(inner_send)
    near_got = swap_band(near_edge, 0)
    inner_own, inner_held, inner_rim, far_relay = forward(inner_mine, inner_theirs, near_part, far_edge)
    far_got = swap_band(far_relay, 1)
    inner_others = swap_half(inner_own, inner_rim)
    row_shape = (row_count, level_count, LANES)
    distance, fraction, keep, gain = call(
        functools.partial(row_kernel, column_count),
        [row_shape] * 3 + [(row_count, 2 * (HALF + 1), level_count, double // 2)],
        [(v, SMALL) for v in (shift_rows, fraction_rows, cutoff, damping)]
        + whole(wave)
        + [(inner_own, UNREAD)],
    )
    (inner_moved,) = shifted("inner", inner_held, inner_own)

    near_mine, near_send = call(
        functools.partial(edge_kernel, True),
        [set_shape(1)] * 2,
        whole(near_edge, near_got, near_part) + [(inner_moved, UNREAD)],
    )
    near_theirs = swap_core(near_send)
    near_own, near_held, near_rim = forward(near_mine, near_theirs, inner_moved)
    near_others = swap_half(near_own, near_rim)
    (near_moved,) = shifted("near", near_held, near_own)
    inner = inverse("inner", inner_held, inner_moved, inner_own, inner_others, near_moved)
    inner_back = swap_core(inner[1])

    far_mine, far_send = call(
        functools.partial(edge_kernel, False),
        [set_shape(1)] * 2,
        whole(far_edge, far_got, far_part) + [(inner[0], UNREAD)],
    )
    far_theirs = swap_core(far_send)
    near = inverse("near", near_held, near_moved, near_own, near_others, far_mine)
    near_back = swap_core(near[1])
    far_own, far_held, far_rim = forward(far_mine, far_theirs, near[0])
    far_others = swap_half(far_own, far_rim)
    (far_moved,) = shifted("far", far_held, far_own)
    far = inverse("far", far_held, far_moved, far_own, far_others, far_moved)
    far_back = swap_core(far[1])
    (half_done,) = call(
        functools.partial(end_kernel, 0),
        [tracers.shape],
        whole(inner[0], near[0], far[0]),
        [(share,) + tracers.shape[1:]],
        share,
        pltpu.HBM,
    )
    (result,) = call(
        functools.partial(end_kernel, 1),
        [tracers.shape],
        whole(inner_back, near_back, far_back) + [(half_done, pltpu.HBM)],
        [(share,) + tracers.shape[1:]],
        share,
        pltpu.HBM,
        {3: 0},
    )
    return result


def solution(mesh):
    placed = (
        P(None, None, "lat", "lon"),
        P(None, "lat", "lon"),
        P(None, "lat"),
        P(None, "lat"),
        P(),
        P(),
    )
    return jax.shard_map(
        body, mesh=mesh, in_specs=placed, out_specs=P(None, None, "lat", "lon"), check_vma=False
    )
```

```python
import functools
import math

import jax
import jax.numpy as jnp
import numpy as np
from jax import lax
from jax.experimental import pallas as pl
from jax.experimental.pallas import tpu as pltpu
from jax.sharding import PartitionSpec as P

MODES = 1024
SMAX = 64
RADIX = 16
HALF = RADIX // 2
LANES = 128
PAIR = 2


def times_phase(value, numerator, denominator):
    re, im = value
    eighth = (8 * numerator % (8 * denominator)) / denominator
    if eighth == 0:
        return re, im
    if eighth == 2:
        return -im, re
    if eighth == 4:
        return -re, -im
    if eighth == 6:
        return im, -re
    c = math.cos(2 * math.pi * numerator / denominator)
    s = math.sin(2 * math.pi * numerator / denominator)
    if eighth == 7:
        return (re + im) * c, (im - re) * c
    if eighth == 1:
        return (re - im) * c, (re + im) * c
    return re * c - im * s, re * s + im * c


def real_dft(values):
    n = len(values)
    if n == 2:
        return [(values[0] + values[1], None), (values[0] - values[1], None)]
    even, odd = real_dft(values[0::2]), real_dft(values[1::2])
    out = [None] * (n // 2 + 1)
    for r in range(n // 4 + 1):
        (er, ei), (tr, ti) = even[r], odd[r]
        if r == 0:
            out[0] = (er + tr, None)
            out[n // 2] = (er - tr, None)
        elif r == n // 4:
            out[r] = (er, -tr)
        else:
            tr, ti = times_phase((tr, ti), -r, n)
            out[r] = (er + tr, ei + ti)
            out[n // 2 - r] = (er - tr, ti - ei)
    return out


def real_inverse(spectrum):
    n = 2 * (len(spectrum) - 1)
    if n == 2:
        a, b = spectrum[0][0], spectrum[1][0]
        return [a + b, a - b]
    even, odd = [None] * (n // 4 + 1), [None] * (n // 4 + 1)
    for r in range(n // 4 + 1):
        (ar, ai), (br, bi) = spectrum[r], spectrum[n // 2 - r]
        if r == 0:
            even[0] = (ar + br, None)
            odd[0] = (ar - br, None)
        elif r == n // 4:
            even[r] = (ar + ar, None)
            odd[r] = (-(ai + ai), None)
        else:
            even[r] = (ar + br, ai - bi)
            odd[r] = times_phase((ar - br, ai + bi), r, n)
    out = [None] * n
    out[0::2] = real_inverse(even)
    out[1::2] = real_inverse(odd)
    return out


def four(values, sign):
    (ar, ai), (br, bi), (cr, ci), (dr, di) = values
    pr, pi, mr, mi = ar + cr, ai + ci, ar - cr, ai - ci
    qr, qi, nr, ni = br + dr, bi + di, br - dr, bi - di
    if sign > 0:
        nr, ni = -nr, -ni
    return [(pr + qr, pi + qi), (mr + ni, mi - nr), (pr - qr, pi - qi), (mr - ni, mi + nr)]


def half_dft(x):
    out = [None] * 9
    out[0::2] = real_dft(x)
    odd = four([times_phase((x[v], -x[v + 4]), -v, 16) for v in range(4)], -1)
    out[1], out[5] = odd[0], odd[1]
    out[7] = (odd[2][0], -odd[2][1])
    out[3] = (odd[3][0], -odd[3][1])
    return out


def half_inverse(w):
    even = real_inverse(w[0::2])
    odd = four([w[1], w[5], (w[7][0], -w[7][1]), (w[3][0], -w[3][1])], 1)
    odd = [times_phase(value, v, 16) for v, value in enumerate(odd)]
    return [even[v] + odd[v][0] for v in range(4)] + [even[v + 4] - odd[v][1] for v in range(4)]


def split(value):
    high = value.astype(jnp.bfloat16)
    return high, (value - high.astype(jnp.float32)).astype(jnp.bfloat16)


def product(left, table_high, table_low, side):
    high, low = split(left)

    def dot(x, y):
        return lax.dot_general(x, y, (((1,), (side,)), ((), ())), preferred_element_type=jnp.float32)

    return dot(high, table_high) + (dot(high, table_low) + dot(low, table_high))


def spans(columns, width):
    return [slice(start, min(start + width, columns)) for start in range(0, columns, width)]


def is_cap(lat):
    count = lax.axis_size("lat")
    return (lat < count // 4) | (lat >= count - count // 4)


def flux_of(face_speed, south, north):
    return jnp.maximum(face_speed, 0.0) * south + jnp.minimum(face_speed, 0.0) * north


def near_is_north():
    return lax.rem(lax.axis_index("lat"), 2) == 0


def begin_kernel(
    cells_hbm, speed_hbm, mine_ref, send_ref, near_ref, far_ref, near_part_ref, far_part_ref,
    cells_ref, speed_ref, sems,
):
    tracer_count, levels, row_count, columns = cells_ref.shape
    share = tracer_count // PAIR
    core = lax.rem(lax.axis_index("lon"), PAIR)
    north = near_is_north()
    loads = [pltpu.make_async_copy(speed_hbm, speed_ref, sems.at[tracer_count])]
    owners = []
    for slot in range(tracer_count):
        place, i = divmod(slot, share)
        owners.append(lax.rem(core + place, PAIR) * share + i)
        loads.append(pltpu.make_async_copy(cells_hbm.at[owners[-1]], cells_ref.at[slot], sems.at[slot]))
    for load in loads:
        load.start()
    loads[0].wait()
    near_ref[tracer_count * levels :] = speed_ref[:, 0]
    far_ref[tracer_count * levels :] = speed_ref[:, 0]
    for slot, t in enumerate(owners):
        loads[slot + 1].wait()
        out_ref, i = (mine_ref, send_ref)[slot // share], slot % share
        place = pl.ds(pl.multiple_of(t * levels, levels), levels)
        for lanes in spans(columns, 3 * LANES):
            speed = [speed_ref[:, j, lanes] for j in range(row_count)]
            x = [cells_ref[slot, :, j, lanes] for j in range(row_count)]
            flux = [flux_of(speed[j], x[j - 1], x[j]) for j in range(1, row_count)]
            for j in range(1, row_count - 1):
                out_ref[i, j - 1, :, lanes] = x[j] + flux[j - 1] - flux[j]
            near_ref[place, lanes] = jnp.where(north, x[-1], x[0])
            far_ref[place, lanes] = jnp.where(north, x[0], x[-1])
            south_part, north_part = x[0] - flux[0], x[-1] + flux[-1]
            near_part_ref[t, :, lanes] = jnp.where(north, north_part, south_part)
            far_part_ref[t, :, lanes] = jnp.where(north, south_part, north_part)


def edge_kernel(is_near, own_ref, got_ref, part_ref, after_ref, mine_ref, send_ref):
    tracer_count, levels, columns = part_ref.shape
    share = tracer_count // PAIR
    total = tracer_count * levels
    core = lax.rem(lax.axis_index("lon"), PAIR)
    lat = lax.axis_index("lat")
    north = near_is_north() if is_near else jnp.logical_not(near_is_north())
    wall = jnp.where(north, lat == lax.axis_size("lat") - 1, lat == 0)
    for lanes in spans(columns, 3 * LANES):
        speed = jnp.where(north, got_ref[total:, lanes], own_ref[total:, lanes])
        speed = jnp.where(wall, 0.0, speed)
        for which, out_ref in enumerate([mine_ref, send_ref]):
            for i in range(share):
                t = lax.rem(core + which, PAIR) * share + i
                place = pl.ds(pl.multiple_of(t * levels, levels), levels)
                own, got = own_ref[place, lanes], got_ref[place, lanes]
                flux = flux_of(speed, jnp.where(north, own, got), jnp.where(north, got, own))
                out_ref[i, 0, :, lanes] = part_ref[t, :, lanes] + jnp.where(north, -flux, flux)


def forward_kernel(
    mine_ref, theirs_ref, phase_ref, high_ref, low_ref, after_ref, message_ref, held_ref, stack_ref
):
    share, number, levels, columns = mine_ref.shape
    piece = columns * PAIR // HALF
    padded = stack_ref.shape[1]
    modes = high_ref.shape[1] // 2
    group = levels * 2 * (HALF + 1)
    core = lax.rem(lax.axis_index("lon"), PAIR)
    count = share * number
    for n in range(count):
        i, j = divmod(n, number)
        held_ref[core, n, :, :columns] = mine_ref[i, j]
        held_ref[1 - core, n, :, :columns] = theirs_ref[i, j]
        for pos in range(PAIR):
            held_ref[pos, n, :, columns:] = jnp.zeros((levels, held_ref.shape[3] - columns), jnp.float32)
        message_ref[n, :, 2 * MODES :] = held_ref[PAIR - 1, n, :, columns - LANES : columns]

    @pl.when(is_cap(lax.axis_index("lat")))
    def _():
        for n in range(count):
            for tile in range(0, padded, LANES):
                lanes = slice(tile, tile + LANES)
                x = []
                for u in range(HALF):
                    pos, start = divmod(u * piece, columns)
                    x.append(held_ref[pos, n, :, start + tile : start + tile + LANES])
                for r, (re, im) in enumerate(half_dft(x)):
                    base = n * group + 2 * r * levels
                    if r == 0:
                        im = jnp.zeros_like(re)
                    else:
                        c, s = phase_ref[2 * r : 2 * r + 1, lanes], phase_ref[2 * r + 1 : 2 * r + 2, lanes]
                        if im is None:
                            re, im = re * c, -(re * s)
                        else:
                            re, im = re * c + im * s, im * c - re * s
                    stack_ref[base : base + levels, lanes] = re
                    stack_ref[base + levels : base + 2 * levels, lanes] = im
        coeffs = product(stack_ref[...], high_ref[...], low_ref[...], 0)
        upper = lax.broadcasted_iota(jnp.int32, (levels, modes), 1) >= modes // 2
        for n in range(count):
            first = None
            for r in [0, HALF] + list(range(1, HALF)):
                base = n * group + 2 * r * levels
                re, im = coeffs[base : base + levels], coeffs[base + levels : base + 2 * levels]
                x_re = re[:, :modes] + im[:, modes:]
                x_im = im[:, :modes] - re[:, modes:]
                if r == 0:
                    first = x_re, x_im
                    continue
                slot = r
                if r == HALF:
                    x_re = jnp.where(upper, first[0], pltpu.roll(x_re, modes // 2, 1))
                    x_im = jnp.where(upper, first[1], pltpu.roll(x_im, modes // 2, 1))
                    slot = 0
                message_ref[n, :, 2 * slot * modes : (2 * slot + 1) * modes] = x_re
                message_ref[n, :, (2 * slot + 1) * modes : (2 * slot + 2) * modes] = x_im


def row_vector(ref, row, levels):
    level = lax.broadcasted_iota(jnp.int32, (levels, LANES), 0)
    out = jnp.full((levels, LANES), ref[row, 0])
    for i in range(1, levels):
        out = jnp.where(level == i, ref[row, i], out)
    return out


def displaced(tiles, distance, share):
    lane = lax.broadcasted_iota(jnp.int32, distance.shape, 1)

    def moved(steps):
        index = (lane - steps) & (LANES - 1)
        turned = [jnp.take_along_axis(v, index, axis=1, mode="promise_in_bounds") for v in tiles]
        from_left = lane < steps
        return [jnp.where(from_left, a, b) for a, b in zip(turned, turned[1:])]

    pairs = zip(moved(distance), moved(distance + 1))
    return [(1.0 - share) * here + share * earlier for here, earlier in pairs]


def rows_of(which, row_count):
    if which == "inner":
        return list(range(1, row_count - 1))
    north = near_is_north() if which == "near" else jnp.logical_not(near_is_north())
    return [jnp.where(north, row_count - 1, 0)]


def wave_angle(steps, lon_cells):
    steps = lax.rem(steps, lon_cells)
    return steps.astype(jnp.float32) * (2.0 * math.pi / lon_cells)


def row_kernel(
    columns, shift_ref, fraction_ref, cutoff_ref, damping_ref, wave_ref, after_ref, source_ref,
    distance_ref, share_ref, keep_ref, gain_ref, relay_ref,
):
    relay_ref[...] = source_ref[...]
    row_count, levels = shift_ref.shape
    lon_cells = columns * PAIR * PAIR
    modes = gain_ref.shape[3]
    lat = lax.axis_index("lat")
    for row in range(row_count):
        distance_ref[row] = row_vector(shift_ref, row, levels).astype(jnp.float32)
        share_ref[row] = row_vector(fraction_ref, row, levels)
        keep_ref[row] = jnp.full((levels, LANES), damping_ref[lat * row_count + row])

    @pl.when(is_cap(lat))
    def _():
        lane = lax.broadcasted_iota(jnp.int32, (levels, modes), 1)
        mode = lane - modes // 2
        for row in range(row_count):
            distance = distance_ref[row].astype(jnp.int32)
            share = share_ref[row]
            limit = cutoff_ref[lat * row_count + row]
            wide = wave_angle(RADIX * mode * distance, lon_cells)
            wide_re, wide_im = jnp.cos(wide), -jnp.sin(wide)
            fine = wave_angle(lane * distance, lon_cells)
            fine_re, fine_im = jnp.cos(fine), -jnp.sin(fine)
            for r in range(HALF + 1):
                wavenumber = RADIX * mode + r
                kept = jnp.abs(wavenumber) <= limit
                if r in (0, HALF):
                    kept = kept & (wavenumber >= 0)
                once = r % 2 == 0 and r not in (0, HALF)
                weight = jnp.full((levels, modes), (1.0 if once else 2.0) / lon_cells)
                if r == 0:
                    weight = jnp.where(wavenumber == 0, 1.0 / lon_cells, weight)
                weight = jnp.where(kept, weight, 0.0)
                mix_re = (1.0 - share) + share * wave_ref[2 * r : 2 * r + 1]
                mix_im = -share * wave_ref[2 * r + 1 : 2 * r + 2]
                turn_re, turn_im = fine_re[:, r : r + 1], fine_im[:, r : r + 1]
                re, im = wide_re * turn_re - wide_im * turn_im, wide_re * turn_im + wide_im * turn_re
                gain_ref[row, 2 * r] = (re * mix_re - im * mix_im) * weight
                gain_ref[row, 2 * r + 1] = (re * mix_im + im * mix_re) * weight


def shift_kernel(which, columns, distance_ref, share_ref, held_ref, after_ref, moved_ref):
    _, count, levels, padded = held_ref.shape
    rows = rows_of(which, share_ref.shape[0])
    number = len(rows)
    for j, row in enumerate(rows):
        distance, share = distance_ref[row].astype(jnp.int32), share_ref[row]
        for n in range(j, count, number):
            for pos in range(PAIR):
                tiles = [held_ref[PAIR - 1 - pos, n, :, columns - LANES : columns]]
                tiles += [held_ref[pos, n, :, lanes] for lanes in spans(padded, LANES)]
                for lanes, tile in zip(spans(padded, LANES), displaced(tiles, distance, share)):
                    moved_ref[n, pos, :, lanes] = tile


def inverse_kernel(
    which, columns, distance_ref, share_ref, keep_ref, gain_ref, phase_ref, high_ref, low_ref,
    held_ref, moved_ref, own_ref, other_ref, after_ref, mine_ref, send_ref,
    stack_ref, back_ref, pair_ref,
):
    _, count, levels, _ = held_ref.shape
    rows = rows_of(which, share_ref.shape[0])
    number = len(rows)
    piece = columns * PAIR // HALF
    padded = stack_ref.shape[1]
    modes = gain_ref.shape[3]
    group = levels * 2 * (HALF + 1)
    core = lax.rem(lax.axis_index("lon"), PAIR)
    cap = is_cap(lax.axis_index("lat"))
    for j, row in enumerate(rows):
        distance, share = distance_ref[row].astype(jnp.int32), share_ref[row]
        for n in range(j, count, number):
            tiles = [other_ref[n, :, 2 * MODES :], held_ref[0, n, :, :LANES]]
            (moved_ref[n, 0, :, :LANES],) = displaced(tiles, distance, share)

    @pl.when(jnp.logical_not(cap))
    def _():
        for n in range(count):
            i, j = divmod(n, number)
            mine_ref[i, j] = moved_ref[n, core, :, :columns]
            send_ref[i, j] = moved_ref[n, 1 - core, :, :columns]

    @pl.when(cap)
    def _():
        for n in range(count):
            row = rows[n % number]
            for r in range(HALF + 1):
                slot = r % HALF
                ours, theirs = (
                    [ref[n, :, (2 * slot + part) * modes : (2 * slot + part + 1) * modes] for part in range(2)]
                    for ref in (own_ref, other_ref)
                )
                if r % 2:
                    re, im = ours[0] - theirs[0], ours[1] - theirs[1]
                else:
                    re, im = ours[0] + theirs[0], ours[1] + theirs[1]
                if r == HALF:
                    re, im = pltpu.roll(re, modes // 2, 1), pltpu.roll(im, modes // 2, 1)
                g_re, g_im = gain_ref[row, 2 * r], gain_ref[row, 2 * r + 1]
                re, im = re * g_re - im * g_im, re * g_im + im * g_re
                base = n * group + 2 * r * levels
                back_ref[base : base + levels, :modes] = re
                back_ref[base : base + levels, modes:] = -im
                back_ref[base + levels : base + 2 * levels, :modes] = im
                back_ref[base + levels : base + 2 * levels, modes:] = re
        stack_ref[...] = product(back_ref[...], high_ref[...], low_ref[...], 1)
        for n in range(count):
            i, j = divmod(n, number)
            keep = keep_ref[rows[j]]
            for tile in range(0, padded, LANES):
                lanes = slice(tile, tile + LANES)
                spectrum = []
                for r in range(HALF + 1):
                    base = n * group + 2 * r * levels
                    re = stack_ref[base : base + levels, lanes]
                    im = stack_ref[base + levels : base + 2 * levels, lanes]
                    if r > 0:
                        c, s = phase_ref[2 * r : 2 * r + 1, lanes], phase_ref[2 * r + 1 : 2 * r + 2, lanes]
                        re, im = re * c - im * s, re * s + im * c
                    spectrum.append((re, im))
                width = min(LANES, piece - tile)
                for u, value in enumerate(half_inverse(spectrum)):
                    pos, start = divmod(u * piece, columns)
                    start += tile
                    shifted = moved_ref[n, pos, :, start : start + LANES]
                    result = keep * shifted + (1.0 - keep) * value
                    pair_ref[pos, n, :, start : start + width] = result[:, :width]
        for n in range(count):
            i, j = divmod(n, number)
            mine_ref[i, j] = pair_ref[core, n, :, :columns]
            send_ref[i, j] = pair_ref[1 - core, n, :, :columns]


def end_kernel(place, inner, near, far, *refs):
    out_hbm, out_ref, sems = refs[-3:]
    share, levels, row_count, columns = out_ref.shape
    core = lax.rem(lax.axis_index("lon"), PAIR)
    north = near_is_north()
    copies = []
    for i in range(share):
        for lanes in spans(columns, 4 * LANES):
            a, b = near[i, 0, :, lanes], far[i, 0, :, lanes]
            out_ref[i, :, 0, lanes] = jnp.where(north, b, a)
            out_ref[i, :, row_count - 1, lanes] = jnp.where(north, a, b)
            for j in range(1, row_count - 1):
                out_ref[i, :, j, lanes] = inner[i, j - 1, :, lanes]
        t = lax.rem(core + place, PAIR) * share + i
        copies.append(pltpu.make_async_copy(out_ref.at[i], out_hbm.at[t], sems.at[i]))
        copies[-1].start()
    for copy in copies:
        copy.wait()


def filter_tables(lon_cells):
    piece = lon_cells // RADIX
    padded = -(-piece // LANES) * LANES
    modes = 2 * MODES // RADIX
    q = np.arange(modes) - modes // 2
    angle = 2 * np.pi * (np.arange(piece)[:, None] * q[None, :] % piece) / piece
    table = np.zeros((padded, 2 * modes))
    table[:piece, :modes] = np.cos(angle)
    table[:piece, modes:] = np.sin(angle)
    high = table.astype(jnp.bfloat16)
    low = (table - high.astype(np.float64)).astype(jnp.bfloat16)
    r = np.arange(HALF + 1)[:, None]

    def waves(steps):
        angle = 2 * np.pi * steps / lon_cells
        pairs = np.stack([np.cos(angle), np.sin(angle)], axis=1)
        return pairs.reshape(-1, steps.shape[1]).astype(np.float32)

    phase = waves(r * np.arange(padded)[None, :])
    wave = waves(RADIX * q[None, :] + r)
    return phase, wave, high, low


SMALL, WHOLE, UNREAD = pltpu.SMEM, pltpu.VMEM, pl.ANY


def call(kernel, outs, operands, scratch=(), sems=0, place=None, aliases=None):
    return pl.pallas_call(
        kernel,
        out_shape=[jax.ShapeDtypeStruct(shape, jnp.float32) for shape in outs],
        in_specs=[pl.BlockSpec(memory_space=place) for _, place in operands],
        out_specs=[pl.BlockSpec(memory_space=place or WHOLE)] * len(outs),
        input_output_aliases=aliases or {},
        scratch_shapes=[pltpu.VMEM(shape, jnp.float32) for shape in scratch]
        + ([pltpu.SemaphoreType.DMA((sems,))] if sems else []),
        compiler_params=pltpu.CompilerParams(vmem_limit_bytes=24 << 20),
        cost_estimate=pl.CostEstimate(flops=1, bytes_accessed=1, transcendentals=0),
    )(*[v for v, _ in operands])


def whole(*values):
    return [(v, WHOLE) for v in values]


def body(tracers, merid_courant, zonal_shift, zonal_fraction, cutoff, damping):
    tracer_count, level_count, row_count, column_count = tracers.shape
    lat_count = lax.axis_size("lat")
    lon_count = lax.axis_size("lon")
    assert lon_count == PAIR * PAIR and tracer_count % PAIR == 0 and row_count > 2
    share = tracer_count // PAIR
    lon_cells = column_count * lon_count
    phase, wave, high, low = [jnp.asarray(t) for t in filter_tables(lon_cells)]
    padded, double = high.shape
    width = -(-column_count // LANES) * LANES
    assert column_count - lon_cells // RADIX + padded <= width
    group = level_count * 2 * (HALF + 1)
    shift_rows, fraction_rows = zonal_shift.T, zonal_fraction.T

    def swap_core(value):
        return lax.ppermute(value, "lon", [(p, p ^ 1) for p in range(lon_count)])

    def swap_half(value):
        return lax.ppermute(value, "lon", [(p, p ^ 2) for p in range(lon_count)])

    def swap_band(value, first):
        pairs = [(b, b) for b in range(first)]
        for b in range(first, lat_count - 1, 2):
            pairs += [(b, b + 1), (b + 1, b)]
        pairs += [(b, b) for b in range(len(pairs), lat_count)]
        return lax.ppermute(value, "lat", pairs)

    def set_shape(number):
        return (share, number, level_count, column_count)

    def forward(mine, theirs, after):
        count = mine.shape[0] * mine.shape[1]
        message_shape = (count, level_count, 2 * MODES + LANES)
        return call(
            forward_kernel,
            [message_shape, (PAIR, count, level_count, width)],
            whole(mine, theirs, phase, high, low) + [(after, UNREAD)],
            [(count * group, padded)],
        )

    def shifted(which, held, after):
        count = held.shape[1]
        return call(
            functools.partial(shift_kernel, which, column_count),
            [(count, PAIR, level_count, width)],
            whole(distance, fraction, held) + [(after, UNREAD)],
        )

    def inverse(which, held, moved, own, other, after):
        count = held.shape[1]
        return call(
            functools.partial(inverse_kernel, which, column_count),
            [set_shape(count // share)] * 2,
            whole(distance, fraction, keep, gain, phase, high, low, held, moved, own, other)
            + [(after, UNREAD)],
            [(count * group, padded), (count * group, double), (PAIR, count, level_count, width)],
        )

    edge_shape = ((tracer_count + 1) * level_count, column_count)
    part_shape = (tracer_count, level_count, column_count)
    inner_mine, inner_send, near_edge, far_edge, near_part, far_part = call(
        begin_kernel,
        [set_shape(row_count - 2)] * 2 + [edge_shape] * 2 + [part_shape] * 2,
        [(pltpu.with_memory_space_constraint(v, pltpu.HBM), pltpu.HBM) for v in (tracers, merid_courant)],
        [tracers.shape, merid_courant.shape],
        tracer_count + 1,
    )
    inner_theirs = swap_core(inner_send)
    near_got = swap_band(near_edge, 0)
    inner_own, inner_held = forward(inner_mine, inner_theirs, near_part)
    inner_other = swap_half(inner_own)
    row_shape = (row_count, level_count, LANES)
    distance, fraction, keep, gain, far_relay = call(
        functools.partial(row_kernel, column_count),
        [row_shape] * 3 + [(row_count, 2 * (HALF + 1), level_count, double // 2), edge_shape],
        [(v, SMALL) for v in (shift_rows, fraction_rows, cutoff, damping)]
        + whole(wave)
        + [(inner_own, UNREAD)]
        + whole(far_edge),
    )
    far_got = swap_band(far_relay, 1)
    (inner_moved,) = shifted("inner", inner_held, inner_own)

    near_mine, near_send = call(
        functools.partial(edge_kernel, True),
        [set_shape(1)] * 2,
        whole(near_edge, near_got, near_part) + [(inner_moved, UNREAD)],
    )
    near_theirs = swap_core(near_send)
    near_own, near_held = forward(near_mine, near_theirs, inner_moved)
    near_other = swap_half(near_own)
    (near_moved,) = shifted("near", near_held, near_own)
    inner = inverse("inner", inner_held, inner_moved, inner_own, inner_other, near_moved)
    inner_back = swap_core(inner[1])

    far_mine, far_send = call(
        functools.partial(edge_kernel, False),
        [set_shape(1)] * 2,
        whole(far_edge, far_got, far_part) + [(inner[0], UNREAD)],
    )
    far_theirs = swap_core(far_send)
    near = inverse("near", near_held, near_moved, near_own, near_other, far_mine)
    near_back = swap_core(near[1])
    far_own, far_held = forward(far_mine, far_theirs, near[0])
    far_other = swap_half(far_own)
    (far_moved,) = shifted("far", far_held, far_own)
    far = inverse("far", far_held, far_moved, far_own, far_other, far_moved)
    far_back = swap_core(far[1])
    (half_done,) = call(
        functools.partial(end_kernel, 0),
        [tracers.shape],
        whole(inner[0], near[0], far[0]),
        [(share,) + tracers.shape[1:]],
        share,
        pltpu.HBM,
    )
    (result,) = call(
        functools.partial(end_kernel, 1),
        [tracers.shape],
        whole(inner_back, near_back, far_back) + [(half_done, pltpu.HBM)],
        [(share,) + tracers.shape[1:]],
        share,
        pltpu.HBM,
        {3: 0},
    )
    return result


def solution(mesh):
    placed = (
        P(None, None, "lat", "lon"),
        P(None, "lat", "lon"),
        P(None, "lat"),
        P(None, "lat"),
        P(),
        P(),
    )
    return jax.shard_map(
        body, mesh=mesh, in_specs=placed, out_specs=P(None, None, "lat", "lon"), check_vma=False
    )
```

```python
import functools
import math

import jax
import jax.numpy as jnp
import numpy as np
from jax import lax
from jax.experimental import pallas as pl
from jax.experimental.pallas import tpu as pltpu
from jax.sharding import PartitionSpec as P

MODES = 1024
SMAX = 64
RADIX = 16
HALF = RADIX // 2
LANES = 128
PAIR = 2


def times_phase(value, numerator, denominator):
    re, im = value
    eighth = (8 * numerator % (8 * denominator)) / denominator
    if eighth == 0:
        return re, im
    if eighth == 2:
        return -im, re
    if eighth == 4:
        return -re, -im
    if eighth == 6:
        return im, -re
    c = math.cos(2 * math.pi * numerator / denominator)
    s = math.sin(2 * math.pi * numerator / denominator)
    if eighth == 7:
        return (re + im) * c, (im - re) * c
    if eighth == 1:
        return (re - im) * c, (re + im) * c
    return re * c - im * s, re * s + im * c


def real_dft(values):
    n = len(values)
    if n == 2:
        return [(values[0] + values[1], None), (values[0] - values[1], None)]
    even, odd = real_dft(values[0::2]), real_dft(values[1::2])
    out = [None] * (n // 2 + 1)
    for r in range(n // 4 + 1):
        (er, ei), (tr, ti) = even[r], odd[r]
        if r == 0:
            out[0] = (er + tr, None)
            out[n // 2] = (er - tr, None)
        elif r == n // 4:
            out[r] = (er, -tr)
        else:
            tr, ti = times_phase((tr, ti), -r, n)
            out[r] = (er + tr, ei + ti)
            out[n // 2 - r] = (er - tr, ti - ei)
    return out


def real_inverse(spectrum):
    n = 2 * (len(spectrum) - 1)
    if n == 2:
        a, b = spectrum[0][0], spectrum[1][0]
        return [a + b, a - b]
    even, odd = [None] * (n // 4 + 1), [None] * (n // 4 + 1)
    for r in range(n // 4 + 1):
        (ar, ai), (br, bi) = spectrum[r], spectrum[n // 2 - r]
        if r == 0:
            even[0] = (ar + br, None)
            odd[0] = (ar - br, None)
        elif r == n // 4:
            even[r] = (ar + ar, None)
            odd[r] = (-(ai + ai), None)
        else:
            even[r] = (ar + br, ai - bi)
            odd[r] = times_phase((ar - br, ai + bi), r, n)
    out = [None] * n
    out[0::2] = real_inverse(even)
    out[1::2] = real_inverse(odd)
    return out


def four(values, sign):
    (ar, ai), (br, bi), (cr, ci), (dr, di) = values
    pr, pi, mr, mi = ar + cr, ai + ci, ar - cr, ai - ci
    qr, qi, nr, ni = br + dr, bi + di, br - dr, bi - di
    if sign > 0:
        nr, ni = -nr, -ni
    return [(pr + qr, pi + qi), (mr + ni, mi - nr), (pr - qr, pi - qi), (mr - ni, mi + nr)]


def half_dft(x):
    out = [None] * 9
    out[0::2] = real_dft(x)
    odd = four([times_phase((x[v], -x[v + 4]), -v, 16) for v in range(4)], -1)
    out[1], out[5] = odd[0], odd[1]
    out[7] = (odd[2][0], -odd[2][1])
    out[3] = (odd[3][0], -odd[3][1])
    return out


def half_inverse(w):
    even = real_inverse(w[0::2])
    odd = four([w[1], w[5], (w[7][0], -w[7][1]), (w[3][0], -w[3][1])], 1)
    odd = [times_phase(value, v, 16) for v, value in enumerate(odd)]
    return [even[v] + odd[v][0] for v in range(4)] + [even[v + 4] - odd[v][1] for v in range(4)]


def split(value):
    high = value.astype(jnp.bfloat16)
    return high, (value - high.astype(jnp.float32)).astype(jnp.bfloat16)


def product(left, table_high, table_low, side):
    high, low = split(left)

    def dot(x, y):
        return lax.dot_general(x, y, (((1,), (side,)), ((), ())), preferred_element_type=jnp.float32)

    return dot(high, table_high) + (dot(high, table_low) + dot(low, table_high))


def spans(columns, width):
    return [slice(start, min(start + width, columns)) for start in range(0, columns, width)]


def is_cap(lat):
    count = lax.axis_size("lat")
    return (lat < count // 4) | (lat >= count - count // 4)


def flux_of(face_speed, south, north):
    return jnp.maximum(face_speed, 0.0) * south + jnp.minimum(face_speed, 0.0) * north


def near_is_north():
    return lax.rem(lax.axis_index("lat"), 2) == 0


def begin_kernel(
    cells_hbm, speed_hbm, mine_ref, send_ref, near_ref, far_ref, near_part_ref, far_part_ref,
    cells_ref, speed_ref, sems,
):
    tracer_count, levels, row_count, columns = cells_ref.shape
    share = tracer_count // PAIR
    core = lax.rem(lax.axis_index("lon"), PAIR)
    north = near_is_north()
    loads = [pltpu.make_async_copy(speed_hbm, speed_ref, sems.at[tracer_count])]
    owners = []
    for slot in range(tracer_count):
        place, i = divmod(slot, share)
        owners.append(lax.rem(core + place, PAIR) * share + i)
        loads.append(pltpu.make_async_copy(cells_hbm.at[owners[-1]], cells_ref.at[slot], sems.at[slot]))
    for load in loads:
        load.start()
    loads[0].wait()
    near_ref[tracer_count * levels :] = speed_ref[:, 0]
    far_ref[tracer_count * levels :] = speed_ref[:, 0]
    for slot, t in enumerate(owners):
        loads[slot + 1].wait()
        out_ref, i = (mine_ref, send_ref)[slot // share], slot % share
        place = pl.ds(pl.multiple_of(t * levels, levels), levels)
        for lanes in spans(columns, 3 * LANES):
            speed = [speed_ref[:, j, lanes] for j in range(row_count)]
            x = [cells_ref[slot, :, j, lanes] for j in range(row_count)]
            flux = [flux_of(speed[j], x[j - 1], x[j]) for j in range(1, row_count)]
            for j in range(1, row_count - 1):
                out_ref[i, j - 1, :, lanes] = x[j] + flux[j - 1] - flux[j]
            near_ref[place, lanes] = jnp.where(north, x[-1], x[0])
            far_ref[place, lanes] = jnp.where(north, x[0], x[-1])
            south_part, north_part = x[0] - flux[0], x[-1] + flux[-1]
            near_part_ref[t, :, lanes] = jnp.where(north, north_part, south_part)
            far_part_ref[t, :, lanes] = jnp.where(north, south_part, north_part)


def edge_kernel(is_near, own_ref, got_ref, part_ref, after_ref, gain_ref, mine_ref, send_ref):
    tracer_count, levels, columns = part_ref.shape
    share = tracer_count // PAIR
    total = tracer_count * levels
    core = lax.rem(lax.axis_index("lon"), PAIR)
    lat = lax.axis_index("lat")
    north = near_is_north() if is_near else jnp.logical_not(near_is_north())
    wall = jnp.where(north, lat == lax.axis_size("lat") - 1, lat == 0)
    for lanes in spans(columns, 3 * LANES):
        speed = jnp.where(north, got_ref[total:, lanes], own_ref[total:, lanes])
        speed = jnp.where(wall, 0.0, speed)
        for which, out_ref in enumerate([mine_ref, send_ref]):
            for i in range(share):
                t = lax.rem(core + which, PAIR) * share + i
                place = pl.ds(pl.multiple_of(t * levels, levels), levels)
                own, got = own_ref[place, lanes], got_ref[place, lanes]
                flux = flux_of(speed, jnp.where(north, own, got), jnp.where(north, got, own))
                out_ref[i, 0, :, lanes] = part_ref[t, :, lanes] + jnp.where(north, -flux, flux)


def forward_kernel(
    mine_ref, theirs_ref, phase_ref, high_ref, low_ref, after_ref, message_ref, held_ref, stack_ref
):
    share, number, levels, columns = mine_ref.shape
    piece = columns * PAIR // HALF
    padded = stack_ref.shape[1]
    modes = high_ref.shape[1] // 2
    group = levels * 2 * (HALF + 1)
    core = lax.rem(lax.axis_index("lon"), PAIR)
    count = share * number
    for n in range(count):
        i, j = divmod(n, number)
        held_ref[core, n, :, :columns] = mine_ref[i, j]
        held_ref[1 - core, n, :, :columns] = theirs_ref[i, j]
        for pos in range(PAIR):
            held_ref[pos, n, :, columns:] = jnp.zeros((levels, held_ref.shape[3] - columns), jnp.float32)
        message_ref[n, :, 2 * MODES :] = held_ref[PAIR - 1, n, :, columns - LANES : columns]

    @pl.when(is_cap(lax.axis_index("lat")))
    def _():
        for n in range(count):
            for tile in range(0, padded, LANES):
                lanes = slice(tile, tile + LANES)
                x = []
                for u in range(HALF):
                    pos, start = divmod(u * piece, columns)
                    x.append(held_ref[pos, n, :, start + tile : start + tile + LANES])
                for r, (re, im) in enumerate(half_dft(x)):
                    base = n * group + 2 * r * levels
                    if r == 0:
                        im = jnp.zeros_like(re)
                    else:
                        c, s = phase_ref[2 * r : 2 * r + 1, lanes], phase_ref[2 * r + 1 : 2 * r + 2, lanes]
                        if im is None:
                            re, im = re * c, -(re * s)
                        else:
                            re, im = re * c + im * s, im * c - re * s
                    stack_ref[base : base + levels, lanes] = re
                    stack_ref[base + levels : base + 2 * levels, lanes] = im
        coeffs = product(stack_ref[...], high_ref[...], low_ref[...], 0)
        upper = lax.broadcasted_iota(jnp.int32, (levels, modes), 1) >= modes // 2
        for n in range(count):
            first = None
            for r in [0, HALF] + list(range(1, HALF)):
                base = n * group + 2 * r * levels
                re, im = coeffs[base : base + levels], coeffs[base + levels : base + 2 * levels]
                x_re = re[:, :modes] + im[:, modes:]
                x_im = im[:, :modes] - re[:, modes:]
                if r == 0:
                    first = x_re, x_im
                    continue
                slot = r
                if r == HALF:
                    x_re = jnp.where(upper, first[0], pltpu.roll(x_re, modes // 2, 1))
                    x_im = jnp.where(upper, first[1], pltpu.roll(x_im, modes // 2, 1))
                    slot = 0
                message_ref[n, :, 2 * slot * modes : (2 * slot + 1) * modes] = x_re
                message_ref[n, :, (2 * slot + 1) * modes : (2 * slot + 2) * modes] = x_im


def row_vector(ref, row, levels):
    level = lax.broadcasted_iota(jnp.int32, (levels, LANES), 0)
    out = jnp.full((levels, LANES), ref[row, 0])
    for i in range(1, levels):
        out = jnp.where(level == i, ref[row, i], out)
    return out


def displaced(tiles, distance, share):
    lane = lax.broadcasted_iota(jnp.int32, distance.shape, 1)

    def moved(steps):
        index = (lane - steps) & (LANES - 1)
        turned = [jnp.take_along_axis(v, index, axis=1, mode="promise_in_bounds") for v in tiles]
        from_left = lane < steps
        return [jnp.where(from_left, a, b) for a, b in zip(turned, turned[1:])]

    pairs = zip(moved(distance), moved(distance + 1))
    return [(1.0 - share) * here + share * earlier for here, earlier in pairs]


def rows_of(which, row_count):
    if which == "inner":
        return list(range(1, row_count - 1))
    north = near_is_north() if which == "near" else jnp.logical_not(near_is_north())
    return [jnp.where(north, row_count - 1, 0)]


def wave_angle(steps, lon_cells):
    steps = lax.rem(steps, lon_cells)
    return steps.astype(jnp.float32) * (2.0 * math.pi / lon_cells)


def row_kernel(
    shift_ref, fraction_ref, cutoff_ref, damping_ref, after_ref, source_ref,
    distance_ref, share_ref, keep_ref, limit_ref, relay_ref,
):
    relay_ref[...] = source_ref[...]
    row_count, levels = shift_ref.shape
    lat = lax.axis_index("lat")
    for row in range(row_count):
        distance_ref[row] = row_vector(shift_ref, row, levels).astype(jnp.float32)
        share_ref[row] = row_vector(fraction_ref, row, levels)
        keep_ref[row] = jnp.full((levels, LANES), damping_ref[lat * row_count + row])
        limit = jnp.full((levels, LANES), cutoff_ref[lat * row_count + row])
        limit_ref[row] = limit.astype(jnp.float32)


def gain_kernel(columns, distance_ref, share_ref, limit_ref, wave_ref, gain_ref):
    row_count, levels = distance_ref.shape[:2]
    lon_cells = columns * PAIR * PAIR
    modes = gain_ref.shape[3]
    lat = lax.axis_index("lat")

    @pl.when(is_cap(lat))
    def _():
        lane = lax.broadcasted_iota(jnp.int32, (levels, modes), 1)
        mode = lane - modes // 2
        for row in range(row_count):
            distance = distance_ref[row].astype(jnp.int32)
            share = share_ref[row]
            limit = limit_ref[row].astype(jnp.int32)
            wide = wave_angle(RADIX * mode * distance, lon_cells)
            wide_re, wide_im = jnp.cos(wide), -jnp.sin(wide)
            fine = wave_angle(lane * distance, lon_cells)
            fine_re, fine_im = jnp.cos(fine), -jnp.sin(fine)
            for r in range(HALF + 1):
                wavenumber = RADIX * mode + r
                kept = jnp.abs(wavenumber) <= limit
                if r in (0, HALF):
                    kept = kept & (wavenumber >= 0)
                once = r % 2 == 0 and r not in (0, HALF)
                weight = jnp.full((levels, modes), (1.0 if once else 2.0) / lon_cells)
                if r == 0:
                    weight = jnp.where(wavenumber == 0, 1.0 / lon_cells, weight)
                weight = jnp.where(kept, weight, 0.0)
                mix_re = (1.0 - share) + share * wave_ref[2 * r : 2 * r + 1]
                mix_im = -share * wave_ref[2 * r + 1 : 2 * r + 2]
                turn_re, turn_im = fine_re[:, r : r + 1], fine_im[:, r : r + 1]
                re, im = wide_re * turn_re - wide_im * turn_im, wide_re * turn_im + wide_im * turn_re
                gain_ref[row, 2 * r] = (re * mix_re - im * mix_im) * weight
                gain_ref[row, 2 * r + 1] = (re * mix_im + im * mix_re) * weight


def shift_kernel(which, columns, distance_ref, share_ref, held_ref, after_ref, moved_ref):
    _, count, levels, padded = held_ref.shape
    rows = rows_of(which, share_ref.shape[0])
    number = len(rows)
    for j, row in enumerate(rows):
        distance, share = distance_ref[row].astype(jnp.int32), share_ref[row]
        for n in range(j, count, number):
            for pos in range(PAIR):
                tiles = [held_ref[PAIR - 1 - pos, n, :, columns - LANES : columns]]
                tiles += [held_ref[pos, n, :, lanes] for lanes in spans(padded, LANES)]
                for lanes, tile in zip(spans(padded, LANES), displaced(tiles, distance, share)):
                    moved_ref[n, pos, :, lanes] = tile


def inverse_kernel(
    which, columns, distance_ref, share_ref, keep_ref, gain_ref, phase_ref, high_ref, low_ref,
    held_ref, moved_ref, own_ref, other_ref, after_ref, mine_ref, send_ref,
    stack_ref, back_ref, pair_ref,
):
    _, count, levels, _ = held_ref.shape
    rows = rows_of(which, share_ref.shape[0])
    number = len(rows)
    piece = columns * PAIR // HALF
    padded = stack_ref.shape[1]
    modes = gain_ref.shape[3]
    group = levels * 2 * (HALF + 1)
    core = lax.rem(lax.axis_index("lon"), PAIR)
    cap = is_cap(lax.axis_index("lat"))
    for j, row in enumerate(rows):
        distance, share = distance_ref[row].astype(jnp.int32), share_ref[row]
        for n in range(j, count, number):
            tiles = [other_ref[n, :, 2 * MODES :], held_ref[0, n, :, :LANES]]
            (moved_ref[n, 0, :, :LANES],) = displaced(tiles, distance, share)

    @pl.when(jnp.logical_not(cap))
    def _():
        for n in range(count):
            i, j = divmod(n, number)
            mine_ref[i, j] = moved_ref[n, core, :, :columns]
            send_ref[i, j] = moved_ref[n, 1 - core, :, :columns]

    @pl.when(cap)
    def _():
        for n in range(count):
            row = rows[n % number]
            for r in range(HALF + 1):
                slot = r % HALF
                ours, theirs = (
                    [ref[n, :, (2 * slot + part) * modes : (2 * slot + part + 1) * modes] for part in range(2)]
                    for ref in (own_ref, other_ref)
                )
                if r % 2:
                    re, im = ours[0] - theirs[0], ours[1] - theirs[1]
                else:
                    re, im = ours[0] + theirs[0], ours[1] + theirs[1]
                if r == HALF:
                    re, im = pltpu.roll(re, modes // 2, 1), pltpu.roll(im, modes // 2, 1)
                g_re, g_im = gain_ref[row, 2 * r], gain_ref[row, 2 * r + 1]
                re, im = re * g_re - im * g_im, re * g_im + im * g_re
                base = n * group + 2 * r * levels
                back_ref[base : base + levels, :modes] = re
                back_ref[base : base + levels, modes:] = -im
                back_ref[base + levels : base + 2 * levels, :modes] = im
                back_ref[base + levels : base + 2 * levels, modes:] = re
        stack_ref[...] = product(back_ref[...], high_ref[...], low_ref[...], 1)
        for n in range(count):
            i, j = divmod(n, number)
            keep = keep_ref[rows[j]]
            for tile in range(0, padded, LANES):
                lanes = slice(tile, tile + LANES)
                spectrum = []
                for r in range(HALF + 1):
                    base = n * group + 2 * r * levels
                    re = stack_ref[base : base + levels, lanes]
                    im = stack_ref[base + levels : base + 2 * levels, lanes]
                    if r > 0:
                        c, s = phase_ref[2 * r : 2 * r + 1, lanes], phase_ref[2 * r + 1 : 2 * r + 2, lanes]
                        re, im = re * c - im * s, re * s + im * c
                    spectrum.append((re, im))
                width = min(LANES, piece - tile)
                for u, value in enumerate(half_inverse(spectrum)):
                    pos, start = divmod(u * piece, columns)
                    start += tile
                    shifted = moved_ref[n, pos, :, start : start + LANES]
                    result = keep * shifted + (1.0 - keep) * value
                    pair_ref[pos, n, :, start : start + width] = result[:, :width]
        for n in range(count):
            i, j = divmod(n, number)
            mine_ref[i, j] = pair_ref[core, n, :, :columns]
            send_ref[i, j] = pair_ref[1 - core, n, :, :columns]


def end_kernel(place, inner, near, far, *refs):
    out_hbm, out_ref, sems = refs[-3:]
    share, levels, row_count, columns = out_ref.shape
    core = lax.rem(lax.axis_index("lon"), PAIR)
    north = near_is_north()
    copies = []
    for i in range(share):
        for lanes in spans(columns, 4 * LANES):
            a, b = near[i, 0, :, lanes], far[i, 0, :, lanes]
            out_ref[i, :, 0, lanes] = jnp.where(north, b, a)
            out_ref[i, :, row_count - 1, lanes] = jnp.where(north, a, b)
            for j in range(1, row_count - 1):
                out_ref[i, :, j, lanes] = inner[i, j - 1, :, lanes]
        t = lax.rem(core + place, PAIR) * share + i
        copies.append(pltpu.make_async_copy(out_ref.at[i], out_hbm.at[t], sems.at[i]))
        copies[-1].start()
    for copy in copies:
        copy.wait()


def filter_tables(lon_cells):
    piece = lon_cells // RADIX
    padded = -(-piece // LANES) * LANES
    modes = 2 * MODES // RADIX
    q = np.arange(modes) - modes // 2
    angle = 2 * np.pi * (np.arange(piece)[:, None] * q[None, :] % piece) / piece
    table = np.zeros((padded, 2 * modes))
    table[:piece, :modes] = np.cos(angle)
    table[:piece, modes:] = np.sin(angle)
    high = table.astype(jnp.bfloat16)
    low = (table - high.astype(np.float64)).astype(jnp.bfloat16)
    r = np.arange(HALF + 1)[:, None]

    def waves(steps):
        angle = 2 * np.pi * steps / lon_cells
        pairs = np.stack([np.cos(angle), np.sin(angle)], axis=1)
        return pairs.reshape(-1, steps.shape[1]).astype(np.float32)

    phase = waves(r * np.arange(padded)[None, :])
    wave = waves(RADIX * q[None, :] + r)
    return phase, wave, high, low


SMALL, WHOLE, UNREAD = pltpu.SMEM, pltpu.VMEM, pl.ANY


def call(kernel, outs, operands, scratch=(), sems=0, place=None, aliases=None):
    return pl.pallas_call(
        kernel,
        out_shape=[jax.ShapeDtypeStruct(shape, jnp.float32) for shape in outs],
        in_specs=[pl.BlockSpec(memory_space=place) for _, place in operands],
        out_specs=[pl.BlockSpec(memory_space=place or WHOLE)] * len(outs),
        input_output_aliases=aliases or {},
        scratch_shapes=[pltpu.VMEM(shape, jnp.float32) for shape in scratch]
        + ([pltpu.SemaphoreType.DMA((sems,))] if sems else []),
        compiler_params=pltpu.CompilerParams(vmem_limit_bytes=24 << 20),
        cost_estimate=pl.CostEstimate(flops=1, bytes_accessed=1, transcendentals=0),
    )(*[v for v, _ in operands])


def whole(*values):
    return [(v, WHOLE) for v in values]


def body(tracers, merid_courant, zonal_shift, zonal_fraction, cutoff, damping):
    tracer_count, level_count, row_count, column_count = tracers.shape
    lat_count = lax.axis_size("lat")
    lon_count = lax.axis_size("lon")
    assert lon_count == PAIR * PAIR and tracer_count % PAIR == 0 and row_count > 2
    share = tracer_count // PAIR
    lon_cells = column_count * lon_count
    phase, wave, high, low = [jnp.asarray(t) for t in filter_tables(lon_cells)]
    padded, double = high.shape
    width = -(-column_count // LANES) * LANES
    assert column_count - lon_cells // RADIX + padded <= width
    group = level_count * 2 * (HALF + 1)
    shift_rows, fraction_rows = zonal_shift.T, zonal_fraction.T

    def swap_core(value):
        return lax.ppermute(value, "lon", [(p, p ^ 1) for p in range(lon_count)])

    def swap_half(value):
        return lax.ppermute(value, "lon", [(p, p ^ 2) for p in range(lon_count)])

    def swap_band(value, first):
        pairs = [(b, b) for b in range(first)]
        for b in range(first, lat_count - 1, 2):
            pairs += [(b, b + 1), (b + 1, b)]
        pairs += [(b, b) for b in range(len(pairs), lat_count)]
        return lax.ppermute(value, "lat", pairs)

    def set_shape(number):
        return (share, number, level_count, column_count)

    def forward(mine, theirs, after):
        count = mine.shape[0] * mine.shape[1]
        message_shape = (count, level_count, 2 * MODES + LANES)
        return call(
            forward_kernel,
            [message_shape, (PAIR, count, level_count, width)],
            whole(mine, theirs, phase, high, low) + [(after, UNREAD)],
            [(count * group, padded)],
        )

    def shifted(which, held, after):
        count = held.shape[1]
        return call(
            functools.partial(shift_kernel, which, column_count),
            [(count, PAIR, level_count, width)],
            whole(distance, fraction, held) + [(after, UNREAD)],
        )

    def inverse(which, held, moved, own, other, after):
        count = held.shape[1]
        return call(
            functools.partial(inverse_kernel, which, column_count),
            [set_shape(count // share)] * 2,
            whole(distance, fraction, keep, gain, phase, high, low, held, moved, own, other)
            + [(after, UNREAD)],
            [(count * group, padded), (count * group, double), (PAIR, count, level_count, width)],
        )

    edge_shape = ((tracer_count + 1) * level_count, column_count)
    part_shape = (tracer_count, level_count, column_count)
    inner_mine, inner_send, near_edge, far_edge, near_part, far_part = call(
        begin_kernel,
        [set_shape(row_count - 2)] * 2 + [edge_shape] * 2 + [part_shape] * 2,
        [(pltpu.with_memory_space_constraint(v, pltpu.HBM), pltpu.HBM) for v in (tracers, merid_courant)],
        [tracers.shape, merid_courant.shape],
        tracer_count + 1,
    )
    inner_theirs = swap_core(inner_send)
    near_got = swap_band(near_edge, 0)
    inner_own, inner_held = forward(inner_mine, inner_theirs, near_part)
    inner_other = swap_half(inner_own)
    row_shape = (row_count, level_count, LANES)
    distance, fraction, keep, limit, far_relay = call(
        row_kernel,
        [row_shape] * 4 + [edge_shape],
        [(v, SMALL) for v in (shift_rows, fraction_rows, cutoff, damping)]
        + [(inner_own, UNREAD)]
        + whole(far_edge),
    )
    (gain,) = call(
        functools.partial(gain_kernel, column_count),
        [(row_count, 2 * (HALF + 1), level_count, double // 2)],
        whole(distance, fraction, limit, wave),
    )
    far_got = swap_band(far_relay, 1)
    (inner_moved,) = shifted("inner", inner_held, inner_own)

    near_mine, near_send = call(
        functools.partial(edge_kernel, True),
        [set_shape(1)] * 2,
        whole(near_edge, near_got, near_part) + [(inner_moved, UNREAD), (gain, UNREAD)],
    )
    near_theirs = swap_core(near_send)
    near_own, near_held = forward(near_mine, near_theirs, inner_moved)
    near_other = swap_half(near_own)
    (near_moved,) = shifted("near", near_held, near_own)
    inner = inverse("inner", inner_held, inner_moved, inner_own, inner_other, near_moved)
    inner_back = swap_core(inner[1])

    far_mine, far_send = call(
        functools.partial(edge_kernel, False),
        [set_shape(1)] * 2,
        whole(far_edge, far_got, far_part) + [(inner[0], UNREAD), (gain, UNREAD)],
    )
    far_theirs = swap_core(far_send)
    near = inverse("near", near_held, near_moved, near_own, near_other, far_mine)
    near_back = swap_core(near[1])
    far_own, far_held = forward(far_mine, far_theirs, near[0])
    far_other = swap_half(far_own)
    (far_moved,) = shifted("far", far_held, far_own)
    far = inverse("far", far_held, far_moved, far_own, far_other, far_moved)
    far_back = swap_core(far[1])
    (half_done,) = call(
        functools.partial(end_kernel, 0),
        [tracers.shape],
        whole(inner[0], near[0], far[0]),
        [(share,) + tracers.shape[1:]],
        share,
        pltpu.HBM,
    )
    (result,) = call(
        functools.partial(end_kernel, 1),
        [tracers.shape],
        whole(inner_back, near_back, far_back) + [(half_done, pltpu.HBM)],
        [(share,) + tracers.shape[1:]],
        share,
        pltpu.HBM,
        {3: 0},
    )
    return result


def solution(mesh):
    placed = (
        P(None, None, "lat", "lon"),
        P(None, "lat", "lon"),
        P(None, "lat"),
        P(None, "lat"),
        P(),
        P(),
    )
    return jax.shard_map(
        body, mesh=mesh, in_specs=placed, out_specs=P(None, None, "lat", "lon"), check_vma=False
    )
```
